32 devices in a mesh: sector: 8 (over z, x), band: 4 (over y, core).
Axes of the slice: x: 2, y: 2, z: 4, core: 2. Of those that a mesh axis runs over, the one named last changes fastest.
Arguments:
- given_load: float32 [3, 64, 64, 256], P(None, 'sector', 'band'), may hold values from -20 to 20, as said below
- displacement: float32 [3, 64, 64, 256], P(None, 'sector', 'band'), may hold values from -3 to 3
- mass_coef: float32 [64, 64, 256], P('sector', 'band'), may hold values from 0.05 to 0.5
- stiffness: float32 [64, 64, 256], P('sector', 'band'), may hold values from 0.5 to 2
- bearing_node: int32 [128], P(('sector', 'band')), may hold values from 0 to 2047
- stick_state: int32 [128], P(('sector', 'band')), may hold values 0 or 1
- slip_prev: float32 [2, 128], P(None, ('sector', 'band')), may hold values from -3 to 3
- bearing_old: float32 [2, 128], P(None, ('sector', 'band')), may hold values from -3 to 3
- bearing_weight: float32 [128], P(('sector', 'band')), may hold values from 4 to 16
Outputs:
- increment: float32 [3, 64, 64, 256], P(None, 'sector', 'band')
- cg_residual: float32 [3, 64, 64, 256], P(None, 'sector', 'band')
- bearing_force: float32 [3, 128], P(None, ('sector', 'band'))
The draws below stay inside these ranges and needn't reach their ends.
Inputs may be any that keep to these rules, and one draw needn't show every extreme that they name: `bearing_node`: each index names a node of the raft-base layer within the bearing's own sector; several bearings may share a node. `given_load`: loads of order one to a few tens.
All inputs are finite; a program needn't handle non-finite values. No bound on the sum of `stick_state` on one device may be relied on, other than what follows from the above.
Results may differ from the reference program's by a relative error of at most 0.00021.
Values sent between devices are 32-bit elements; how exact they have to be, the bound alone decides.
No kernel may reach another device: no remote copies, remote signals or barrier semaphores. Data moves between devices by JAX's collectives and lax.ppermute only.
A program may use at most 64 MiB of HBM per device.

```python
import math
import jax
import jax.numpy as jnp

CA = 8
NR = 256
ITERS = 4
BEAR_DEV = 4
NA = 64
NH = 64
NB = 128
N_SECTOR = 8
N_BAND = 4


def draw_given_load(key, part):
    key_base = jax.random.fold_in(key, 0)
    ramp = 1.0 + 2.0 * jnp.arange(NA, dtype=jnp.float32) / max(NA - 1, 1)
    ramp = ramp[None, :, None, None]
    base = jax.random.normal(key_base, (3, NA, NH, NR), jnp.float32)
    values = ramp * jnp.clip(base, -6.0, 6.0)
    return values.astype(jnp.float32)


def place_ends(values, rng, smallest, largest):
    longest = values.shape.index(max(values.shape))
    spots = []
    for shift in (0, 1):
        where = [jax.random.randint(jax.random.fold_in(rng, axis), (), 0, length) for axis, length in enumerate(values.shape)]
        where[longest] = (where[longest] + shift) % values.shape[longest]
        spots.append(tuple(where))
    return values.at[spots[0]].set(smallest).at[spots[1]].set(largest)


def steps_of(rng, dims, cuts, smallest, largest):
    gain = 1.0
    for axis_at, shards_of in cuts:
        draws = jax.random.uniform(jax.random.fold_in(jax.random.fold_in(rng, 6), axis_at), (shards_of,), jnp.float32, smallest / len(cuts), largest / len(cuts))
        gain = gain * jnp.repeat(jnp.exp(draws), dims[axis_at] // shards_of).reshape((-1,) + (1,) * (len(dims) - 1 - axis_at))
    return gain


def centred(own_key, shape, scale, bound, cuts=(), kind=jnp.bfloat16):
    values = scale * jax.random.normal(own_key, shape, jnp.float32)
    if cuts:
        values = values * steps_of(own_key, shape, cuts, -0.22, 0.18)
    return jnp.clip(values, -bound, bound).astype(kind)


def setup_inputs(seed: int = 0) -> dict:
    key_list = jax.random.split(jax.random.key(seed), 10)
    given_load = draw_given_load(jax.random.fold_in(key_list[9], 71), 0)
    displacement = centred(key_list[1], (3, NA, NH, NR), 0.5, 3.0, ((1, 8), (2, 4)), jnp.float32)
    mass_coef = jnp.clip(jnp.exp(math.log(0.5) - 2.3025851 * jax.random.uniform(key_list[2], (NA, NH, NR), jnp.float32) ** steps_of(key_list[2], (NA, NH, NR), ((0, 8), (1, 4)), -0.2, 0.2)), 0.05, 0.5)
    stiffness = jnp.clip(jnp.exp(math.log(2.0) - 1.3862944 * jax.random.uniform(key_list[3], (NA, NH, NR), jnp.float32) ** steps_of(key_list[3], (NA, NH, NR), ((0, 8), (1, 4)), -0.2, 0.2)), 0.5, 2.0)
    bearing_node = place_ends(jax.random.randint(key_list[4], (NB,), 0, CA * NR), jax.random.fold_in(key_list[4], 1), 0, (CA * NR) - 1).astype(jnp.int32)
    stick_state = place_ends((jax.random.randint(key_list[5], (NB,), 0, 2) < 1).astype(jnp.int32), jax.random.fold_in(key_list[5], 1), 0, 1)
    slip_prev = centred(key_list[6], (2, NB), 0.5, 3.0, ((1, 32),), jnp.float32)
    bearing_old = centred(key_list[7], (2, NB), 0.5, 3.0, ((1, 32),), jnp.float32)
    bearing_weight = jnp.clip(jnp.exp(math.log(16.0) - 1.3862944 * jax.random.uniform(key_list[8], (NB,), jnp.float32) ** steps_of(key_list[8], (NB,), ((0, 32),), -0.2, 0.2)), 4.0, 16.0)
    return dict(given_load=given_load, displacement=displacement, mass_coef=mass_coef, stiffness=stiffness, bearing_node=bearing_node, stick_state=stick_state, slip_prev=slip_prev, bearing_old=bearing_old, bearing_weight=bearing_weight)


K_STICK = 4.0
K_VERT = 8.0
MU_FAST = 0.15
MU_SLOW = 0.04
RATE_GAIN = 2.0
RATE_DECAY = 2.0
V_FLOOR = 0.05
COMPONENT_SCALE = (1.0, 1.0, 2.0)

def face_conductance(left, right):
    return 2.0 * left * right / (left + right)

def conductances(stiffness):
    cycle_padded = jnp.concatenate([stiffness[-1:], stiffness, stiffness[:1]], axis=0)
    cond_sector = face_conductance(cycle_padded[:-1], cycle_padded[1:])
    height_padded = jnp.pad(stiffness, ((0, 0), (1, 1), (0, 0)))
    cond_height = face_conductance(height_padded[:, :-1], height_padded[:, 1:])
    cond_radial = face_conductance(stiffness[:, :, :-1], stiffness[:, :, 1:])
    return (cond_sector, cond_height, cond_radial)

def operate(field, mass_coef, conds, bottom_diag):
    cond_sector, cond_height, cond_radial = conds
    scales = jnp.array(COMPONENT_SCALE, jnp.float32)[:, None, None, None]
    cycle_padded = jnp.concatenate([field[:, -1:], field, field[:, :1]], axis=1)
    flux_sector = cond_sector[None] * (cycle_padded[:, 1:] - cycle_padded[:, :-1])
    total = -(flux_sector[:, 1:] - flux_sector[:, :-1])
    height_padded = jnp.pad(field, ((0, 0), (0, 0), (1, 1), (0, 0)))
    flux_height = cond_height[None] * (height_padded[:, :, 1:] - height_padded[:, :, :-1])
    total = total - (flux_height[:, :, 1:] - flux_height[:, :, :-1])
    flux_radial = cond_radial[None] * (field[..., 1:] - field[..., :-1])
    flux_radial = jnp.pad(flux_radial, ((0, 0), (0, 0), (0, 0), (1, 1)))
    total = total - (flux_radial[..., 1:] - flux_radial[..., :-1])
    layers = field.shape[2]
    diag_full = jnp.pad(bottom_diag[:, :, None, :], ((0, 0), (0, 0), (0, layers - 1), (0, 0)))
    return mass_coef[None] * field + scales * total + diag_full * field

def bearing_law(at_node, stick_state, slip_prev, bearing_old, bearing_weight):
    moved = at_node[:2]
    trial = K_STICK * (moved - slip_prev)
    slip_rate = RATE_GAIN * (moved - bearing_old)
    slip_speed = jnp.sqrt(slip_rate[0] * slip_rate[0] + slip_rate[1] * slip_rate[1] + V_FLOOR * V_FLOOR)
    friction = MU_FAST - (MU_FAST - MU_SLOW) * jnp.exp(-RATE_DECAY * slip_speed)
    capacity = friction * bearing_weight
    magnitude = jnp.sqrt(trial[0] * trial[0] + trial[1] * trial[1])
    sliding = capacity[None] * trial / jnp.maximum(magnitude, capacity)[None]
    sticking = stick_state[None] == 1
    horizontal = jnp.where(sticking, trial, sliding)
    vertical = K_VERT * at_node[2]
    force = jnp.concatenate([horizontal, vertical[None]], axis=0)
    stick_k = jnp.where(stick_state == 1, K_STICK, 0.0).astype(jnp.float32)
    stiff = jnp.stack([stick_k, stick_k, jnp.full_like(stick_k, K_VERT)], axis=0)
    return (force, stiff)

def reference(given_load, displacement, mass_coef, stiffness, bearing_node, stick_state, slip_prev, bearing_old, bearing_weight):
    conds = conductances(stiffness)
    raft = displacement[:, :, 0, :].reshape(3, N_SECTOR, CA * NR)
    sector_of = (jnp.arange(NB, dtype=jnp.int32) // (BEAR_DEV * N_BAND)).astype(jnp.int32)
    at_node = raft[:, sector_of, bearing_node]
    force, stiff = bearing_law(at_node, stick_state, slip_prev, bearing_old, bearing_weight)
    loads = jnp.zeros((3, N_SECTOR, CA * NR), jnp.float32).at[:, sector_of, bearing_node].add(force)
    bottom = jnp.zeros((3, N_SECTOR, CA * NR), jnp.float32).at[:, sector_of, bearing_node].add(stiff)
    loads = loads.reshape(3, NA, NR)
    bottom = bottom.reshape(3, NA, NR)
    zero_diag = jnp.zeros((3, NA, NR), jnp.float32)
    load_full = jnp.pad(loads[:, :, None, :], ((0, 0), (0, 0), (0, NH - 1), (0, 0)))
    newton_rhs = given_load - operate(displacement, mass_coef, conds, zero_diag) - load_full
    increment = jnp.zeros_like(newton_rhs)
    residual = newton_rhs
    direction = newton_rhs
    norm_now = jnp.sum(residual * residual)
    for iteration in range(ITERS):
        image = operate(direction, mass_coef, conds, bottom)
        alpha = norm_now / jnp.sum(direction * image)
        increment = increment + alpha * direction
        residual = residual - alpha * image
        norm_next = jnp.sum(residual * residual)
        direction = residual + norm_next / norm_now * direction
        norm_now = norm_next
    return (increment, residual, force)
```

```python
import functools

import jax
import jax.numpy as jnp
from jax import lax
from jax.experimental import pallas as pl
from jax.experimental.pallas import tpu as pltpu
from jax.sharding import PartitionSpec as P

ITERS = 4
DEPTH = ITERS

K_STICK = 4.0
K_VERT = 8.0
MU_FAST = 0.15
MU_SLOW = 0.04
RATE_GAIN = 2.0
RATE_DECAY = 2.0
V_FLOOR = 0.05
COMPONENT_SCALE = (1.0, 1.0, 2.0)

CENTER = 12.0
SPREAD = 12.0
FLOOR = 0.25

AXES = ("sector", "band")
F32 = jnp.float32
PARAM_ROW, PARAM_LANE, PARAM_STICK, PARAM_SLIP, PARAM_OLD, PARAM_WEIGHT = (0, 1, 2, 3, 5, 7)
VMEM_LIMIT = 48 * 1024 * 1024


def conductance(left, right):
    return 2.0 * left * right / jnp.maximum(left + right, FLOOR)


def ahead(x, axis):
    return pltpu.roll(x, x.shape[axis] - 1, axis)


def behind(x, axis):
    return pltpu.roll(x, 1, axis)


def round_up(n, multiple):
    return -(-n // multiple) * multiple


class SectorSlab:
    def __init__(self, comps, layers, bearings):
        d = DEPTH
        self.comps, self.layers, self.bearings = comps, layers, bearings
        self.stiff = comps * d * layers
        self.mass = self.stiff + d * layers
        self.disp = self.mass + (d - 1) * layers
        self.low = self.disp + comps * layers
        self.params = self.low + comps * d
        self.high = self.params + bearings
        self.rows = round_up(self.high + comps * d, 8)

    def residual_at(self, c, i):
        return (c * DEPTH + i) * self.layers


def local_kernel(
    u, load, mass, stiff, node, stick, slip, old, weight, r, slab_a, slab_b, band_a, band_b, own, *, radial
):
    comps, rows, layers, width = u.shape
    bearings = node.shape[0]
    d = DEPTH
    lane = lax.broadcasted_iota(jnp.int32, (layers, width), 1)
    layer = lax.broadcasted_iota(jnp.int32, (layers, width), 0)
    before = [None] * comps
    for a in range(rows):
        k = stiff[a]
        k_r = jnp.where(lane < width - 1, conductance(k, ahead(k, 1)), 0.0)
        k_h = jnp.where(layer < layers - 1, conductance(k, ahead(k, 0)), 0.0)
        k_s = conductance(k, stiff[a + 1]) if a + 1 < rows else None
        m = mass[a]
        for c in range(comps):
            v = u[c, a]
            flux_r = k_r * (ahead(v, 1) - v)
            flux_h = k_h * (ahead(v, 0) - v)
            total = flux_r - behind(flux_r, 1) + flux_h - behind(flux_h, 0)
            if before[c] is not None:
                total = total - before[c]
            if k_s is not None:
                before[c] = k_s * (u[c, a + 1] - v)
                total = total + before[c]
            r[c, a] = load[c, a] - m * v + COMPONENT_SCALE[c] * total

    at = lax.broadcasted_iota(jnp.int32, (8, 128), 0)
    col = lax.broadcasted_iota(jnp.int32, (8, 128), 1)
    tile = jnp.zeros((8, 128), F32)
    for j in range(bearings):
        row = node[j] // radial
        values = {
            PARAM_ROW: row.astype(F32),
            PARAM_LANE: (node[j] - row * radial).astype(F32),
            PARAM_STICK: stick[j].astype(F32),
            PARAM_SLIP: slip[0, j],
            PARAM_SLIP + 1: slip[1, j],
            PARAM_OLD: old[0, j],
            PARAM_OLD + 1: old[1, j],
            PARAM_WEIGHT: weight[j],
        }
        for p, value in values.items():
            tile = jnp.where((at == j) & (col == p), value, tile)
    own[...] = tile

    slab = SectorSlab(comps, layers, bearings)
    even = lax.rem(lax.axis_index("sector"), 2) == 0
    for out, upper in ((slab_a, even), (slab_b, jnp.logical_not(even))):
        first = jnp.where(upper, rows - d, 0)
        for i in range(d):
            for c in range(comps):
                out[pl.ds(slab.residual_at(c, i), layers)] = r[c, first + i]
                out[pl.ds(slab.low + c * d + i, 1)] = u[c, first + i, 0:1]
                out[pl.ds(slab.high + c * d + i, 1)] = u[c, first + i, layers - 1 : layers]
            out[pl.ds(slab.stiff + i * layers, layers)] = stiff[first + i]
        for i in range(d - 1):
            out[pl.ds(slab.mass + i * layers, layers)] = mass[jnp.where(upper, rows - (d - 1), 0) + i]
        for c in range(comps):
            out[pl.ds(slab.disp + c * layers, layers)] = u[c, jnp.where(upper, rows - 1, 0)]
        out[pl.ds(slab.params, bearings)] = jnp.zeros((bearings, width), F32)
        out[pl.ds(slab.params, bearings), 0:128] = tile[0:bearings]
        end = slab.high + comps * d
        if slab.rows > end:
            out[pl.ds(end, slab.rows - end)] = jnp.zeros((slab.rows - end, width), F32)

    even = lax.rem(lax.axis_index("band"), 2) == 0
    fields = [r.at[c] for c in range(comps)] + [u.at[c] for c in range(comps)] + [stiff, mass]
    for f, field in enumerate(fields):
        for pair in range(rows // 2):
            planes = [field[2 * pair + i] for i in range(2)]
            top = jnp.concatenate([x[layers - d :] for x in planes], axis=0)
            low = jnp.concatenate([x[:d] for x in planes], axis=0)
            band_a[f * (rows // 2) + pair] = jnp.where(even, top, low)
            band_b[f * (rows // 2) + pair] = jnp.where(even, low, top)


class CornerSlab:
    def __init__(self, comps, bearings):
        pairs = DEPTH // 2
        self.pairs = pairs
        self.stiff = comps * 2 * pairs
        self.mass = self.stiff + 2 * pairs
        self.disp = self.mass + 2 * pairs
        self.edge = self.disp + comps
        self.params = self.edge + comps
        self.bearing_rows = round_up(3 * bearings, 8)
        self.blocks = self.params + self.bearing_rows // 8


def corner_kernel(slab_a, slab_b, own, corner_a, corner_b, params, *, comps, layers, bearings):
    d = DEPTH
    slab, corner = SectorSlab(comps, layers, bearings), CornerSlab(comps, bearings)
    even = lax.rem(lax.axis_index("band"), 2) == 0

    def put(block, planes):
        top = jnp.concatenate([x[layers - d :] for x in planes], axis=0)
        low = jnp.concatenate([x[:d] for x in planes], axis=0)
        corner_a[block] = jnp.where(even, top, low)
        corner_b[block] = jnp.where(even, low, top)

    sides = (slab_a, slab_b)
    for n, side in enumerate(sides):

        def plane(offset):
            return side[pl.ds(offset, layers)]

        for pair in range(corner.pairs):
            rows = (2 * pair, 2 * pair + 1)
            at = n * corner.pairs + pair
            for c in range(comps):
                put(c * 2 * corner.pairs + at, [plane(slab.residual_at(c, i)) for i in rows])
            put(corner.stiff + at, [plane(slab.stiff + i * layers) for i in rows])
            put(corner.mass + at, [plane(slab.mass + min(i, d - 2) * layers) for i in rows])
    for c in range(comps):
        put(corner.disp + c, [x[pl.ds(slab.disp + c * layers, layers)] for x in sides])
        high = jnp.concatenate([x[pl.ds(slab.high + c * d, d)] for x in sides], axis=0)
        low = jnp.concatenate([x[pl.ds(slab.low + c * d, d)] for x in sides], axis=0)
        corner_a[corner.edge + c] = jnp.where(even, high, low)
        corner_b[corner.edge + c] = jnp.where(even, low, high)
    known = [own[0:bearings]] + [x[pl.ds(slab.params, bearings), 0:128] for x in sides]
    spare = corner.bearing_rows - 3 * bearings
    if spare:
        known.append(jnp.full((spare, 128), -1.0, F32))
    known = jnp.concatenate(known, axis=0)
    params[...] = known
    for i in range(corner.bearing_rows // 8):
        for out in (corner_a, corner_b):
            out[corner.params + i] = jnp.zeros(out.shape[1:], F32)
            out[corner.params + i, :, 0:128] = known[8 * i : 8 * i + 8]


def bearing_law(moved, vertical, stick, slip, old, weight):
    trial = [K_STICK * (moved[i] - slip[i]) for i in range(2)]
    rate = [RATE_GAIN * (moved[i] - old[i]) for i in range(2)]
    slip_speed = jnp.sqrt(rate[0] * rate[0] + rate[1] * rate[1] + V_FLOOR * V_FLOOR)
    friction = MU_FAST - (MU_FAST - MU_SLOW) * jnp.exp(-RATE_DECAY * slip_speed)
    capacity = friction * weight
    magnitude = jnp.sqrt(trial[0] * trial[0] + trial[1] * trial[1])
    largest = jnp.maximum(magnitude, capacity)
    forces = [jnp.where(stick == 1.0, t, capacity * t / largest) for t in trial]
    return forces + [K_VERT * vertical]


def power_kernel(
    r, u, mass, stiff, slab_a, slab_b, band_a, band_b, corner_a, corner_b, params, params_2, params_3,
    b0, b1, b2, b3, b4, payload,
    t0, t1, t2, t3, t4, ux, kx, mx, ks, kh, kr, diag, raft,
    *, bearings, sectors, bands,
):
    comps, rows, layers, width = r.shape
    d = DEPTH
    slab, corner = SectorSlab(comps, layers, bearings), CornerSlab(comps, bearings)
    sector, band = lax.axis_index("sector"), lax.axis_index("band")
    sector_even = lax.rem(sector, 2) == 0
    band_even = lax.rem(band, 2) == 0
    all_rows, all_layers = rows + 2 * d, layers + 2 * d
    own = pl.ds(d, layers)

    def place(a, carry):
        for c in range(comps):
            t0[c, d + a, own] = r[c, a]
            ux[c, d + a, own] = u[c, a]
        kx[d + a, own] = stiff[a]
        mx[d + a, own] = mass[a]
        return carry

    lax.fori_loop(0, rows, place, 0)
    first = {}
    for n, (side, above) in enumerate(((slab_a, sector_even), (slab_b, jnp.logical_not(sector_even)))):
        base = jnp.where(above, d + rows, 0)
        first[n] = base
        nearest = jnp.where(above, d + rows, d - 1)
        for i in range(d):
            for c in range(comps):
                t0[c, base + i, own] = side[pl.ds(slab.residual_at(c, i), layers)]
                ux[c, base + i, d : d + 1] = side[pl.ds(slab.low + c * d + i, 1)]
                ux[c, base + i, d + layers - 1 : d + layers] = side[pl.ds(slab.high + c * d + i, 1)]
            kx[base + i, own] = side[pl.ds(slab.stiff + i * layers, layers)]
        for i in range(d - 1):
            mx[jnp.where(above, d + rows, 1) + i, own] = side[pl.ds(slab.mass + i * layers, layers)]
        for c in range(comps):
            ux[c, nearest, own] = side[pl.ds(slab.disp + c * layers, layers)]

    def place_bands(a_above):
        for n, (side, corners) in enumerate(((band_a, corner_a), (band_b, corner_b))):
            above = a_above == (n == 0)
            at = d + layers if above else 0
            near = d + layers if above else d - 1
            where = pl.ds(at, d)

            def own_pair(pair, carry):
                for i in range(2):
                    part = slice(i * d, i * d + d)
                    row = d + 2 * pair + i
                    for c in range(comps):
                        t0[c, row, where] = side[c * (rows // 2) + pair, part]
                        ux[c, row, where] = side[(comps + c) * (rows // 2) + pair, part]
                    kx[row, where] = side[2 * comps * (rows // 2) + pair, part]
                    mx[row, where] = side[(2 * comps + 1) * (rows // 2) + pair, part]
                return carry

            lax.fori_loop(0, rows // 2, own_pair, 0)
            for m in range(2):
                base = first[m]
                above_m = sector_even if m == 0 else jnp.logical_not(sector_even)
                mass_base = jnp.where(above_m, d + rows, 1)
                nearest = jnp.where(above_m, d + rows, d - 1)
                for i in range(d):
                    part = slice((i % 2) * d, (i % 2) * d + d)
                    block = m * corner.pairs + i // 2
                    for c in range(comps):
                        t0[c, base + i, where] = corners[c * 2 * corner.pairs + block, part]
                        ux[c, base + i, near : near + 1] = corners[corner.edge + c, m * d + i : m * d + i + 1]
                    kx[base + i, where] = corners[corner.stiff + block, part]
                    if i < d - 1:
                        mx[mass_base + i, where] = corners[corner.mass + block, part]
                for c in range(comps):
                    ux[c, nearest, where] = corners[corner.disp + c, m * d : m * d + d]

    @pl.when(band_even)
    def _():
        place_bands(True)

    @pl.when(jnp.logical_not(band_even))
    def _():
        place_bands(False)

    lane = lax.broadcasted_iota(jnp.int32, (all_layers, width), 1)
    layer = lax.broadcasted_iota(jnp.int32, (all_layers, width), 0)

    raft[...] = jnp.zeros_like(raft)
    payload[...] = jnp.zeros_like(payload)

    @pl.when(band == 0)
    def _():
        sources = [params[...]]
        sources.append(corner_a[pl.ds(corner.params, corner.bearing_rows // 8), :, 0:128].reshape(corner.bearing_rows, 128))
        sources += [params_2[...], params_3[...]]
        known = jnp.concatenate(sources[:bands], axis=0)
        count = known.shape[0]
        within = lax.rem(lax.broadcasted_iota(jnp.int32, (count, 1), 0), corner.bearing_rows)
        shift_a = jnp.where(sector_even, d + rows, d - rows)
        shift_b = jnp.where(sector_even, d - rows, d + rows)
        shift = jnp.where(within < bearings, d, jnp.where(within < 2 * bearings, shift_a, shift_b))
        column = lambda p: known[:, p : p + 1]
        row_of = column(PARAM_ROW).astype(jnp.int32) + shift
        row_of = jnp.where(within < 3 * bearings, row_of, -1)
        row_of = jnp.broadcast_to(row_of, (count, width))
        lane_of = jnp.broadcast_to(column(PARAM_LANE).astype(jnp.int32), (count, width))
        here = lane_of == lax.broadcasted_iota(jnp.int32, (count, width), 1)
        at_node = [jnp.zeros((count, width), F32) for _ in range(comps)]
        for a in range(all_rows):
            hit = row_of == a
            for c in range(comps):
                at_node[c] = jnp.where(hit, ux[c, a, d : d + 1], at_node[c])
        stick = jnp.broadcast_to(column(PARAM_STICK), (count, width))
        force = bearing_law(
            at_node[:2], at_node[2], stick,
            [column(PARAM_SLIP), column(PARAM_SLIP + 1)], [column(PARAM_OLD), column(PARAM_OLD + 1)], column(PARAM_WEIGHT),
        )
        force = [jnp.where(here, f, 0.0) for f in force]
        stiffness = [jnp.where(here & (stick == 1.0), K_STICK, 0.0), jnp.where(here, K_VERT, 0.0)]
        for a in range(all_rows):
            hit = row_of == a
            for q, value in enumerate(force + stiffness):
                raft[q, a : a + 1] = jnp.sum(jnp.where(hit, value, 0.0), axis=0, keepdims=True)
        place_of = lax.broadcasted_iota(jnp.int32, payload.shape, 0) - sector * bands
        col = lax.broadcasted_iota(jnp.int32, payload.shape, 1)
        reply = jnp.zeros(payload.shape, F32)
        for c in range(comps):
            total = jnp.sum(force[c], axis=1, keepdims=True)
            for q in range(bands):
                for j in range(bearings):
                    value = total[q * corner.bearing_rows + j : q * corner.bearing_rows + j + 1]
                    reply = jnp.where((place_of == q) & (col == 64 + c * bearings + j), value, reply)
        payload[...] = reply

    interface = (layer == d - 1) | (layer == d + layers - 1)

    def faces(a, carry):
        k = kx[a]
        k_h = conductance(k, ahead(k, 0))
        kh[a] = k_h
        kr[a] = jnp.where(lane < width - 1, conductance(k, ahead(k, 1)), 0.0)
        ks[a] = conductance(k, kx[jnp.minimum(a + 1, all_rows - 1)])
        for c in range(comps):
            v = ux[c, a]
            flux = jnp.where(interface, k_h * (ahead(v, 0) - v), 0.0)
            change = COMPONENT_SCALE[c] * (flux - behind(flux, 0))
            change = change - jnp.where(layer == d, raft[c, pl.ds(a, 1)], 0.0)
            t0[c, a] = t0[c, a] + change
        return carry

    lax.fori_loop(0, all_rows, faces, 0)
    for a in (d - 1, d + rows - 1):
        for c in range(comps):
            flux = COMPONENT_SCALE[c] * (ks[a] * (ux[c, a + 1] - ux[c, a]))
            t0[c, a] = t0[c, a] + flux
            t0[c, a + 1] = t0[c, a + 1] - flux

    def diagonals(a, carry):
        k_h, k_r = kh[a], kr[a]
        around = k_h + behind(k_h, 0) + k_r + behind(k_r, 1) + ks[a] + ks[a - 1]
        centre = mx[a] - CENTER
        diag[0, a] = (centre + COMPONENT_SCALE[0] * around + jnp.where(layer == d, raft[comps, pl.ds(a, 1)], 0.0)) * (1.0 / SPREAD)
        diag[1, a] = (centre + COMPONENT_SCALE[2] * around + jnp.where(layer == d, raft[comps + 1, pl.ds(a, 1)], 0.0)) * (1.0 / SPREAD)
        return carry

    lax.fori_loop(1, all_rows - 1, diagonals, 0)

    levels = (t0, t1, t2, t3, t4)
    for step in range(1, ITERS + 1):
        src, dst = levels[step - 1], levels[step]
        factor = 1.0 if step == 1 else 2.0

        def apply(a, carry):
            k_h, k_r, k_next, k_back = kh[a], kr[a], ks[a], ks[a - 1]
            for c in range(comps):
                v = src[c, a]
                around = k_next * src[c, a + 1] + k_back * src[c, a - 1]
                around = around + (k_h * ahead(v, 0) + behind(k_h * v, 0))
                around = around + (k_r * ahead(v, 1) + behind(k_r * v, 1))
                centre = diag[0 if c < 2 else 1, a] * v
                if step > 1:
                    centre = 2.0 * centre - levels[step - 2][c, a]
                dst[c, a] = centre - (factor * COMPONENT_SCALE[c] / SPREAD) * around
            return carry

        lax.fori_loop(step, all_rows - step, apply, 0)

    pairs = ((0, 0), (0, 1), (0, 2), (0, 3), (0, 4), (1, 4), (2, 4), (3, 4))
    outs = (b0, b1, b2, b3, b4)

    def products(a, sums):
        for c in range(comps):
            block = [t[c, d + a, own] for t in levels]
            for out, x in zip(outs, block):
                out[c, a] = x
            sums = tuple(
                s + jnp.sum((block[i] * block[j]).reshape(layers // 8, 8, width), axis=0) for s, (i, j) in zip(sums, pairs)
            )
        return sums

    sums = lax.fori_loop(0, rows, products, tuple(jnp.zeros((8, width), F32) for _ in pairs))
    col = lax.broadcasted_iota(jnp.int32, payload.shape, 1)
    reply = payload[...]
    for p, s in enumerate(sums):
        total = jnp.sum(jnp.sum(s, axis=0, keepdims=True), axis=1, keepdims=True)
        reply = jnp.where(col == p, total, reply)
    payload[...] = reply


def combine_kernel(received, b0, b1, b2, b3, b4, increment, residual, force, *, bearings, bands):
    comps, rows, layers, width = b0.shape
    sector = lax.axis_index("sector")
    total = jnp.sum(received[...], axis=0, keepdims=True)
    col = lax.broadcasted_iota(jnp.int32, total.shape, 1)
    mu = [jnp.sum(jnp.where(col == p, total, 0.0), axis=1, keepdims=True) for p in range(8)]
    mu[5] = 2.0 * mu[5] - mu[3]
    mu[6] = 2.0 * mu[6] - mu[2]
    mu[7] = 2.0 * mu[7] - mu[1]
    gram = lambda i, j: mu[0] if i + j == 0 else 0.5 * (mu[i + j] + mu[abs(i - j)])
    table = {(i, j): gram(min(i, j), max(i, j)) for i in range(ITERS) for j in range(i, ITERS + 1)}
    g = lambda i, j: table[min(i, j), max(i, j)]
    zero, one = jnp.zeros_like(mu[0]), jnp.ones_like(mu[0])
    res = [one] + [zero] * ITERS
    direction, inc = list(res), [zero] * (ITERS + 1)
    norm = mu[0]
    for it in range(ITERS):
        image = [CENTER * x for x in direction]
        for i in range(it + 1):
            if i == 0:
                image[1] = image[1] + SPREAD * direction[0]
            else:
                image[i + 1] = image[i + 1] + (0.5 * SPREAD) * direction[i]
                image[i - 1] = image[i - 1] + (0.5 * SPREAD) * direction[i]
        product = sum(
            direction[i] * sum(image[j] * g(i, j) for j in range(it + 2)) for i in range(it + 1)
        )
        alpha = norm / product
        inc = [x + alpha * y for x, y in zip(inc, direction)]
        res = [x - alpha * y for x, y in zip(res, image)]
        if it + 1 < ITERS:
            norm_next = sum(res[i] * sum(res[j] * g(i, j) for j in range(it + 2)) for i in range(it + 2))
            ratio = norm_next / norm
            direction = [x + ratio * y for x, y in zip(res, direction)]
            norm = norm_next
    basis = (b0, b1, b2, b3, b4)
    inc = [jnp.broadcast_to(x, (layers, width)) for x in inc[:ITERS]]
    res = [jnp.broadcast_to(x, (layers, width)) for x in res]

    def combine(a, carry):
        for c in range(comps):
            x = [b[c, a] for b in basis]
            increment[c, a] = sum(y * z for y, z in zip(inc, x))
            residual[c, a] = sum(y * z for y, z in zip(res, x))
        return carry

    lax.fori_loop(0, rows, combine, 0)
    mine = received[pl.ds(sector * bands, 1)]
    for c in range(comps):
        force[c : c + 1] = mine[:, 64 + c * bearings : 64 + (c + 1) * bearings]


def kernel_call(body, outs, operands, scratch=(), smem=()):
    vmem = pl.BlockSpec(memory_space=pltpu.VMEM)
    specs = [pl.BlockSpec(memory_space=pltpu.SMEM) if i in smem else vmem for i in range(len(operands))]
    return pl.pallas_call(
        body,
        out_shape=[jax.ShapeDtypeStruct(s, F32) for s in outs],
        in_specs=specs,
        out_specs=[vmem] * len(outs),
        scratch_shapes=[pltpu.VMEM(s, F32) for s in scratch],
        compiler_params=pltpu.CompilerParams(vmem_limit_bytes=VMEM_LIMIT),
    )(*operands)


def pair_up(i, n):
    return i ^ 1


def pair_down(i, n):
    return (((i + 1) % n) ^ 1) - 1 if ((i + 1) % n) ^ 1 else n - 1


def per_device(
    given_load, displacement, mass_coef, stiffness, bearing_node, stick_state, slip_prev, bearing_old, bearing_weight
):
    comps, rows, layers, radial = displacement.shape
    bearings = bearing_node.shape[0]
    sectors, bands = lax.axis_size("sector"), lax.axis_size("band")
    d = DEPTH
    slab, corner = SectorSlab(comps, layers, bearings), CornerSlab(comps, bearings)

    def along_sector(x, partner):
        return lax.ppermute(
            x, AXES, [(s * bands + b, partner(s, sectors) * bands + b) for s in range(sectors) for b in range(bands)]
        )

    def along_band(x, partner):
        pairs = [(b, partner(b)) for b in range(bands) if 0 <= partner(b) < bands and partner(b) != b]
        return lax.ppermute(x, AXES, [(s * bands + i, s * bands + j) for s in range(sectors) for i, j in pairs])

    inner = lambda b: -1 if b in (0, bands - 1) else ((b + 1) ^ 1) - 1

    field = displacement.shape
    slab_shape, band_shape = (slab.rows, radial), ((2 * comps + 2) * (rows // 2), 2 * d, radial)
    r, slab_a, slab_b, band_a, band_b, own = kernel_call(
        functools.partial(local_kernel, radial=radial),
        [field, slab_shape, slab_shape, band_shape, band_shape, (8, 128)],
        (displacement, given_load, mass_coef, stiffness, bearing_node, stick_state, slip_prev, bearing_old, bearing_weight),
        smem=(4, 5, 6, 7, 8),
    )
    slab_b = along_sector(slab_b, pair_down)
    slab_a = along_sector(slab_a, pair_up)
    band_a = along_band(band_a, lambda b: b ^ 1)
    band_b = along_band(band_b, inner)
    corner_shape = (corner.blocks, 2 * d, radial)
    corner_a, corner_b, params = kernel_call(
        functools.partial(corner_kernel, comps=comps, layers=layers, bearings=bearings),
        [corner_shape, corner_shape, (corner.bearing_rows, 128)],
        (slab_a, slab_b, own),
    )
    corner_a = along_band(corner_a, lambda b: b ^ 1)
    params_2 = along_band(params, lambda b: b ^ 2)
    params_3 = along_band(params, lambda b: b ^ 3)
    corner_b = along_band(corner_b, inner)
    devices = sectors * bands
    extended = (rows + 2 * d, layers + 2 * d, radial)
    *basis, payload = kernel_call(
        functools.partial(power_kernel, bearings=bearings, sectors=sectors, bands=bands),
        [field] * (ITERS + 1) + [(devices, 128)],
        (r, displacement, mass_coef, stiffness, slab_a, slab_b, band_a, band_b, corner_a, corner_b, params, params_2, params_3),
        scratch=[(comps, *extended)] * (ITERS + 2) + [extended] * 5 + [(2, *extended), (comps + 2, rows + 2 * d, radial)],
    )
    received = lax.all_to_all(payload, AXES, 0, 0, tiled=True)
    increment, residual, force = kernel_call(
        functools.partial(combine_kernel, bearings=bearings, bands=bands),
        [field, field, (comps, bearings)],
        (received, *basis),
    )
    return (increment, residual, force)


def solution(mesh):
    return jax.shard_map(
        per_device,
        mesh=mesh,
        in_specs=(
            P(None, "sector", "band", None),
            P(None, "sector", "band", None),
            P("sector", "band", None),
            P("sector", "band", None),
            P(("sector", "band")),
            P(("sector", "band")),
            P(None, ("sector", "band")),
            P(None, ("sector", "band")),
            P(("sector", "band")),
        ),
        out_specs=(
            P(None, "sector", "band", None),
            P(None, "sector", "band", None),
            P(None, ("sector", "band")),
        ),
        check_vma=False,
    )
```

```python
import functools

import jax
import jax.numpy as jnp
from jax import lax
from jax.experimental import pallas as pl
from jax.experimental.pallas import tpu as pltpu
from jax.sharding import PartitionSpec as P

ITERS = 4
DEPTH = ITERS

K_STICK = 4.0
K_VERT = 8.0
MU_FAST = 0.15
MU_SLOW = 0.04
RATE_GAIN = 2.0
RATE_DECAY = 2.0
V_FLOOR = 0.05
COMPONENT_SCALE = (1.0, 1.0, 2.0)

STATS = 1 + 2 * (ITERS - 1)
TINY = 1e-30
FLOOR = 0.25

AXES = ("sector", "band")
F32 = jnp.float32
PARAM_ROW, PARAM_LANE, PARAM_STICK, PARAM_SLIP, PARAM_OLD, PARAM_WEIGHT = (0, 1, 2, 3, 5, 7)
PARAMS = 8
PARAM_AT = 32
FORCE_AT = 64
VMEM_LIMIT = 48 * 1024 * 1024
VMEM_WHOLE = 64 * 1024 * 1024 - 65536


def conductance(left, right):
    return 2.0 * left * right / jnp.maximum(left + right, FLOOR)


def ahead(x, axis):
    return pltpu.roll(x, x.shape[axis] - 1, axis)


def behind(x, axis):
    return pltpu.roll(x, 1, axis)


def round_up(n, multiple):
    return -(-n // multiple) * multiple


def put_band(out, at, r, u, stiff, mass, top):
    comps, rows, layers, _ = r.shape
    fields = [r.at[c] for c in range(comps)] + [u.at[c] for c in range(comps)] + [stiff, mass]
    for f, field in enumerate(fields):
        for pair in range(rows // 2):
            planes = [field[2 * pair + i] for i in range(2)]
            high = jnp.concatenate([x[layers - DEPTH :] for x in planes], axis=0)
            low = jnp.concatenate([x[:DEPTH] for x in planes], axis=0)
            out[at + f * (rows // 2) + pair] = jnp.where(top, high, low)


class SectorSlab:
    def __init__(self, comps, layers):
        d = DEPTH
        self.layers = layers
        self.stiff = comps * d * layers
        self.mass = self.stiff + d * layers
        self.disp = self.mass + (d - 1) * layers
        self.low = self.disp + comps * layers
        self.high = self.low + comps * d
        self.rows = round_up(self.high + comps * d, 8)

    def residual_at(self, c, i):
        return (c * DEPTH + i) * self.layers


def parts_of(work):
    comps = (work.shape[0] - 5) // 2
    return work.at[0:comps], work.at[comps : 2 * comps], work.at[2 * comps : 2 * comps + 3], work.at[2 * comps + 3], work.at[2 * comps + 4]


def local_kernel(
    u_far, load_far, mass_far, stiff_far, node_far, stick_far, slip_far, old_far, weight_far,
    work, slab_a, slab_b, band_b,
    load, node, stick, slip, old, weight, arrived, *, radial,
):
    comps, rows, layers, width = load.shape
    d = DEPTH
    r, u, cond, mass, stiff = parts_of(work)
    fields = ((stiff_far, stiff), (u_far, u), (mass_far, mass), (load_far, load))
    small = ((node_far, node), (stick_far, stick), (slip_far, slip), (old_far, old), (weight_far, weight))
    moves = [pltpu.make_async_copy(src, dst, arrived.at[n]) for n, (src, dst) in enumerate(fields + small)]
    for move in moves:
        move.start()
    lane = lax.broadcasted_iota(jnp.int32, (layers, width), 1)
    layer = lax.broadcasted_iota(jnp.int32, (layers, width), 0)
    moves[0].wait()
    for a in range(rows):
        k = stiff[a]
        cond[0, a] = jnp.where(lane < width - 1, conductance(k, ahead(k, 1)), 0.0)
        cond[1, a] = jnp.where(layer < layers - 1, conductance(k, ahead(k, 0)), 0.0)
        cond[2, a] = conductance(k, stiff[a + 1]) if a + 1 < rows else jnp.zeros((layers, width), F32)
    for move in moves[1 : len(fields)]:
        move.wait()
    before = [None] * comps
    for a in range(rows):
        k_r, k_h, k_s = cond[0, a], cond[1, a], cond[2, a]
        m = mass[a]
        for c in range(comps):
            v = u[c, a]
            flux_r = k_r * (ahead(v, 1) - v)
            flux_h = k_h * (ahead(v, 0) - v)
            total = flux_r - behind(flux_r, 1) + flux_h - behind(flux_h, 0)
            if before[c] is not None:
                total = total - before[c]
            if a + 1 < rows:
                before[c] = k_s * (u[c, a + 1] - v)
                total = total + before[c]
            r[c, a] = load[c, a] - m * v + COMPONENT_SCALE[c] * total

    for move in moves[len(fields) :]:
        move.wait()
    col = lax.broadcasted_iota(jnp.int32, (8, 128), 1)
    tile = jnp.zeros((8, 128), F32)
    for j in range(node.shape[0]):
        at = node[j] // radial
        values = {
            PARAM_ROW: at.astype(F32),
            PARAM_LANE: (node[j] - at * radial).astype(F32),
            PARAM_STICK: stick[j].astype(F32),
            PARAM_SLIP: slip[0, j],
            PARAM_SLIP + 1: slip[1, j],
            PARAM_OLD: old[0, j],
            PARAM_OLD + 1: old[1, j],
            PARAM_WEIGHT: weight[j],
        }
        for p, value in values.items():
            tile = jnp.where(col == PARAM_AT + PARAMS * j + p, value, tile)
    cond[2, rows - 1, 0:8, 0:128] = tile

    slab = SectorSlab(comps, layers)
    even = lax.rem(lax.axis_index("sector"), 2) == 0
    for out, upper in ((slab_a, even), (slab_b, jnp.logical_not(even))):
        first = jnp.where(upper, rows - d, 0)
        for i in range(d):
            for c in range(comps):
                out[pl.ds(slab.residual_at(c, i), layers)] = r[c, first + i]
                out[pl.ds(slab.low + c * d + i, 1)] = u[c, first + i, 0:1]
                out[pl.ds(slab.high + c * d + i, 1)] = u[c, first + i, layers - 1 : layers]
            out[pl.ds(slab.stiff + i * layers, layers)] = stiff[first + i]
        for i in range(d - 1):
            out[pl.ds(slab.mass + i * layers, layers)] = mass[jnp.where(upper, rows - (d - 1), 0) + i]
        for c in range(comps):
            out[pl.ds(slab.disp + c * layers, layers)] = u[c, jnp.where(upper, rows - 1, 0)]
        end = slab.high + comps * d
        if slab.rows > end:
            out[pl.ds(end, slab.rows - end)] = jnp.zeros((slab.rows - end, width), F32)

    even = lax.rem(lax.axis_index("band"), 2) == 0
    put_band(band_b, 0, r, u, stiff, mass, jnp.logical_not(even))


REACH = [DEPTH] + [max(DEPTH - n, 1) for n in range(2, DEPTH + 1)]


class Wedge:
    counts = REACH
    starts = [sum(REACH[:n]) for n in range(DEPTH)]
    height = round_up(sum(REACH), 8)

    def __init__(self, comps):
        self.stiff, self.mass, self.disp = comps, comps + 1, comps + 2
        self.blocks = 2 * comps + 2


def padded_block(parts):
    parts = list(parts)
    spare = Wedge.height - sum(p.shape[0] for p in parts)
    if spare:
        parts.append(jnp.zeros((spare, parts[0].shape[1]), F32))
    return jnp.concatenate(parts, axis=0)


def put_wedge(out, at, comps, layers, top, residual, stiff, mass, disp, edges):
    wedge, d = Wedge(comps), DEPTH
    sources = [functools.partial(residual, c) for c in range(comps)] + [stiff, mass]
    for f, source in enumerate(sources):
        planes = [source(n) for n in range(1, d + 1)]
        high = padded_block(p[layers - k :] for p, k in zip(planes, wedge.counts))
        low = padded_block(p[:k] for p, k in zip(planes, wedge.counts))
        out[at + f] = jnp.where(top, high, low)
    for c in range(comps):
        row, rims = disp(c), [edges(c, n) for n in range(1, d + 1)]
        high = padded_block([row[layers - d :]] + [rim[1] for rim in rims])
        low = padded_block([row[:d]] + [rim[0] for rim in rims])
        out[at + wedge.disp + c] = jnp.where(top, high, low)


def corner_kernel(slab_a, slab_b, work, survey, band_b, corner_a, corner_b, *, comps, layers):
    d = DEPTH
    slab, wedge = SectorSlab(comps, layers), Wedge(comps)
    band_even = lax.rem(lax.axis_index("band"), 2) == 0
    sector_even = lax.rem(lax.axis_index("sector"), 2) == 0
    for n, (side, above) in enumerate(((slab_a, sector_even), (slab_b, jnp.logical_not(sector_even)))):

        def plane(offset, side=side):
            return side[pl.ds(pl.multiple_of(offset, 8), layers)]

        def step(n, count, above=above):
            return jnp.where(above, n - 1, count - n)

        for out, top in ((corner_a, band_even), (corner_b, jnp.logical_not(band_even))):
            put_wedge(
                out,
                n * wedge.blocks,
                comps,
                layers,
                top,
                lambda c, n: plane(slab.residual_at(c, step(n, d))),
                lambda n: plane(slab.stiff + step(n, d) * layers),
                lambda n: plane(slab.mass + step(min(n, d - 1), d - 1) * layers),
                lambda c: plane(slab.disp + c * layers),
                lambda c, n: [side[pl.ds(at + c * d + step(n, d), 1)] for at in (slab.low, slab.high)],
            )
    r, u, _, mass, stiff = parts_of(work)
    put_band(corner_a, 2 * wedge.blocks, r, u, stiff, mass, band_even)


def dot(x, y):
    return jnp.sum((x * y).reshape(x.shape[0] // 8, 8, x.shape[1]), axis=0)


def total_of(x):
    return jnp.sum(jnp.sum(x, axis=0, keepdims=True), axis=1, keepdims=True)


def survey_kernel(work, row, image, basis_1, basis_2):
    r, _, cond, mass, _ = parts_of(work)
    comps, rows, layers, width = r.shape
    zero = jnp.zeros((8, width), F32)

    def apply(src):
        norm, product = zero, zero
        for a in range(rows):
            k_r, k_h, k_next = cond[0, a], cond[1, a], cond[2, a]
            for c in range(comps):
                v = src[c, a]
                flux_r = k_r * (ahead(v, 1) - v)
                flux_h = k_h * (ahead(v, 0) - v)
                total = flux_r - behind(flux_r, 1) + flux_h - behind(flux_h, 0)
                if a + 1 < rows:
                    total = total + k_next * (src[c, a + 1] - v)
                if a:
                    total = total - cond[2, a - 1] * (v - src[c, a - 1])
                out = mass[a] * v - COMPONENT_SCALE[c] * total
                image[c, a] = out
                norm, product = norm + dot(v, v), product + dot(v, out)
        return total_of(norm), total_of(product)

    level, back, weight_here, stats = r, None, None, []
    outs = (basis_1, basis_2)
    norm_back = None
    for step in range(ITERS - 1):
        norm, product = apply(level)
        if step:
            stats.append(norm / jnp.maximum(norm_back, TINY))
        else:
            weight_here = norm
        stats.append(product / jnp.maximum(norm, TINY))
        if step < ITERS - 2:
            a_k = jnp.broadcast_to(stats[-1], (layers, width))
            c_k = jnp.broadcast_to(stats[-2], (layers, width)) if step else None
            for a in range(rows):
                for c in range(comps):
                    x = image[c, a] - a_k * level[c, a]
                    outs[step][c, a] = x if back is None else x - c_k * back[c, a]
            back, level, norm_back = level, outs[step], norm
        else:
            a_k = jnp.broadcast_to(stats[-1], (layers, width))
            c_k = jnp.broadcast_to(stats[-2], (layers, width))
            last = zero
            for a in range(rows):
                for c in range(comps):
                    x = image[c, a] - a_k * level[c, a] - c_k * back[c, a]
                    last = last + dot(x, x)
            stats.append(total_of(last) / jnp.maximum(norm, TINY))
    col = lax.broadcasted_iota(jnp.int32, (8, 128), 1)
    tile = jnp.where(col == 0, weight_here, 0.0)
    for n, value in enumerate(stats):
        tile = jnp.where(col == 1 + n, weight_here * value, tile)
    tile = tile + cond[2, rows - 1, 0:8, 0:128]
    for n in range(row.shape[0] // 8):
        row[8 * n : 8 * n + 8] = tile


def coefficients(survey):
    total = jnp.sum(survey, axis=0, keepdims=True)
    col = lax.broadcasted_iota(jnp.int32, total.shape, 1)
    pick = lambda n: jnp.sum(jnp.where(col == n, total, 0.0), axis=1, keepdims=True)
    weight = jnp.maximum(pick(0), TINY)
    stats = [pick(n) / weight for n in range(1, STATS)]
    a, c = stats[0::2], stats[1::2]
    return a + [a[-1]], [None] + c


def bearing_law(moved, vertical, stick, slip, old, weight):
    trial = [K_STICK * (moved[i] - slip[i]) for i in range(2)]
    rate = [RATE_GAIN * (moved[i] - old[i]) for i in range(2)]
    slip_speed = jnp.sqrt(rate[0] * rate[0] + rate[1] * rate[1] + V_FLOOR * V_FLOOR)
    friction = MU_FAST - (MU_FAST - MU_SLOW) * jnp.exp(-RATE_DECAY * slip_speed)
    capacity = friction * weight
    magnitude = jnp.sqrt(trial[0] * trial[0] + trial[1] * trial[1])
    largest = jnp.maximum(magnitude, capacity)
    forces = [jnp.where(stick == 1.0, t, capacity * t / largest) for t in trial]
    return forces + [K_VERT * vertical]


def gram_pairs():
    return [(i, j) for i in range(ITERS) for j in range(i, ITERS + 1)]


def power_kernel(
    work, slab_a, slab_b, band_b, corner_a, corner_b, survey,
    b0, b1, b2, b3, b4, payload,
    t0, t1, t2, t3, t4, ux, kx, mx, ks, kh, kr, diag, raft,
    *, bearings, sectors, bands,
):
    r, u, _, mass, stiff = parts_of(work)
    comps, rows, layers, width = r.shape
    d = DEPTH
    slab, wedge = SectorSlab(comps, layers), Wedge(comps)
    sector, band = lax.axis_index("sector"), lax.axis_index("band")
    sector_even = lax.rem(sector, 2) == 0
    band_even = lax.rem(band, 2) == 0
    all_rows, all_layers = rows + 2 * d, layers + 2 * d
    own = pl.ds(d, layers)

    def place(a, carry):
        for c in range(comps):
            t0[c, d + a, own] = r[c, a]
            ux[c, d + a, own] = u[c, a]
        kx[d + a, own] = stiff[a]
        mx[d + a, own] = mass[a]
        return carry

    lax.fori_loop(0, rows, place, 0, unroll=True)
    first = {}
    for n, (side, above) in enumerate(((slab_a, sector_even), (slab_b, jnp.logical_not(sector_even)))):
        base = jnp.where(above, d + rows, 0)
        first[n] = base
        nearest = jnp.where(above, d + rows, d - 1)
        for i in range(d):
            for c in range(comps):
                t0[c, base + i, own] = side[pl.ds(slab.residual_at(c, i), layers)]
                ux[c, base + i, d : d + 1] = side[pl.ds(slab.low + c * d + i, 1)]
                ux[c, base + i, d + layers - 1 : d + layers] = side[pl.ds(slab.high + c * d + i, 1)]
            kx[base + i, own] = side[pl.ds(slab.stiff + i * layers, layers)]
        for i in range(d - 1):
            mx[jnp.where(above, d + rows, 1) + i, own] = side[pl.ds(slab.mass + i * layers, layers)]
        for c in range(comps):
            ux[c, nearest, own] = side[pl.ds(slab.disp + c * layers, layers)]

    def place_bands(a_above):
        corners = [[(x, 0), (x, wedge.blocks)] for x in (corner_a, corner_b)]
        for n, (side, first_block) in enumerate(((corner_a, 2 * wedge.blocks), (band_b, 0))):
            above = a_above == (n == 0)
            near = d + layers if above else d - 1
            where = pl.ds(d + layers if above else 0, d)

            def own_pair(pair, carry):
                for i in range(2):
                    part = slice(i * d, i * d + d)
                    row = d + 2 * pair + i
                    for c in range(comps):
                        t0[c, row, where] = side[first_block + c * (rows // 2) + pair, part]
                        ux[c, row, where] = side[first_block + (comps + c) * (rows // 2) + pair, part]
                    kx[row, where] = side[first_block + 2 * comps * (rows // 2) + pair, part]
                    mx[row, where] = side[first_block + (2 * comps + 1) * (rows // 2) + pair, part]
                return carry

            lax.fori_loop(0, rows // 2, own_pair, 0, unroll=True)
            for m, (block, at) in enumerate(corners[n]):
                above_m = sector_even if m == 0 else jnp.logical_not(sector_even)
                for step in range(1, d + 1):
                    row = jnp.where(above_m, d + rows - 1 + step, d - step)
                    count, start = wedge.counts[step - 1], wedge.starts[step - 1]
                    part = slice(start, start + count)
                    near_rows = slice(near, near + count) if above else slice(near + 1 - count, near + 1)
                    for c in range(comps):
                        t0[c, row, near_rows] = block[at + c, part]
                        ux[c, row, near : near + 1] = block[at + wedge.disp + c, d + step - 1 : d + step]
                    kx[row, near_rows] = block[at + wedge.stiff, part]
                    mx[row, near_rows] = block[at + wedge.mass, part]
                nearest = jnp.where(above_m, d + rows, d - 1)
                for c in range(comps):
                    ux[c, nearest, where] = block[at + wedge.disp + c, 0:d]

    @pl.when(band_even)
    def _():
        place_bands(True)

    @pl.when(jnp.logical_not(band_even))
    def _():
        place_bands(False)

    lane = lax.broadcasted_iota(jnp.int32, (all_layers, width), 1)
    layer = lax.broadcasted_iota(jnp.int32, (all_layers, width), 0)

    raft[...] = jnp.zeros_like(raft)
    payload[...] = jnp.zeros_like(payload)

    @pl.when(band == 0)
    def _():
        around = (sector, lax.rem(sector + 1, sectors), lax.rem(sector + sectors - 1, sectors))
        rows_of = jnp.concatenate([survey[pl.ds(x * bands, bands)] for x in around], axis=0)
        known = jnp.concatenate(
            [pltpu.roll(rows_of, 128 - PARAM_AT - PARAMS * j, 1) for j in range(bearings)], axis=0
        )
        each = len(around) * bands
        count = bearings * each
        within = lax.rem(lax.broadcasted_iota(jnp.int32, (count, 1), 0), each)
        shift = jnp.where(within < bands, d, jnp.where(within < 2 * bands, d + rows, d - rows))
        column = lambda p: known[:, p : p + 1]
        row_of = column(PARAM_ROW).astype(jnp.int32) + shift
        row_of = jnp.broadcast_to(row_of, (count, width))
        lane_of = jnp.broadcast_to(column(PARAM_LANE).astype(jnp.int32), (count, width))
        here = lane_of == lax.broadcasted_iota(jnp.int32, (count, width), 1)
        at_node = [jnp.zeros((count, width), F32) for _ in range(comps)]
        for a in range(all_rows):
            hit = row_of == a
            for c in range(comps):
                at_node[c] = jnp.where(hit, ux[c, a, d : d + 1], at_node[c])
        stick = jnp.broadcast_to(column(PARAM_STICK), (count, width))
        force = bearing_law(
            at_node[:2], at_node[2], stick,
            [column(PARAM_SLIP), column(PARAM_SLIP + 1)], [column(PARAM_OLD), column(PARAM_OLD + 1)], column(PARAM_WEIGHT),
        )
        force = [jnp.where(here, f, 0.0) for f in force]
        stiffness = [jnp.where(here & (stick == 1.0), K_STICK, 0.0), jnp.where(here, K_VERT, 0.0)]
        for a in range(all_rows):
            hit = row_of == a
            for q, value in enumerate(force + stiffness):
                raft[q, a : a + 1] = jnp.sum(jnp.where(hit, value, 0.0), axis=0, keepdims=True)
        place_of = lax.broadcasted_iota(jnp.int32, payload.shape, 0) - sector * bands
        col = lax.broadcasted_iota(jnp.int32, payload.shape, 1)
        reply = jnp.zeros(payload.shape, F32)
        for c in range(comps):
            total = jnp.sum(force[c], axis=1, keepdims=True)
            for q in range(bands):
                for j in range(bearings):
                    value = total[j * each + q : j * each + q + 1]
                    reply = jnp.where((place_of == q) & (col == FORCE_AT + c * bearings + j), value, reply)
        payload[...] = reply

    interface = (layer == d - 1) | (layer == d + layers - 1)

    def faces(a, carry):
        k = kx[a]
        k_h = conductance(k, ahead(k, 0))
        kh[a] = k_h
        kr[a] = jnp.where(lane < width - 1, conductance(k, ahead(k, 1)), 0.0)
        ks[a] = conductance(k, kx[jnp.minimum(a + 1, all_rows - 1)])
        for c in range(comps):
            v = ux[c, a]
            flux = jnp.where(interface, k_h * (ahead(v, 0) - v), 0.0)
            change = COMPONENT_SCALE[c] * (flux - behind(flux, 0))
            change = change - jnp.where(layer == d, raft[c, pl.ds(a, 1)], 0.0)
            t0[c, a] = t0[c, a] + change
        return carry

    lax.fori_loop(0, all_rows, faces, 0, unroll=True)
    for a in (d - 1, d + rows - 1):
        for c in range(comps):
            flux = COMPONENT_SCALE[c] * (ks[a] * (ux[c, a + 1] - ux[c, a]))
            t0[c, a] = t0[c, a] + flux
            t0[c, a + 1] = t0[c, a + 1] - flux

    def diagonals(a, carry):
        k_h, k_r = kh[a], kr[a]
        around = k_h + behind(k_h, 0) + k_r + behind(k_r, 1) + ks[a] + ks[a - 1]
        diag[0, a] = mx[a] + COMPONENT_SCALE[0] * around + jnp.where(layer == d, raft[comps, pl.ds(a, 1)], 0.0)
        diag[1, a] = mx[a] + COMPONENT_SCALE[2] * around + jnp.where(layer == d, raft[comps + 1, pl.ds(a, 1)], 0.0)
        return carry

    lax.fori_loop(1, all_rows - 1, diagonals, 0, unroll=True)

    levels = (t0, t1, t2, t3, t4)
    shift_of, link_of = coefficients(survey[...])
    for step in range(1, ITERS + 1):
        src, dst = levels[step - 1], levels[step]
        a_k = jnp.broadcast_to(shift_of[step - 1], (all_layers, width))
        c_k = jnp.broadcast_to(link_of[step - 1], (all_layers, width)) if step > 1 else None

        def apply(a, carry):
            k_h, k_r, k_next, k_back = kh[a], kr[a], ks[a], ks[a - 1]
            for c in range(comps):
                v = src[c, a]
                around = k_next * src[c, a + 1] + k_back * src[c, a - 1]
                around = around + (k_h * ahead(v, 0) + behind(k_h * v, 0))
                around = around + (k_r * ahead(v, 1) + behind(k_r * v, 1))
                centre = (diag[0 if c < 2 else 1, a] - a_k) * v
                if step > 1:
                    centre = centre - c_k * levels[step - 2][c, a]
                dst[c, a] = centre - (around if COMPONENT_SCALE[c] == 1.0 else COMPONENT_SCALE[c] * around)
            return carry

        lax.fori_loop(step, all_rows - step, apply, 0, unroll=True)

    pairs = gram_pairs()
    outs = (b0, b1, b2, b3, b4)

    def products(a, sums):
        for c in range(comps):
            block = [t[c, d + a, own] for t in levels]
            for out, x in zip(outs, block):
                out[c, a] = x
            sums = tuple(
                s + dot(block[i], block[j]) for s, (i, j) in zip(sums, pairs)
            )
        return sums

    sums = lax.fori_loop(0, rows, products, tuple(jnp.zeros((8, width), F32) for _ in pairs))
    col = lax.broadcasted_iota(jnp.int32, payload.shape, 1)
    reply = payload[...]
    for p, s in enumerate(sums):
        reply = jnp.where(col == p, total_of(s), reply)
    payload[...] = reply


def combine_kernel(received, survey, b0, b1, b2, b3, b4, increment, residual, force, *, bearings, bands):
    comps, rows, layers, width = b0.shape
    sector = lax.axis_index("sector")
    total = jnp.sum(received[...], axis=0, keepdims=True)
    col = lax.broadcasted_iota(jnp.int32, total.shape, 1)
    table = {ij: jnp.sum(jnp.where(col == p, total, 0.0), axis=1, keepdims=True) for p, ij in enumerate(gram_pairs())}
    shift_of, link_of = coefficients(survey[...])
    g = lambda i, j: table[min(i, j), max(i, j)]
    zero, one = jnp.zeros_like(table[0, 0]), jnp.ones_like(table[0, 0])
    res = [one] + [zero] * ITERS
    direction, inc = list(res), [zero] * (ITERS + 1)
    norm = table[0, 0]
    for it in range(ITERS):
        image = [zero] * (ITERS + 1)
        for i in range(it + 1):
            image[i] = image[i] + shift_of[i] * direction[i]
            image[i + 1] = image[i + 1] + direction[i]
            if i:
                image[i - 1] = image[i - 1] + link_of[i] * direction[i]
        product = sum(
            direction[i] * sum(image[j] * g(i, j) for j in range(it + 2)) for i in range(it + 1)
        )
        alpha = norm / product
        inc = [x + alpha * y for x, y in zip(inc, direction)]
        res = [x - alpha * y for x, y in zip(res, image)]
        if it + 1 < ITERS:
            norm_next = sum(res[i] * sum(res[j] * g(i, j) for j in range(it + 2)) for i in range(it + 2))
            ratio = norm_next / norm
            direction = [x + ratio * y for x, y in zip(res, direction)]
            norm = norm_next
    basis = (b0, b1, b2, b3, b4)
    inc = [jnp.broadcast_to(x, (layers, width)) for x in inc[:ITERS]]
    res = [jnp.broadcast_to(x, (layers, width)) for x in res]

    def combine(a, carry):
        for c in range(comps):
            x = [b[c, a] for b in basis]
            increment[c, a] = sum(y * z for y, z in zip(inc, x))
            residual[c, a] = sum(y * z for y, z in zip(res, x))
        return carry

    lax.fori_loop(0, rows, combine, 0)
    mine = received[pl.ds(sector * bands, 1)]
    for c in range(comps):
        force[c : c + 1] = mine[:, FORCE_AT + c * bearings : FORCE_AT + (c + 1) * bearings]


def kernel_call(body, outs, operands, far=(), scratch=(), grant=VMEM_LIMIT):
    vmem = pl.BlockSpec(memory_space=pltpu.VMEM)
    return pl.pallas_call(
        body,
        out_shape=[jax.ShapeDtypeStruct(s, F32) for s in outs],
        in_specs=[pl.BlockSpec(memory_space=pltpu.HBM) if i in far else vmem for i in range(len(operands))],
        out_specs=[vmem] * len(outs),
        scratch_shapes=[pltpu.VMEM(s, F32) if isinstance(s, tuple) else s for s in scratch],
        compiler_params=pltpu.CompilerParams(vmem_limit_bytes=grant),
    )(*operands)


def pair_up(i, n):
    return i ^ 1


def pair_down(i, n):
    return (((i + 1) % n) ^ 1) - 1 if ((i + 1) % n) ^ 1 else n - 1


def per_device(
    given_load, displacement, mass_coef, stiffness, bearing_node, stick_state, slip_prev, bearing_old, bearing_weight
):
    comps, rows, layers, radial = displacement.shape
    bearings = bearing_node.shape[0]
    sectors, bands = lax.axis_size("sector"), lax.axis_size("band")
    d = DEPTH
    slab, wedge = SectorSlab(comps, layers), Wedge(comps)

    def exchange(x, sector_partner=None, band_partner=None):
        pairs = []
        for s in range(sectors):
            for b in range(bands):
                t = s if sector_partner is None else sector_partner(s, sectors)
                q = b if band_partner is None else band_partner(b)
                if 0 <= q < bands:
                    pairs.append((s * bands + b, t * bands + q))
        return lax.ppermute(x, AXES, pairs)

    inner = lambda b: -1 if b in (0, bands - 1) else ((b + 1) ^ 1) - 1

    field, block = displacement.shape, mass_coef.shape
    slab_shape, band_shape = (slab.rows, radial), ((2 * comps + 2) * (rows // 2), 2 * d, radial)
    small = [
        pltpu.SMEM((bearings,), jnp.int32),
        pltpu.SMEM((bearings,), jnp.int32),
        pltpu.SMEM((2, bearings), F32),
        pltpu.SMEM((2, bearings), F32),
        pltpu.SMEM((bearings,), F32),
    ]
    work, slab_a, slab_b, band_b = kernel_call(
        functools.partial(local_kernel, radial=radial),
        [(2 * comps + 5, *block), slab_shape, slab_shape, band_shape],
        (displacement, given_load, mass_coef, stiffness, bearing_node, stick_state, slip_prev, bearing_old, bearing_weight),
        far=range(9),
        grant=VMEM_WHOLE,
        scratch=[field, *small, pltpu.SemaphoreType.DMA((9,))],
    )
    outer = lambda b: b ^ 1
    slab_b = exchange(slab_b, pair_down)
    slab_a = exchange(slab_a, pair_up)
    band_b = exchange(band_b, None, inner)
    (survey,) = kernel_call(survey_kernel, [(sectors * bands, 128)], (work,), scratch=[field] * 3)
    survey = lax.all_to_all(survey, AXES, 0, 0, tiled=True)
    corner_a, corner_b = kernel_call(
        functools.partial(corner_kernel, comps=comps, layers=layers),
        [(2 * wedge.blocks + band_shape[0], 2 * d, radial), (2 * wedge.blocks, 2 * d, radial)],
        (slab_a, slab_b, work, survey, band_b),
    )
    corner_b = exchange(corner_b, None, inner)
    corner_a = exchange(corner_a, None, outer)
    devices = sectors * bands
    extended = (rows + 2 * d, layers + 2 * d, radial)
    *basis, payload = kernel_call(
        functools.partial(power_kernel, bearings=bearings, sectors=sectors, bands=bands),
        [field] * (ITERS + 1) + [(devices, 128)],
        (work, slab_a, slab_b, band_b, corner_a, corner_b, survey),
        scratch=[(comps, *extended)] * (ITERS + 2) + [extended] * 5 + [(2, *extended), (comps + 2, rows + 2 * d, radial)],
    )
    received = lax.all_to_all(payload, AXES, 0, 0, tiled=True)
    increment, residual, force = kernel_call(
        functools.partial(combine_kernel, bearings=bearings, bands=bands),
        [field, field, (comps, bearings)],
        (received, survey, *basis),
    )
    return (increment, residual, force)


def solution(mesh):
    return jax.shard_map(
        per_device,
        mesh=mesh,
        in_specs=(
            P(None, "sector", "band", None),
            P(None, "sector", "band", None),
            P("sector", "band", None),
            P("sector", "band", None),
            P(("sector", "band")),
            P(("sector", "band")),
            P(None, ("sector", "band")),
            P(None, ("sector", "band")),
            P(("sector", "band")),
        ),
        out_specs=(
            P(None, "sector", "band", None),
            P(None, "sector", "band", None),
            P(None, ("sector", "band")),
        ),
        check_vma=False,
    )
```

```python
import functools

import jax
import jax.numpy as jnp
from jax import lax
from jax.experimental import pallas as pl
from jax.experimental.pallas import tpu as pltpu
from jax.sharding import PartitionSpec as P

ITERS = 4
DEPTH = ITERS

K_STICK = 4.0
K_VERT = 8.0
MU_FAST = 0.15
MU_SLOW = 0.04
RATE_GAIN = 2.0
RATE_DECAY = 2.0
V_FLOOR = 0.05
COMPONENT_SCALE = (1.0, 1.0, 2.0)

STATS = 1 + 2 * (ITERS - 1)
TINY = 1e-30
FLOOR = 0.25

AXES = ("sector", "band")
F32 = jnp.float32
PARAM_ROW, PARAM_LANE, PARAM_STICK, PARAM_SLIP, PARAM_OLD, PARAM_WEIGHT = (0, 1, 2, 3, 5, 7)
PARAMS = 8
PARAM_AT = 32
FORCE_AT = 64
VMEM_LIMIT = 24 * 1024 * 1024
TILE = 8


def conductance(left, right):
    return 2.0 * left * right / jnp.maximum(left + right, FLOOR)


def ahead(x, axis):
    return pltpu.roll(x, x.shape[axis] - 1, axis)


def behind(x, axis):
    return pltpu.roll(x, 1, axis)


def round_up(n, multiple):
    return -(-n // multiple) * multiple


def put_band(out, at, r, u, stiff, mass, top):
    comps, rows, layers, _ = r.shape
    fields = [r.at[c] for c in range(comps)] + [u.at[c] for c in range(comps)] + [stiff, mass]
    for f, field in enumerate(fields):
        for pair in range(rows // 2):
            planes = [field[2 * pair + i] for i in range(2)]
            high = jnp.concatenate([x[layers - DEPTH :] for x in planes], axis=0)
            low = jnp.concatenate([x[:DEPTH] for x in planes], axis=0)
            out[at + f * (rows // 2) + pair] = jnp.where(top, high, low)


class SectorSlab:
    def __init__(self, comps, layers):
        d = DEPTH
        self.layers = layers
        self.stiff = comps * d * layers
        self.mass = self.stiff + d * layers
        self.disp = self.mass + (d - 1) * layers
        self.low = self.disp + comps * layers
        self.high = self.low + comps * d
        self.rows = round_up(self.high + comps * d, 8)

    def residual_at(self, c, i):
        return (c * DEPTH + i) * self.layers


def parts_of(work):
    comps = (work.shape[0] - 5) // 2
    return work.at[0:comps], work.at[comps : 2 * comps], work.at[2 * comps : 2 * comps + 3], work.at[2 * comps + 3], work.at[2 * comps + 4]


def local_kernel(
    u_far, load_far, mass_far, stiff_far, node_far, stick_far, slip_far, old_far, weight_far,
    work, slab_a, slab_b, band_b,
    load, node, stick, slip, old, weight, arrived, *, radial,
):
    comps, rows, layers, width = load.shape
    d = DEPTH
    r, u, cond, mass, stiff = parts_of(work)
    fields = ((stiff_far, stiff), (u_far, u), (mass_far, mass), (load_far, load))
    small = ((node_far, node), (stick_far, stick), (slip_far, slip), (old_far, old), (weight_far, weight))
    moves = [pltpu.make_async_copy(src, dst, arrived.at[n]) for n, (src, dst) in enumerate(fields + small)]
    for move in moves:
        move.start()
    lane = lax.broadcasted_iota(jnp.int32, (layers, width), 1)
    layer = lax.broadcasted_iota(jnp.int32, (layers, width), 0)
    moves[0].wait()
    for a in range(rows):
        k = stiff[a]
        cond[0, a] = jnp.where(lane < width - 1, conductance(k, ahead(k, 1)), 0.0)
        cond[1, a] = jnp.where(layer < layers - 1, conductance(k, ahead(k, 0)), 0.0)
        cond[2, a] = conductance(k, stiff[a + 1]) if a + 1 < rows else jnp.zeros((layers, width), F32)
    for move in moves[1 : len(fields)]:
        move.wait()
    before = [None] * comps
    for a in range(rows):
        k_r, k_h, k_s = cond[0, a], cond[1, a], cond[2, a]
        m = mass[a]
        for c in range(comps):
            v = u[c, a]
            flux_r = k_r * (ahead(v, 1) - v)
            flux_h = k_h * (ahead(v, 0) - v)
            total = flux_r - behind(flux_r, 1) + flux_h - behind(flux_h, 0)
            if before[c] is not None:
                total = total - before[c]
            if a + 1 < rows:
                before[c] = k_s * (u[c, a + 1] - v)
                total = total + before[c]
            r[c, a] = load[c, a] - m * v + COMPONENT_SCALE[c] * total

    for move in moves[len(fields) :]:
        move.wait()
    col = lax.broadcasted_iota(jnp.int32, (8, 128), 1)
    tile = jnp.zeros((8, 128), F32)
    for j in range(node.shape[0]):
        at = node[j] // radial
        values = {
            PARAM_ROW: at.astype(F32),
            PARAM_LANE: (node[j] - at * radial).astype(F32),
            PARAM_STICK: stick[j].astype(F32),
            PARAM_SLIP: slip[0, j],
            PARAM_SLIP + 1: slip[1, j],
            PARAM_OLD: old[0, j],
            PARAM_OLD + 1: old[1, j],
            PARAM_WEIGHT: weight[j],
        }
        for p, value in values.items():
            tile = jnp.where(col == PARAM_AT + PARAMS * j + p, value, tile)
    cond[2, rows - 1, 0:8, 0:128] = tile

    slab = SectorSlab(comps, layers)
    even = lax.rem(lax.axis_index("sector"), 2) == 0
    for out, upper in ((slab_a, even), (slab_b, jnp.logical_not(even))):
        first = jnp.where(upper, rows - d, 0)
        for i in range(d):
            for c in range(comps):
                out[pl.ds(slab.residual_at(c, i), layers)] = r[c, first + i]
                out[pl.ds(slab.low + c * d + i, 1)] = u[c, first + i, 0:1]
                out[pl.ds(slab.high + c * d + i, 1)] = u[c, first + i, layers - 1 : layers]
            out[pl.ds(slab.stiff + i * layers, layers)] = stiff[first + i]
        for i in range(d - 1):
            out[pl.ds(slab.mass + i * layers, layers)] = mass[jnp.where(upper, rows - (d - 1), 0) + i]
        for c in range(comps):
            out[pl.ds(slab.disp + c * layers, layers)] = u[c, jnp.where(upper, rows - 1, 0)]
        end = slab.high + comps * d
        if slab.rows > end:
            out[pl.ds(end, slab.rows - end)] = jnp.zeros((slab.rows - end, width), F32)

    even = lax.rem(lax.axis_index("band"), 2) == 0
    put_band(band_b, 0, r, u, stiff, mass, jnp.logical_not(even))


REACH = [DEPTH] + [max(DEPTH - n, 1) for n in range(2, DEPTH + 1)]


class Wedge:
    counts = REACH
    starts = [sum(REACH[:n]) for n in range(DEPTH)]
    height = round_up(sum(REACH), 8)

    def __init__(self, comps):
        self.stiff, self.mass, self.disp = comps, comps + 1, comps + 2
        self.blocks = 2 * comps + 2


def padded_block(parts):
    parts = list(parts)
    spare = Wedge.height - sum(p.shape[0] for p in parts)
    if spare:
        parts.append(jnp.zeros((spare, parts[0].shape[1]), F32))
    return jnp.concatenate(parts, axis=0)


def put_wedge(out, at, comps, layers, top, residual, stiff, mass, disp, edges):
    wedge, d = Wedge(comps), DEPTH
    sources = [functools.partial(residual, c) for c in range(comps)] + [stiff, mass]
    for f, source in enumerate(sources):
        planes = [source(n) for n in range(1, d + 1)]
        high = padded_block(p[layers - k :] for p, k in zip(planes, wedge.counts))
        low = padded_block(p[:k] for p, k in zip(planes, wedge.counts))
        out[at + f] = jnp.where(top, high, low)
    for c in range(comps):
        row, rims = disp(c), [edges(c, n) for n in range(1, d + 1)]
        high = padded_block([row[layers - d :]] + [rim[1] for rim in rims])
        low = padded_block([row[:d]] + [rim[0] for rim in rims])
        out[at + wedge.disp + c] = jnp.where(top, high, low)


def corner_kernel(slab_a, slab_b, work, survey, band_b, corner_a, corner_b, *, comps, layers):
    d = DEPTH
    slab, wedge = SectorSlab(comps, layers), Wedge(comps)
    band_even = lax.rem(lax.axis_index("band"), 2) == 0
    sector_even = lax.rem(lax.axis_index("sector"), 2) == 0
    for n, (side, above) in enumerate(((slab_a, sector_even), (slab_b, jnp.logical_not(sector_even)))):

        def plane(offset, side=side):
            return side[pl.ds(pl.multiple_of(offset, 8), layers)]

        def step(n, count, above=above):
            return jnp.where(above, n - 1, count - n)

        for out, top in ((corner_a, band_even), (corner_b, jnp.logical_not(band_even))):
            put_wedge(
                out,
                n * wedge.blocks,
                comps,
                layers,
                top,
                lambda c, n: plane(slab.residual_at(c, step(n, d))),
                lambda n: plane(slab.stiff + step(n, d) * layers),
                lambda n: plane(slab.mass + step(min(n, d - 1), d - 1) * layers),
                lambda c: plane(slab.disp + c * layers),
                lambda c, n: [side[pl.ds(at + c * d + step(n, d), 1)] for at in (slab.low, slab.high)],
            )
    r, u, _, mass, stiff = parts_of(work)
    put_band(corner_a, 2 * wedge.blocks, r, u, stiff, mass, band_even)


def dot(x, y):
    return jnp.sum((x * y).reshape(x.shape[0] // 8, 8, x.shape[1]), axis=0)


def total_of(x):
    return jnp.sum(jnp.sum(x, axis=0, keepdims=True), axis=1, keepdims=True)


def survey_kernel(work, row, image, basis_1, basis_2):
    r, _, cond, mass, _ = parts_of(work)
    comps, rows, layers, width = r.shape
    zero = jnp.zeros((8, width), F32)

    def apply(src):
        norm, product = zero, zero
        for a in range(rows):
            k_r, k_h, k_next = cond[0, a], cond[1, a], cond[2, a]
            for c in range(comps):
                v = src[c, a]
                flux_r = k_r * (ahead(v, 1) - v)
                flux_h = k_h * (ahead(v, 0) - v)
                total = flux_r - behind(flux_r, 1) + flux_h - behind(flux_h, 0)
                if a + 1 < rows:
                    total = total + k_next * (src[c, a + 1] - v)
                if a:
                    total = total - cond[2, a - 1] * (v - src[c, a - 1])
                out = mass[a] * v - COMPONENT_SCALE[c] * total
                image[c, a] = out
                norm, product = norm + dot(v, v), product + dot(v, out)
        return total_of(norm), total_of(product)

    level, back, weight_here, stats = r, None, None, []
    outs = (basis_1, basis_2)
    norm_back = None
    for step in range(ITERS - 1):
        norm, product = apply(level)
        if step:
            stats.append(norm / jnp.maximum(norm_back, TINY))
        else:
            weight_here = norm
        stats.append(product / jnp.maximum(norm, TINY))
        if step < ITERS - 2:
            a_k = jnp.broadcast_to(stats[-1], (layers, width))
            c_k = jnp.broadcast_to(stats[-2], (layers, width)) if step else None
            for a in range(rows):
                for c in range(comps):
                    x = image[c, a] - a_k * level[c, a]
                    outs[step][c, a] = x if back is None else x - c_k * back[c, a]
            back, level, norm_back = level, outs[step], norm
        else:
            a_k = jnp.broadcast_to(stats[-1], (layers, width))
            c_k = jnp.broadcast_to(stats[-2], (layers, width))
            last = zero
            for a in range(rows):
                for c in range(comps):
                    x = image[c, a] - a_k * level[c, a] - c_k * back[c, a]
                    last = last + dot(x, x)
            stats.append(total_of(last) / jnp.maximum(norm, TINY))
    col = lax.broadcasted_iota(jnp.int32, (8, 128), 1)
    tile = jnp.where(col == 0, weight_here, 0.0)
    for n, value in enumerate(stats):
        tile = jnp.where(col == 1 + n, weight_here * value, tile)
    tile = tile + cond[2, rows - 1, 0:8, 0:128]
    for n in range(row.shape[0] // 8):
        row[8 * n : 8 * n + 8] = tile


def coefficients(survey):
    total = jnp.sum(survey, axis=0, keepdims=True)
    col = lax.broadcasted_iota(jnp.int32, total.shape, 1)
    pick = lambda n: jnp.sum(jnp.where(col == n, total, 0.0), axis=1, keepdims=True)
    weight = jnp.maximum(pick(0), TINY)
    stats = [pick(n) / weight for n in range(1, STATS)]
    a, c = stats[0::2], stats[1::2]
    return a + [a[-1]], [None] + c


def bearing_law(moved, vertical, stick, slip, old, weight):
    trial = [K_STICK * (moved[i] - slip[i]) for i in range(2)]
    rate = [RATE_GAIN * (moved[i] - old[i]) for i in range(2)]
    slip_speed = jnp.sqrt(rate[0] * rate[0] + rate[1] * rate[1] + V_FLOOR * V_FLOOR)
    friction = MU_FAST - (MU_FAST - MU_SLOW) * jnp.exp(-RATE_DECAY * slip_speed)
    capacity = friction * weight
    magnitude = jnp.sqrt(trial[0] * trial[0] + trial[1] * trial[1])
    largest = jnp.maximum(magnitude, capacity)
    forces = [jnp.where(stick == 1.0, t, capacity * t / largest) for t in trial]
    return forces + [K_VERT * vertical]


def gram_pairs():
    return [(i, j) for i in range(ITERS) for j in range(i, ITERS + 1)]


def place_wedge(t, ux, kx, mx, block, at, wedge, comps, rows, above, near, upward):
    d = DEPTH
    for step in range(1, d + 1):
        row = jnp.where(above, d + rows - 1 + step, d - step)
        count, start = wedge.counts[step - 1], wedge.starts[step - 1]
        part = slice(start, start + count)
        where = slice(near, near + count) if upward else slice(near + 1 - count, near + 1)
        for c in range(comps):
            t[c, row, where] = block[at + c, part]
            ux[c, row, near : near + 1] = block[at + wedge.disp + c, d + step - 1 : d + step]
        kx[row, where] = block[at + wedge.stiff, part]
        mx[row, where] = block[at + wedge.mass, part]
    nearest = jnp.where(above, d + rows, d - 1)
    for c in range(comps):
        ux[c, nearest, slice(near, near + d) if upward else slice(near + 1 - d, near + 1)] = block[at + wedge.disp + c, 0:d]


def early_kernel(
    work, slab_a, slab_b, band_b, corner_a, survey,
    t0, t1, t2, t3, t4, kx, kh, late_t, late_u, late_m, raft, payload,
    raw, ux, mx, ks, kr, diag,
    *, bearings, sectors, bands,
):
    r, u, _, mass, stiff = parts_of(work)
    comps, rows, layers, width = r.shape
    d = DEPTH
    slab, wedge = SectorSlab(comps, layers), Wedge(comps)
    sector, band = lax.axis_index("sector"), lax.axis_index("band")
    sector_even = lax.rem(sector, 2) == 0
    band_even = lax.rem(band, 2) == 0
    all_rows, all_layers = rows + 2 * d, layers + 2 * d
    own = pl.ds(d, layers)

    for a in range(rows):
        for c in range(comps):
            raw[c, d + a, own] = r[c, a]
            ux[c, d + a, own] = u[c, a]
        kx[d + a, own] = stiff[a]
        mx[d + a, own] = mass[a]
    sides = ((slab_a, sector_even), (slab_b, jnp.logical_not(sector_even)))
    for side, above in sides:
        base = jnp.where(above, d + rows, 0)
        nearest = jnp.where(above, d + rows, d - 1)
        for i in range(d):
            for c in range(comps):
                raw[c, base + i, own] = side[pl.ds(slab.residual_at(c, i), layers)]
                ux[c, base + i, d : d + 1] = side[pl.ds(slab.low + c * d + i, 1)]
                ux[c, base + i, d + layers - 1 : d + layers] = side[pl.ds(slab.high + c * d + i, 1)]
            kx[base + i, own] = side[pl.ds(slab.stiff + i * layers, layers)]
        for i in range(d - 1):
            mx[jnp.where(above, d + rows, 1) + i, own] = side[pl.ds(slab.mass + i * layers, layers)]
        for c in range(comps):
            ux[c, nearest, own] = side[pl.ds(slab.disp + c * layers, layers)]

    def place_bands(even):
        for side, first_block, upward in ((corner_a, 2 * wedge.blocks, even), (band_b, 0, not even)):
            where = pl.ds(d + layers if upward else 0, d)
            for a in range(rows):
                part = slice((a % 2) * d, (a % 2) * d + d)
                block = lambda f: side[first_block + f * (rows // 2) + a // 2, part]
                for c in range(comps):
                    raw[c, d + a, where] = block(c)
                    ux[c, d + a, where] = block(comps + c)
                kx[d + a, where] = block(2 * comps)
                mx[d + a, where] = block(2 * comps + 1)
        near = d + layers if even else d - 1
        for m, (_, above) in enumerate(sides):
            place_wedge(raw, ux, kx, mx, corner_a, m * wedge.blocks, wedge, comps, rows, above, near, even)
        late = pl.ds(0 if even else all_layers - TILE, TILE)
        for a in range(all_rows):
            for c in range(comps):
                late_t[c, a] = raw[c, a, late]
                late_u[c, a] = ux[c, a, late]
            late_m[a] = mx[a, late]

    @pl.when(band_even)
    def _():
        place_bands(True)

    @pl.when(jnp.logical_not(band_even))
    def _():
        place_bands(False)

    lane = lax.broadcasted_iota(jnp.int32, (all_layers, width), 1)
    layer = lax.broadcasted_iota(jnp.int32, (all_layers, width), 0)

    raft[...] = jnp.zeros_like(raft)
    payload[...] = jnp.zeros_like(payload)

    @pl.when(band == 0)
    def _():
        around = (sector, lax.rem(sector + 1, sectors), lax.rem(sector + sectors - 1, sectors))
        rows_of = jnp.concatenate([survey[pl.ds(x * bands, bands)] for x in around], axis=0)
        known = jnp.concatenate(
            [pltpu.roll(rows_of, 128 - PARAM_AT - PARAMS * j, 1) for j in range(bearings)], axis=0
        )
        each = len(around) * bands
        count = bearings * each
        within = lax.rem(lax.broadcasted_iota(jnp.int32, (count, 1), 0), each)
        shift = jnp.where(within < bands, d, jnp.where(within < 2 * bands, d + rows, d - rows))
        column = lambda p: known[:, p : p + 1]
        row_of = column(PARAM_ROW).astype(jnp.int32) + shift
        row_of = jnp.broadcast_to(row_of, (count, width))
        lane_of = jnp.broadcast_to(column(PARAM_LANE).astype(jnp.int32), (count, width))
        here = lane_of == lax.broadcasted_iota(jnp.int32, (count, width), 1)
        at_node = [jnp.zeros((count, width), F32) for _ in range(comps)]
        for a in range(all_rows):
            hit = row_of == a
            for c in range(comps):
                at_node[c] = jnp.where(hit, ux[c, a, d : d + 1], at_node[c])
        stick = jnp.broadcast_to(column(PARAM_STICK), (count, width))
        force = bearing_law(
            at_node[:2], at_node[2], stick,
            [column(PARAM_SLIP), column(PARAM_SLIP + 1)], [column(PARAM_OLD), column(PARAM_OLD + 1)], column(PARAM_WEIGHT),
        )
        force = [jnp.where(here, f, 0.0) for f in force]
        stiffness = [jnp.where(here & (stick == 1.0), K_STICK, 0.0), jnp.where(here, K_VERT, 0.0)]
        for a in range(all_rows):
            hit = row_of == a
            for q, value in enumerate(force + stiffness):
                raft[q, a : a + 1] = jnp.sum(jnp.where(hit, value, 0.0), axis=0, keepdims=True)
        place_of = lax.broadcasted_iota(jnp.int32, payload.shape, 0) - sector * bands
        col = lax.broadcasted_iota(jnp.int32, payload.shape, 1)
        reply = jnp.zeros(payload.shape, F32)
        for c in range(comps):
            total = jnp.sum(force[c], axis=1, keepdims=True)
            for q in range(bands):
                for j in range(bearings):
                    value = total[j * each + q : j * each + q + 1]
                    reply = jnp.where((place_of == q) & (col == FORCE_AT + c * bearings + j), value, reply)
        payload[...] = reply

    interface = (layer == d - 1) | (layer == d + layers - 1)

    def faces(a, carry):
        k = kx[a]
        k_h = conductance(k, ahead(k, 0))
        kh[a] = k_h
        kr[a] = jnp.where(lane < width - 1, conductance(k, ahead(k, 1)), 0.0)
        ks[a] = conductance(k, kx[jnp.minimum(a + 1, all_rows - 1)])
        for c in range(comps):
            v = ux[c, a]
            flux = jnp.where(interface, k_h * (ahead(v, 0) - v), 0.0)
            change = COMPONENT_SCALE[c] * (flux - behind(flux, 0))
            change = change - jnp.where(layer == d, raft[c, pl.ds(a, 1)], 0.0)
            t0[c, a] = raw[c, a] + change
        return carry

    lax.fori_loop(0, all_rows, faces, 0, unroll=True)
    for a in (d - 1, d + rows - 1):
        for c in range(comps):
            flux = COMPONENT_SCALE[c] * (ks[a] * (ux[c, a + 1] - ux[c, a]))
            t0[c, a] = t0[c, a] + flux
            t0[c, a + 1] = t0[c, a + 1] - flux

    def diagonals(a, carry):
        k_h, k_r = kh[a], kr[a]
        around = k_h + behind(k_h, 0) + k_r + behind(k_r, 1) + ks[a] + ks[a - 1]
        diag[0, a] = mx[a] + COMPONENT_SCALE[0] * around + jnp.where(layer == d, raft[comps, pl.ds(a, 1)], 0.0)
        diag[1, a] = mx[a] + COMPONENT_SCALE[2] * around + jnp.where(layer == d, raft[comps + 1, pl.ds(a, 1)], 0.0)
        return carry

    lax.fori_loop(1, all_rows - 1, diagonals, 0, unroll=True)

    levels = (t0, t1, t2, t3, t4)
    shift_of, link_of = coefficients(survey[...])
    for step in range(1, ITERS + 1):
        src, dst = levels[step - 1], levels[step]
        a_k = jnp.broadcast_to(shift_of[step - 1], (all_layers, width))
        c_k = jnp.broadcast_to(link_of[step - 1], (all_layers, width)) if step > 1 else None

        def apply(a, carry):
            k_h, k_r, k_next, k_back = kh[a], kr[a], ks[a], ks[a - 1]
            for c in range(comps):
                v = src[c, a]
                around = k_next * src[c, a + 1] + k_back * src[c, a - 1]
                around = around + (k_h * ahead(v, 0) + behind(k_h * v, 0))
                around = around + (k_r * ahead(v, 1) + behind(k_r * v, 1))
                centre = (diag[0 if c < 2 else 1, a] - a_k) * v
                if step > 1:
                    centre = centre - c_k * levels[step - 2][c, a]
                dst[c, a] = centre - (around if COMPONENT_SCALE[c] == 1.0 else COMPONENT_SCALE[c] * around)
            return carry

        lax.fori_loop(step, all_rows - step, apply, 0, unroll=True)


def late_kernel(
    t0, t1, t2, t3, t4, kx, kh, late_t, late_u, late_m, raft, payload_in, corner_b, survey,
    b0, b1, b2, b3, b4, payload,
    s0, s1, s2, s3, s4, raw, ux, k_tile, m_tile, ks, kh_tile, kh_back, kr, diag,
):
    comps, rows, layers, width = b0.shape
    d = DEPTH
    wedge = Wedge(comps)
    all_rows, all_layers = rows + 2 * d, layers + 2 * d
    sector_even = lax.rem(lax.axis_index("sector"), 2) == 0
    band_even = lax.rem(lax.axis_index("band"), 2) == 0
    lane = lax.broadcasted_iota(jnp.int32, (TILE, width), 1)
    layer = lax.broadcasted_iota(jnp.int32, (TILE, width), 0)
    shift_of, link_of = coefficients(survey[...])
    wide = lambda x: None if x is None else jnp.broadcast_to(x, (TILE, width))
    shift_of, link_of = [wide(x) for x in shift_of], [wide(x) for x in link_of]
    early, late = (t0, t1, t2, t3, t4), (s0, s1, s2, s3, s4)
    outs, pairs = (b0, b1, b2, b3, b4), gram_pairs()

    def run(even):
        off = 0 if even else all_layers - TILE

        def upper(x, whole, *at):
            x = ahead(x, 0)
            return jnp.where(layer == TILE - 1, whole[(*at, slice(TILE, TILE + 1))], x) if even else x

        def lower(x, whole, *at):
            x = behind(x, 0)
            return x if even else jnp.where(layer == 0, whole[(*at, slice(off - 1, off))], x)

        for a in range(all_rows):
            for c in range(comps):
                raw[c, a] = late_t[c, a]
                ux[c, a] = late_u[c, a]
            k_tile[a] = kx[a, off : off + TILE]
            m_tile[a] = late_m[a]
        near = d - 1 if even else d + layers - off
        for m, above in enumerate((sector_even, jnp.logical_not(sector_even))):
            place_wedge(raw, ux, k_tile, m_tile, corner_b, m * wedge.blocks, wedge, comps, rows, above, near, not even)

        crossing = layer == (d - 1 if even else d + layers - 1 - off)
        on_raft = layer == d
        for a in range(all_rows):
            k = k_tile[a]
            k_h = conductance(k, upper(k, kx, a))
            kh_tile[a], kh_back[a] = k_h, lower(k_h, kh, a)
            kr[a] = jnp.where(lane < width - 1, conductance(k, ahead(k, 1)), 0.0)
            if a + 1 < all_rows:
                ks[a] = conductance(k, k_tile[a + 1])
            for c in range(comps):
                v = ux[c, a]
                flux = jnp.where(crossing, k_h * (ahead(v, 0) - v), 0.0)
                change = COMPONENT_SCALE[c] * (flux - behind(flux, 0))
                if even:
                    change = change - jnp.where(on_raft, raft[c, a : a + 1], 0.0)
                s0[c, a] = raw[c, a] + change
        for a in (d - 1, d + rows - 1):
            for c in range(comps):
                flux = COMPONENT_SCALE[c] * (ks[a] * (ux[c, a + 1] - ux[c, a]))
                s0[c, a] = s0[c, a] + flux
                s0[c, a + 1] = s0[c, a + 1] - flux
        for a in range(1, all_rows - 1):
            k_r = kr[a]
            around = kh_tile[a] + kh_back[a] + k_r + behind(k_r, 1) + ks[a] + ks[a - 1]
            for n, scale in enumerate((COMPONENT_SCALE[0], COMPONENT_SCALE[2])):
                total = m_tile[a] + scale * around
                diag[n, a] = total + jnp.where(on_raft, raft[comps + n, a : a + 1], 0.0) if even else total
        for step in range(1, ITERS + 1):
            src, dst = late[step - 1], late[step]
            for a in range(step, all_rows - step):
                k_r = kr[a]
                for c in range(comps):
                    v = src[c, a]
                    around = ks[a] * src[c, a + 1] + ks[a - 1] * src[c, a - 1]
                    around = around + (
                        kh_tile[a] * upper(v, early[step - 1], c, a) + kh_back[a] * lower(v, early[step - 1], c, a)
                    )
                    around = around + (k_r * ahead(v, 1) + behind(k_r * v, 1))
                    centre = (diag[0 if c < 2 else 1, a] - shift_of[step - 1]) * v
                    if step > 1:
                        centre = centre - link_of[step - 1] * late[step - 2][c, a]
                    dst[c, a] = centre - (around if COMPONENT_SCALE[c] == 1.0 else COMPONENT_SCALE[c] * around)

        sums = [jnp.zeros((8, width), F32) for _ in pairs]
        for a in range(rows):
            for c in range(comps):
                if even:
                    block = [jnp.concatenate([x[c, d + a, d:], t[c, d + a, TILE : d + layers]], axis=0) for t, x in zip(early, late)]
                else:
                    block = [jnp.concatenate([t[c, d + a, d:off], x[c, d + a, : d + layers - off]], axis=0) for t, x in zip(early, late)]
                for out, x in zip(outs, block):
                    out[c, a] = x
                sums = [s + dot(block[i], block[j]) for s, (i, j) in zip(sums, pairs)]
        col = lax.broadcasted_iota(jnp.int32, payload.shape, 1)
        reply = payload_in[...]
        for p, s in enumerate(sums):
            reply = jnp.where(col == p, total_of(s), reply)
        payload[...] = reply

    @pl.when(band_even)
    def _():
        run(True)

    @pl.when(jnp.logical_not(band_even))
    def _():
        run(False)


def combine_kernel(received, survey, b0, b1, b2, b3, b4, increment, residual, force, *, bearings, bands):
    comps, rows, layers, width = b0.shape
    sector = lax.axis_index("sector")
    total = jnp.sum(received[...], axis=0, keepdims=True)
    col = lax.broadcasted_iota(jnp.int32, total.shape, 1)
    table = {ij: jnp.sum(jnp.where(col == p, total, 0.0), axis=1, keepdims=True) for p, ij in enumerate(gram_pairs())}
    shift_of, link_of = coefficients(survey[...])
    g = lambda i, j: table[min(i, j), max(i, j)]
    zero, one = jnp.zeros_like(table[0, 0]), jnp.ones_like(table[0, 0])
    res = [one] + [zero] * ITERS
    direction, inc = list(res), [zero] * (ITERS + 1)
    norm = table[0, 0]
    for it in range(ITERS):
        image = [zero] * (ITERS + 1)
        for i in range(it + 1):
            image[i] = image[i] + shift_of[i] * direction[i]
            image[i + 1] = image[i + 1] + direction[i]
            if i:
                image[i - 1] = image[i - 1] + link_of[i] * direction[i]
        product = sum(
            direction[i] * sum(image[j] * g(i, j) for j in range(it + 2)) for i in range(it + 1)
        )
        alpha = norm / product
        inc = [x + alpha * y for x, y in zip(inc, direction)]
        res = [x - alpha * y for x, y in zip(res, image)]
        if it + 1 < ITERS:
            norm_next = sum(res[i] * sum(res[j] * g(i, j) for j in range(it + 2)) for i in range(it + 2))
            ratio = norm_next / norm
            direction = [x + ratio * y for x, y in zip(res, direction)]
            norm = norm_next
    basis = (b0, b1, b2, b3, b4)
    inc = [jnp.broadcast_to(x, (layers, width)) for x in inc[:ITERS]]
    res = [jnp.broadcast_to(x, (layers, width)) for x in res]

    def combine(a, carry):
        for c in range(comps):
            x = [b[c, a] for b in basis]
            increment[c, a] = sum(y * z for y, z in zip(inc, x))
            residual[c, a] = sum(y * z for y, z in zip(res, x))
        return carry

    lax.fori_loop(0, rows, combine, 0)
    mine = received[pl.ds(sector * bands, 1)]
    for c in range(comps):
        force[c : c + 1] = mine[:, FORCE_AT + c * bearings : FORCE_AT + (c + 1) * bearings]


def kernel_call(body, outs, operands, far=(), scratch=()):
    vmem = pl.BlockSpec(memory_space=pltpu.VMEM)
    operands = [pltpu.with_memory_space_constraint(x, pltpu.HBM) if i in far else x for i, x in enumerate(operands)]
    return pl.pallas_call(
        body,
        out_shape=[jax.ShapeDtypeStruct(s, F32) for s in outs],
        in_specs=[pl.BlockSpec(memory_space=pltpu.HBM) if i in far else vmem for i in range(len(operands))],
        out_specs=[vmem] * len(outs),
        scratch_shapes=[pltpu.VMEM(s, F32) if isinstance(s, tuple) else s for s in scratch],
        compiler_params=pltpu.CompilerParams(vmem_limit_bytes=VMEM_LIMIT),
    )(*operands)


def pair_up(i, n):
    return i ^ 1


def pair_down(i, n):
    return (((i + 1) % n) ^ 1) - 1 if ((i + 1) % n) ^ 1 else n - 1


def per_device(
    given_load, displacement, mass_coef, stiffness, bearing_node, stick_state, slip_prev, bearing_old, bearing_weight
):
    comps, rows, layers, radial = displacement.shape
    bearings = bearing_node.shape[0]
    sectors, bands = lax.axis_size("sector"), lax.axis_size("band")
    d = DEPTH
    slab, wedge = SectorSlab(comps, layers), Wedge(comps)

    def exchange(x, sector_partner=None, band_partner=None):
        pairs = []
        for s in range(sectors):
            for b in range(bands):
                t = s if sector_partner is None else sector_partner(s, sectors)
                q = b if band_partner is None else band_partner(b)
                if 0 <= q < bands:
                    pairs.append((s * bands + b, t * bands + q))
        return lax.ppermute(x, AXES, pairs)

    inner = lambda b: -1 if b in (0, bands - 1) else ((b + 1) ^ 1) - 1

    field, block = displacement.shape, mass_coef.shape
    slab_shape, band_shape = (slab.rows, radial), ((2 * comps + 2) * (rows // 2), 2 * d, radial)
    small = [
        pltpu.SMEM((bearings,), jnp.int32),
        pltpu.SMEM((bearings,), jnp.int32),
        pltpu.SMEM((2, bearings), F32),
        pltpu.SMEM((2, bearings), F32),
        pltpu.SMEM((bearings,), F32),
    ]
    work, slab_a, slab_b, band_b = kernel_call(
        functools.partial(local_kernel, radial=radial),
        [(2 * comps + 5, *block), slab_shape, slab_shape, band_shape],
        (displacement, given_load, mass_coef, stiffness, bearing_node, stick_state, slip_prev, bearing_old, bearing_weight),
        far=range(9),
        scratch=[field, *small, pltpu.SemaphoreType.DMA((9,))],
    )
    outer = lambda b: b ^ 1
    slab_b = exchange(slab_b, pair_down)
    slab_a = exchange(slab_a, pair_up)
    band_b = exchange(band_b, None, inner)
    (survey,) = kernel_call(survey_kernel, [(sectors * bands, 128)], (work,), scratch=[field] * 3)
    survey = lax.all_to_all(survey, AXES, 0, 0, tiled=True)
    corner_a, corner_b = kernel_call(
        functools.partial(corner_kernel, comps=comps, layers=layers),
        [(2 * wedge.blocks + band_shape[0], 2 * d, radial), (2 * wedge.blocks, 2 * d, radial)],
        (slab_a, slab_b, work, survey, band_b),
    )
    corner_b = exchange(corner_b, None, inner)
    corner_a = exchange(corner_a, None, outer)
    devices = sectors * bands
    extended = (rows + 2 * d, layers + 2 * d, radial)
    all_rows = extended[0]
    tile_field, tile_block = (comps, all_rows, TILE, radial), (all_rows, TILE, radial)
    *early, payload = kernel_call(
        functools.partial(early_kernel, bearings=bearings, sectors=sectors, bands=bands),
        [(comps, *extended)] * (ITERS + 1)
        + [extended] * 2
        + [tile_field, tile_field, tile_block, (comps + 2, all_rows, radial), (devices, 128)],
        (work, slab_a, slab_b, band_b, corner_a, survey),
        scratch=[(comps, *extended)] * 2 + [extended] * 3 + [(2, *extended)],
    )
    *basis, payload = kernel_call(
        late_kernel,
        [field] * (ITERS + 1) + [(devices, 128)],
        (*early, payload, corner_b, survey),
        scratch=[tile_field] * (ITERS + 3) + [tile_block] * 6 + [(2, *tile_block)],
    )
    received = lax.all_to_all(payload, AXES, 0, 0, tiled=True)
    increment, residual, force = kernel_call(
        functools.partial(combine_kernel, bearings=bearings, bands=bands),
        [field, field, (comps, bearings)],
        (received, survey, *basis),
    )
    return (increment, residual, force)


def solution(mesh):
    return jax.shard_map(
        per_device,
        mesh=mesh,
        in_specs=(
            P(None, "sector", "band", None),
            P(None, "sector", "band", None),
            P("sector", "band", None),
            P("sector", "band", None),
            P(("sector", "band")),
            P(("sector", "band")),
            P(None, ("sector", "band")),
            P(None, ("sector", "band")),
            P(("sector", "band")),
        ),
        out_specs=(
            P(None, "sector", "band", None),
            P(None, "sector", "band", None),
            P(None, ("sector", "band")),
        ),
        check_vma=False,
    )
```

```python
import functools

import jax
import jax.numpy as jnp
from jax import lax
from jax.experimental import pallas as pl
from jax.experimental.pallas import tpu as pltpu
from jax.sharding import PartitionSpec as P

ITERS = 4
DEPTH = ITERS

K_STICK = 4.0
K_VERT = 8.0
MU_FAST = 0.15
MU_SLOW = 0.04
RATE_GAIN = 2.0
RATE_DECAY = 2.0
V_FLOOR = 0.05
COMPONENT_SCALE = (1.0, 1.0, 2.0)

STATS = 1 + 2 * (ITERS - 1)
TINY = 1e-30
FLOOR = 0.25

AXES = ("sector", "band")
F32 = jnp.float32
PARAM_ROW, PARAM_LANE, PARAM_STICK, PARAM_SLIP, PARAM_OLD, PARAM_WEIGHT = (0, 1, 2, 3, 5, 7)
PARAMS = 8
PARAM_AT = 32
FORCE_AT = 64
VMEM_LIMIT = 24 * 1024 * 1024
TILE = 8


def conductance(left, right):
    return 2.0 * left * right / jnp.maximum(left + right, FLOOR)


def ahead(x, axis):
    return pltpu.roll(x, x.shape[axis] - 1, axis)


def behind(x, axis):
    return pltpu.roll(x, 1, axis)


def shifted(x, axis, by):
    size = 8 if axis == 0 else 128
    count = x.shape[axis] // size
    parts = [lax.slice_in_dim(x, i * size, (i + 1) * size, axis=axis) for i in range(count)]
    turned = [pltpu.roll(p, size - 1 if by == 1 else 1, axis) for p in parts]
    edge = lax.broadcasted_iota(jnp.int32, parts[0].shape, axis) == (size - 1 if by == 1 else 0)
    out = [jnp.where(edge, turned[i + by], turned[i]) if 0 <= i + by < count else turned[i] for i in range(count)]
    return out[0] if count == 1 else jnp.concatenate(out, axis=axis)


def round_up(n, multiple):
    return -(-n // multiple) * multiple


def put_band(out, at, r, u, stiff, mass, top):
    comps, rows, layers, _ = r.shape
    fields = [r.at[c] for c in range(comps)] + [u.at[c] for c in range(comps)] + [stiff, mass]
    for f, field in enumerate(fields):
        for pair in range(rows // 2):
            planes = [field[2 * pair + i] for i in range(2)]
            high = jnp.concatenate([x[layers - DEPTH :] for x in planes], axis=0)
            low = jnp.concatenate([x[:DEPTH] for x in planes], axis=0)
            out[at + f * (rows // 2) + pair] = jnp.where(top, high, low)


class SectorSlab:
    def __init__(self, comps, layers):
        d = DEPTH
        self.layers = layers
        self.stiff = comps * d * layers
        self.mass = self.stiff + d * layers
        self.disp = self.mass + (d - 1) * layers
        self.low = self.disp + comps * layers
        self.high = self.low + comps * d
        self.rows = round_up(self.high + comps * d, 8)

    def residual_at(self, c, i):
        return (c * DEPTH + i) * self.layers


def parts_of(work):
    comps = (work.shape[0] - 5) // 2
    return work.at[0:comps], work.at[comps : 2 * comps], work.at[2 * comps : 2 * comps + 3], work.at[2 * comps + 3], work.at[2 * comps + 4]


def local_kernel(
    u_far, load_far, mass_far, stiff_far, node_far, stick_far, slip_far, old_far, weight_far,
    work, slab_a, slab_b, band_b,
    load, node, stick, slip, old, weight, arrived, *, radial,
):
    comps, rows, layers, width = load.shape
    d = DEPTH
    r, u, cond, mass, stiff = parts_of(work)
    half = rows // 2
    fields = [(stiff_far, stiff)]
    for part in (pl.ds(0, half), pl.ds(half, rows - half)):
        fields += [
            (u_far.at[:, part], u.at[:, part]),
            (mass_far.at[part], mass.at[part]),
            (load_far.at[:, part], load.at[:, part]),
        ]
    small = ((node_far, node), (stick_far, stick), (slip_far, slip), (old_far, old), (weight_far, weight))
    moves = [pltpu.make_async_copy(src, dst, arrived.at[n]) for n, (src, dst) in enumerate([*fields, *small])]
    for move in moves:
        move.start()
    lane = lax.broadcasted_iota(jnp.int32, (layers, width), 1)
    layer = lax.broadcasted_iota(jnp.int32, (layers, width), 0)
    moves[0].wait()
    for a in range(rows):
        k = stiff[a]
        cond[0, a] = jnp.where(lane < width - 1, conductance(k, ahead(k, 1)), 0.0)
        cond[1, a] = jnp.where(layer < layers - 1, conductance(k, ahead(k, 0)), 0.0)
        cond[2, a] = conductance(k, stiff[a + 1]) if a + 1 < rows else jnp.zeros((layers, width), F32)
    before = [None] * comps
    for a in range(rows):
        if a == 0:
            for move in moves[1:4]:
                move.wait()
        if a == half - 1:
            for move in moves[4:7]:
                move.wait()
        k_r, k_h, k_s = cond[0, a], cond[1, a], cond[2, a]
        m = mass[a]
        for c in range(comps):
            v = u[c, a]
            flux_r = k_r * (ahead(v, 1) - v)
            flux_h = k_h * (ahead(v, 0) - v)
            total = flux_r - behind(flux_r, 1) + flux_h - behind(flux_h, 0)
            if before[c] is not None:
                total = total - before[c]
            if a + 1 < rows:
                before[c] = k_s * (u[c, a + 1] - v)
                total = total + before[c]
            r[c, a] = load[c, a] - m * v + COMPONENT_SCALE[c] * total

    for move in moves[len(fields) :]:
        move.wait()
    col = lax.broadcasted_iota(jnp.int32, (8, 128), 1)
    tile = jnp.zeros((8, 128), F32)
    for j in range(node.shape[0]):
        at = node[j] // radial
        values = {
            PARAM_ROW: at.astype(F32),
            PARAM_LANE: (node[j] - at * radial).astype(F32),
            PARAM_STICK: stick[j].astype(F32),
            PARAM_SLIP: slip[0, j],
            PARAM_SLIP + 1: slip[1, j],
            PARAM_OLD: old[0, j],
            PARAM_OLD + 1: old[1, j],
            PARAM_WEIGHT: weight[j],
        }
        for p, value in values.items():
            tile = jnp.where(col == PARAM_AT + PARAMS * j + p, value, tile)
    cond[2, rows - 1, 0:8, 0:128] = tile

    slab = SectorSlab(comps, layers)
    even = lax.rem(lax.axis_index("sector"), 2) == 0
    for out, upper in ((slab_a, even), (slab_b, jnp.logical_not(even))):
        first = jnp.where(upper, rows - d, 0)
        for i in range(d):
            for c in range(comps):
                out[pl.ds(slab.residual_at(c, i), layers)] = r[c, first + i]
                out[pl.ds(slab.low + c * d + i, 1)] = u[c, first + i, 0:1]
                out[pl.ds(slab.high + c * d + i, 1)] = u[c, first + i, layers - 1 : layers]
            out[pl.ds(slab.stiff + i * layers, layers)] = stiff[first + i]
        for i in range(d - 1):
            out[pl.ds(slab.mass + i * layers, layers)] = mass[jnp.where(upper, rows - (d - 1), 0) + i]
        for c in range(comps):
            out[pl.ds(slab.disp + c * layers, layers)] = u[c, jnp.where(upper, rows - 1, 0)]
        end = slab.high + comps * d
        if slab.rows > end:
            out[pl.ds(end, slab.rows - end)] = jnp.zeros((slab.rows - end, width), F32)

    even = lax.rem(lax.axis_index("band"), 2) == 0
    put_band(band_b, 0, r, u, stiff, mass, jnp.logical_not(even))


REACH = [DEPTH] + [max(DEPTH - n, 1) for n in range(2, DEPTH + 1)]


class Wedge:
    counts = REACH
    starts = [sum(REACH[:n]) for n in range(DEPTH)]
    height = round_up(sum(REACH), 8)

    def __init__(self, comps):
        self.stiff, self.mass, self.disp = comps, comps + 1, comps + 2
        self.blocks = 2 * comps + 2


def padded_block(parts):
    parts = list(parts)
    spare = Wedge.height - sum(p.shape[0] for p in parts)
    if spare:
        parts.append(jnp.zeros((spare, parts[0].shape[1]), F32))
    return jnp.concatenate(parts, axis=0)


def put_wedge(out, at, comps, layers, top, residual, stiff, mass, disp, edges):
    wedge, d = Wedge(comps), DEPTH
    sources = [functools.partial(residual, c) for c in range(comps)] + [stiff, mass]
    for f, source in enumerate(sources):
        planes = [source(n) for n in range(1, d + 1)]
        high = padded_block(p[layers - k :] for p, k in zip(planes, wedge.counts))
        low = padded_block(p[:k] for p, k in zip(planes, wedge.counts))
        out[at + f] = jnp.where(top, high, low)
    for c in range(comps):
        row, rims = disp(c), [edges(c, n) for n in range(1, d + 1)]
        high = padded_block([row[layers - d :]] + [rim[1] for rim in rims])
        low = padded_block([row[:d]] + [rim[0] for rim in rims])
        out[at + wedge.disp + c] = jnp.where(top, high, low)


def corner_kernel(slab_a, slab_b, work, survey, band_b, corner_a, corner_b, *, comps, layers):
    d = DEPTH
    slab, wedge = SectorSlab(comps, layers), Wedge(comps)
    band_even = lax.rem(lax.axis_index("band"), 2) == 0
    sector_even = lax.rem(lax.axis_index("sector"), 2) == 0
    for n, (side, above) in enumerate(((slab_a, sector_even), (slab_b, jnp.logical_not(sector_even)))):

        def plane(offset, side=side):
            return side[pl.ds(pl.multiple_of(offset, 8), layers)]

        def step(n, count, above=above):
            return jnp.where(above, n - 1, count - n)

        for out, top in ((corner_a, band_even), (corner_b, jnp.logical_not(band_even))):
            put_wedge(
                out,
                n * wedge.blocks,
                comps,
                layers,
                top,
                lambda c, n: plane(slab.residual_at(c, step(n, d))),
                lambda n: plane(slab.stiff + step(n, d) * layers),
                lambda n: plane(slab.mass + step(min(n, d - 1), d - 1) * layers),
                lambda c: plane(slab.disp + c * layers),
                lambda c, n: [side[pl.ds(at + c * d + step(n, d), 1)] for at in (slab.low, slab.high)],
            )
    r, u, _, mass, stiff = parts_of(work)
    put_band(corner_a, 2 * wedge.blocks, r, u, stiff, mass, band_even)


def dot(x, y):
    return jnp.sum((x * y).reshape(x.shape[0] // 8, 8, x.shape[1]), axis=0)


def total_of(x):
    return jnp.sum(jnp.sum(x, axis=0, keepdims=True), axis=1, keepdims=True)


def survey_kernel(work, row, image, basis_1, basis_2):
    r, _, cond, mass, _ = parts_of(work)
    comps, rows, layers, width = r.shape
    zero = jnp.zeros((8, width), F32)

    def apply(src):
        norm, product = zero, zero
        for a in range(rows):
            k_r, k_h, k_next = cond[0, a], cond[1, a], cond[2, a]
            for c in range(comps):
                v = src[c, a]
                flux_r = k_r * (ahead(v, 1) - v)
                flux_h = k_h * (ahead(v, 0) - v)
                total = flux_r - behind(flux_r, 1) + flux_h - behind(flux_h, 0)
                if a + 1 < rows:
                    total = total + k_next * (src[c, a + 1] - v)
                if a:
                    total = total - cond[2, a - 1] * (v - src[c, a - 1])
                out = mass[a] * v - COMPONENT_SCALE[c] * total
                image[c, a] = out
                norm, product = norm + dot(v, v), product + dot(v, out)
        return total_of(norm), total_of(product)

    level, back, weight_here, stats = r, None, None, []
    outs = (basis_1, basis_2)
    norm_back = None
    for step in range(ITERS - 1):
        norm, product = apply(level)
        if step:
            stats.append(norm / jnp.maximum(norm_back, TINY))
        else:
            weight_here = norm
        stats.append(product / jnp.maximum(norm, TINY))
        if step < ITERS - 2:
            a_k = jnp.broadcast_to(stats[-1], (layers, width))
            c_k = jnp.broadcast_to(stats[-2], (layers, width)) if step else None
            for a in range(rows):
                for c in range(comps):
                    x = image[c, a] - a_k * level[c, a]
                    outs[step][c, a] = x if back is None else x - c_k * back[c, a]
            back, level, norm_back = level, outs[step], norm
        else:
            a_k = jnp.broadcast_to(stats[-1], (layers, width))
            c_k = jnp.broadcast_to(stats[-2], (layers, width))
            last = zero
            for a in range(rows):
                for c in range(comps):
                    x = image[c, a] - a_k * level[c, a] - c_k * back[c, a]
                    last = last + dot(x, x)
            stats.append(total_of(last) / jnp.maximum(norm, TINY))
    col = lax.broadcasted_iota(jnp.int32, (8, 128), 1)
    tile = jnp.where(col == 0, weight_here, 0.0)
    for n, value in enumerate(stats):
        tile = jnp.where(col == 1 + n, weight_here * value, tile)
    tile = tile + cond[2, rows - 1, 0:8, 0:128]
    for n in range(row.shape[0] // 8):
        row[8 * n : 8 * n + 8] = tile


def coefficients(survey):
    total = jnp.sum(survey, axis=0, keepdims=True)
    col = lax.broadcasted_iota(jnp.int32, total.shape, 1)
    pick = lambda n: jnp.sum(jnp.where(col == n, total, 0.0), axis=1, keepdims=True)
    weight = jnp.maximum(pick(0), TINY)
    stats = [pick(n) / weight for n in range(1, STATS)]
    a, c = stats[0::2], stats[1::2]
    return a + [a[-1]], [None] + c


def bearing_law(moved, vertical, stick, slip, old, weight):
    trial = [K_STICK * (moved[i] - slip[i]) for i in range(2)]
    rate = [RATE_GAIN * (moved[i] - old[i]) for i in range(2)]
    slip_speed = jnp.sqrt(rate[0] * rate[0] + rate[1] * rate[1] + V_FLOOR * V_FLOOR)
    friction = MU_FAST - (MU_FAST - MU_SLOW) * jnp.exp(-RATE_DECAY * slip_speed)
    capacity = friction * weight
    magnitude = jnp.sqrt(trial[0] * trial[0] + trial[1] * trial[1])
    largest = jnp.maximum(magnitude, capacity)
    forces = [jnp.where(stick == 1.0, t, capacity * t / largest) for t in trial]
    return forces + [K_VERT * vertical]


def gram_pairs():
    return [(i, j) for i in range(ITERS) for j in range(i, ITERS + 1)]


def place_wedge(t, ux, kx, mx, block, at, wedge, comps, rows, above, near, upward):
    d = DEPTH
    for step in range(1, d + 1):
        row = jnp.where(above, d + rows - 1 + step, d - step)
        count, start = wedge.counts[step - 1], wedge.starts[step - 1]
        part = slice(start, start + count)
        where = slice(near, near + count) if upward else slice(near + 1 - count, near + 1)
        for c in range(comps):
            t[c, row, where] = block[at + c, part]
            ux[c, row, near : near + 1] = block[at + wedge.disp + c, d + step - 1 : d + step]
        kx[row, where] = block[at + wedge.stiff, part]
        mx[row, where] = block[at + wedge.mass, part]
    nearest = jnp.where(above, d + rows, d - 1)
    for c in range(comps):
        ux[c, nearest, slice(near, near + d) if upward else slice(near + 1 - d, near + 1)] = block[at + wedge.disp + c, 0:d]


def early_kernel(
    work, slab_a, slab_b, band_b, corner_a, survey,
    t0, t1, t2, t3, t4, kx, kh, late_t, late_u, late_m, raft, payload,
    raw, ux, mx, ks, kr, kh_back, kr_back, diag,
    *, bearings, sectors, bands,
):
    r, u, _, mass, stiff = parts_of(work)
    comps, rows, layers, width = r.shape
    d = DEPTH
    slab, wedge = SectorSlab(comps, layers), Wedge(comps)
    sector, band = lax.axis_index("sector"), lax.axis_index("band")
    sector_even = lax.rem(sector, 2) == 0
    band_even = lax.rem(band, 2) == 0
    all_rows, all_layers = rows + 2 * d, layers + 2 * d
    own = pl.ds(d, layers)

    for a in range(rows):
        for c in range(comps):
            raw[c, d + a, own] = r[c, a]
            ux[c, d + a, own] = u[c, a]
        kx[d + a, own] = stiff[a]
        mx[d + a, own] = mass[a]
    sides = ((slab_a, sector_even), (slab_b, jnp.logical_not(sector_even)))
    for side, above in sides:
        base = jnp.where(above, d + rows, 0)
        nearest = jnp.where(above, d + rows, d - 1)
        for i in range(d):
            for c in range(comps):
                raw[c, base + i, own] = side[pl.ds(slab.residual_at(c, i), layers)]
                ux[c, base + i, d : d + 1] = side[pl.ds(slab.low + c * d + i, 1)]
                ux[c, base + i, d + layers - 1 : d + layers] = side[pl.ds(slab.high + c * d + i, 1)]
            kx[base + i, own] = side[pl.ds(slab.stiff + i * layers, layers)]
        for i in range(d - 1):
            mx[jnp.where(above, d + rows, 1) + i, own] = side[pl.ds(slab.mass + i * layers, layers)]
        for c in range(comps):
            ux[c, nearest, own] = side[pl.ds(slab.disp + c * layers, layers)]

    def place_bands(even):
        for side, first_block, upward in ((corner_a, 2 * wedge.blocks, even), (band_b, 0, not even)):
            where = pl.ds(d + layers if upward else 0, d)
            for a in range(rows):
                part = slice((a % 2) * d, (a % 2) * d + d)
                block = lambda f: side[first_block + f * (rows // 2) + a // 2, part]
                for c in range(comps):
                    raw[c, d + a, where] = block(c)
                    ux[c, d + a, where] = block(comps + c)
                kx[d + a, where] = block(2 * comps)
                mx[d + a, where] = block(2 * comps + 1)
        near = d + layers if even else d - 1
        for m, (_, above) in enumerate(sides):
            place_wedge(raw, ux, kx, mx, corner_a, m * wedge.blocks, wedge, comps, rows, above, near, even)
        late = pl.ds(0 if even else all_layers - TILE, TILE)
        for a in range(all_rows):
            for c in range(comps):
                late_t[c, a] = raw[c, a, late]
                late_u[c, a] = ux[c, a, late]
            late_m[a] = mx[a, late]

    @pl.when(band_even)
    def _():
        place_bands(True)

    @pl.when(jnp.logical_not(band_even))
    def _():
        place_bands(False)

    lane = lax.broadcasted_iota(jnp.int32, (all_layers, width), 1)
    layer = lax.broadcasted_iota(jnp.int32, (all_layers, width), 0)

    raft[...] = jnp.zeros_like(raft)
    payload[...] = jnp.zeros_like(payload)

    @pl.when(band == 0)
    def _():
        around = (sector, lax.rem(sector + 1, sectors), lax.rem(sector + sectors - 1, sectors))
        rows_of = jnp.concatenate([survey[pl.ds(x * bands, bands)] for x in around], axis=0)
        known = jnp.concatenate(
            [pltpu.roll(rows_of, 128 - PARAM_AT - PARAMS * j, 1) for j in range(bearings)], axis=0
        )
        each = len(around) * bands
        count = bearings * each
        within = lax.rem(lax.broadcasted_iota(jnp.int32, (count, 1), 0), each)
        shift = jnp.where(within < bands, d, jnp.where(within < 2 * bands, d + rows, d - rows))
        column = lambda p: known[:, p : p + 1]
        row_of = column(PARAM_ROW).astype(jnp.int32) + shift
        row_of = jnp.broadcast_to(row_of, (count, width))
        lane_of = jnp.broadcast_to(column(PARAM_LANE).astype(jnp.int32), (count, width))
        here = lane_of == lax.broadcasted_iota(jnp.int32, (count, width), 1)
        at_node = [jnp.zeros((count, width), F32) for _ in range(comps)]
        for a in range(all_rows):
            hit = row_of == a
            for c in range(comps):
                at_node[c] = jnp.where(hit, ux[c, a, d : d + 1], at_node[c])
        stick = jnp.broadcast_to(column(PARAM_STICK), (count, width))
        force = bearing_law(
            at_node[:2], at_node[2], stick,
            [column(PARAM_SLIP), column(PARAM_SLIP + 1)], [column(PARAM_OLD), column(PARAM_OLD + 1)], column(PARAM_WEIGHT),
        )
        force = [jnp.where(here, f, 0.0) for f in force]
        stiffness = [jnp.where(here & (stick == 1.0), K_STICK, 0.0), jnp.where(here, K_VERT, 0.0)]
        for a in range(all_rows):
            hit = row_of == a
            for q, value in enumerate(force + stiffness):
                raft[q, a : a + 1] = jnp.sum(jnp.where(hit, value, 0.0), axis=0, keepdims=True)
        place_of = lax.broadcasted_iota(jnp.int32, payload.shape, 0) - sector * bands
        col = lax.broadcasted_iota(jnp.int32, payload.shape, 1)
        reply = jnp.zeros(payload.shape, F32)
        for c in range(comps):
            total = jnp.sum(force[c], axis=1, keepdims=True)
            for q in range(bands):
                for j in range(bearings):
                    value = total[j * each + q : j * each + q + 1]
                    reply = jnp.where((place_of == q) & (col == FORCE_AT + c * bearings + j), value, reply)
        payload[...] = reply

    interface = (layer == d - 1) | (layer == d + layers - 1)

    def faces(a, carry):
        k = kx[a]
        k_h = conductance(k, ahead(k, 0))
        k_r = jnp.where(lane < width - 1, conductance(k, ahead(k, 1)), 0.0)
        kh[a], kh_back[a], kr[a], kr_back[a] = k_h, behind(k_h, 0), k_r, behind(k_r, 1)
        ks[a] = conductance(k, kx[jnp.minimum(a + 1, all_rows - 1)])
        for c in range(comps):
            v = ux[c, a]
            flux = jnp.where(interface, k_h * (ahead(v, 0) - v), 0.0)
            change = COMPONENT_SCALE[c] * (flux - behind(flux, 0))
            change = change - jnp.where(layer == d, raft[c, pl.ds(a, 1)], 0.0)
            t0[c, a] = raw[c, a] + change
        return carry

    lax.fori_loop(0, all_rows, faces, 0, unroll=True)
    for a in (d - 1, d + rows - 1):
        for c in range(comps):
            flux = COMPONENT_SCALE[c] * (ks[a] * (ux[c, a + 1] - ux[c, a]))
            t0[c, a] = t0[c, a] + flux
            t0[c, a + 1] = t0[c, a + 1] - flux

    def diagonals(a, carry):
        around = kh[a] + kh_back[a] + kr[a] + kr_back[a] + ks[a] + ks[a - 1]
        diag[0, a] = mx[a] + COMPONENT_SCALE[0] * around + jnp.where(layer == d, raft[comps, pl.ds(a, 1)], 0.0)
        diag[1, a] = mx[a] + COMPONENT_SCALE[2] * around + jnp.where(layer == d, raft[comps + 1, pl.ds(a, 1)], 0.0)
        return carry

    lax.fori_loop(1, all_rows - 1, diagonals, 0, unroll=True)

    levels = (t0, t1, t2, t3, t4)
    shift_of, link_of = coefficients(survey[...])
    within = lax.broadcasted_iota(jnp.int32, (8, width), 0)
    for step in range(1, ITERS + 1):
        src, dst = levels[step - 1], levels[step]
        a_k = jnp.broadcast_to(shift_of[step - 1], (8, width))
        c_k = jnp.broadcast_to(link_of[step - 1], (8, width)) if step > 1 else None
        for a in range(step, all_rows - step):
            for start in range(0, all_layers, 8):
                part = slice(start, start + 8)
                k_h, k_low, k_r, k_left = kh[a, part], kh_back[a, part], kr[a, part], kr_back[a, part]
                k_next, k_back = ks[a, part], ks[a - 1, part]
                centres = [diag[n, a, part] - a_k for n in range(2)]
                for c in range(comps):
                    v = src[c, a, part]
                    upper, lower = ahead(v, 0), behind(v, 0)
                    if start + 8 < all_layers:
                        upper = jnp.where(within == 7, src[c, a, start + 8 : start + 9], upper)
                    if start:
                        lower = jnp.where(within == 0, src[c, a, start - 1 : start], lower)
                    around = k_next * src[c, a + 1, part] + k_back * src[c, a - 1, part]
                    around = around + (k_h * upper + k_low * lower)
                    around = around + (k_r * shifted(v, 1, 1) + k_left * shifted(v, 1, -1))
                    centre = centres[0 if c < 2 else 1] * v
                    if step > 1:
                        centre = centre - c_k * levels[step - 2][c, a, part]
                    dst[c, a, part] = centre - (around if COMPONENT_SCALE[c] == 1.0 else COMPONENT_SCALE[c] * around)


def late_kernel(
    t0, t1, t2, t3, t4, kx, kh, late_t, late_u, late_m, raft, payload_in, corner_b, survey,
    b0, b1, b2, b3, b4, payload,
    s0, s1, s2, s3, s4, raw, ux, k_tile, m_tile, ks, kh_tile, kh_back, kr, kr_back, diag,
):
    comps, rows, layers, width = b0.shape
    d = DEPTH
    wedge = Wedge(comps)
    all_rows, all_layers = rows + 2 * d, layers + 2 * d
    sector_even = lax.rem(lax.axis_index("sector"), 2) == 0
    band_even = lax.rem(lax.axis_index("band"), 2) == 0
    lane = lax.broadcasted_iota(jnp.int32, (TILE, width), 1)
    layer = lax.broadcasted_iota(jnp.int32, (TILE, width), 0)
    shift_of, link_of = coefficients(survey[...])
    wide = lambda x: None if x is None else jnp.broadcast_to(x, (TILE, width))
    shift_of, link_of = [wide(x) for x in shift_of], [wide(x) for x in link_of]
    early, late = (t0, t1, t2, t3, t4), (s0, s1, s2, s3, s4)
    outs, pairs = (b0, b1, b2, b3, b4), gram_pairs()

    def run(even):
        off = 0 if even else all_layers - TILE

        def upper(x, whole, *at):
            x = ahead(x, 0)
            return jnp.where(layer == TILE - 1, whole[(*at, slice(TILE, TILE + 1))], x) if even else x

        def lower(x, whole, *at):
            x = behind(x, 0)
            return x if even else jnp.where(layer == 0, whole[(*at, slice(off - 1, off))], x)

        for a in range(all_rows):
            for c in range(comps):
                raw[c, a] = late_t[c, a]
                ux[c, a] = late_u[c, a]
            k_tile[a] = kx[a, off : off + TILE]
            m_tile[a] = late_m[a]
        near = d - 1 if even else d + layers - off
        for m, above in enumerate((sector_even, jnp.logical_not(sector_even))):
            place_wedge(raw, ux, k_tile, m_tile, corner_b, m * wedge.blocks, wedge, comps, rows, above, near, not even)

        crossing = layer == (d - 1 if even else d + layers - 1 - off)
        on_raft = layer == d
        for a in range(all_rows):
            k = k_tile[a]
            k_h = conductance(k, upper(k, kx, a))
            kh_tile[a], kh_back[a] = k_h, lower(k_h, kh, a)
            k_r = jnp.where(lane < width - 1, conductance(k, ahead(k, 1)), 0.0)
            kr[a], kr_back[a] = k_r, behind(k_r, 1)
            if a + 1 < all_rows:
                ks[a] = conductance(k, k_tile[a + 1])
            for c in range(comps):
                v = ux[c, a]
                flux = jnp.where(crossing, k_h * (ahead(v, 0) - v), 0.0)
                change = COMPONENT_SCALE[c] * (flux - behind(flux, 0))
                if even:
                    change = change - jnp.where(on_raft, raft[c, a : a + 1], 0.0)
                s0[c, a] = raw[c, a] + change
        for a in (d - 1, d + rows - 1):
            for c in range(comps):
                flux = COMPONENT_SCALE[c] * (ks[a] * (ux[c, a + 1] - ux[c, a]))
                s0[c, a] = s0[c, a] + flux
                s0[c, a + 1] = s0[c, a + 1] - flux
        for a in range(1, all_rows - 1):
            around = kh_tile[a] + kh_back[a] + kr[a] + kr_back[a] + ks[a] + ks[a - 1]
            for n, scale in enumerate((COMPONENT_SCALE[0], COMPONENT_SCALE[2])):
                total = m_tile[a] + scale * around
                diag[n, a] = total + jnp.where(on_raft, raft[comps + n, a : a + 1], 0.0) if even else total
        for step in range(1, ITERS + 1):
            src, dst = late[step - 1], late[step]
            for a in range(step, all_rows - step):
                centres = [diag[n, a] - shift_of[step - 1] for n in range(2)]
                for c in range(comps):
                    v = src[c, a]
                    around = ks[a] * src[c, a + 1] + ks[a - 1] * src[c, a - 1]
                    around = around + (
                        kh_tile[a] * upper(v, early[step - 1], c, a) + kh_back[a] * lower(v, early[step - 1], c, a)
                    )
                    around = around + (kr[a] * shifted(v, 1, 1) + kr_back[a] * shifted(v, 1, -1))
                    centre = centres[0 if c < 2 else 1] * v
                    if step > 1:
                        centre = centre - link_of[step - 1] * late[step - 2][c, a]
                    dst[c, a] = centre - (around if COMPONENT_SCALE[c] == 1.0 else COMPONENT_SCALE[c] * around)

        sums = [jnp.zeros((8, width), F32) for _ in pairs]
        for a in range(rows):
            for c in range(comps):
                if even:
                    block = [jnp.concatenate([x[c, d + a, d:], t[c, d + a, TILE : d + layers]], axis=0) for t, x in zip(early, late)]
                else:
                    block = [jnp.concatenate([t[c, d + a, d:off], x[c, d + a, : d + layers - off]], axis=0) for t, x in zip(early, late)]
                for out, x in zip(outs, block):
                    out[c, a] = x
                sums = [s + dot(block[i], block[j]) for s, (i, j) in zip(sums, pairs)]
        col = lax.broadcasted_iota(jnp.int32, payload.shape, 1)
        reply = payload_in[...]
        for p, s in enumerate(sums):
            reply = jnp.where(col == p, total_of(s), reply)
        payload[...] = reply

    @pl.when(band_even)
    def _():
        run(True)

    @pl.when(jnp.logical_not(band_even))
    def _():
        run(False)


def combine_kernel(received, survey, b0, b1, b2, b3, b4, increment, residual, force, *, bearings, bands):
    comps, rows, layers, width = b0.shape
    sector = lax.axis_index("sector")
    total = jnp.sum(received[...], axis=0, keepdims=True)
    col = lax.broadcasted_iota(jnp.int32, total.shape, 1)
    table = {ij: jnp.sum(jnp.where(col == p, total, 0.0), axis=1, keepdims=True) for p, ij in enumerate(gram_pairs())}
    shift_of, link_of = coefficients(survey[...])
    g = lambda i, j: table[min(i, j), max(i, j)]
    zero, one = jnp.zeros_like(table[0, 0]), jnp.ones_like(table[0, 0])
    res = [one] + [zero] * ITERS
    direction, inc = list(res), [zero] * (ITERS + 1)
    norm = table[0, 0]
    for it in range(ITERS):
        image = [zero] * (ITERS + 1)
        for i in range(it + 1):
            image[i] = image[i] + shift_of[i] * direction[i]
            image[i + 1] = image[i + 1] + direction[i]
            if i:
                image[i - 1] = image[i - 1] + link_of[i] * direction[i]
        product = sum(
            direction[i] * sum(image[j] * g(i, j) for j in range(it + 2)) for i in range(it + 1)
        )
        alpha = norm / product
        inc = [x + alpha * y for x, y in zip(inc, direction)]
        res = [x - alpha * y for x, y in zip(res, image)]
        if it + 1 < ITERS:
            norm_next = sum(res[i] * sum(res[j] * g(i, j) for j in range(it + 2)) for i in range(it + 2))
            ratio = norm_next / norm
            direction = [x + ratio * y for x, y in zip(res, direction)]
            norm = norm_next
    basis = (b0, b1, b2, b3, b4)
    inc = [jnp.broadcast_to(x, (layers, width)) for x in inc[:ITERS]]
    res = [jnp.broadcast_to(x, (layers, width)) for x in res]

    def combine(a, carry):
        for c in range(comps):
            x = [b[c, a] for b in basis]
            increment[c, a] = sum(y * z for y, z in zip(inc, x))
            residual[c, a] = sum(y * z for y, z in zip(res, x))
        return carry

    lax.fori_loop(0, rows, combine, 0)
    mine = received[pl.ds(sector * bands, 1)]
    for c in range(comps):
        force[c : c + 1] = mine[:, FORCE_AT + c * bearings : FORCE_AT + (c + 1) * bearings]


def kernel_call(body, outs, operands, far=(), scratch=()):
    vmem = pl.BlockSpec(memory_space=pltpu.VMEM)
    operands = [pltpu.with_memory_space_constraint(x, pltpu.HBM) if i in far else x for i, x in enumerate(operands)]
    return pl.pallas_call(
        body,
        out_shape=[jax.ShapeDtypeStruct(s, F32) for s in outs],
        in_specs=[pl.BlockSpec(memory_space=pltpu.HBM) if i in far else vmem for i in range(len(operands))],
        out_specs=[vmem] * len(outs),
        scratch_shapes=[pltpu.VMEM(s, F32) if isinstance(s, tuple) else s for s in scratch],
        compiler_params=pltpu.CompilerParams(vmem_limit_bytes=VMEM_LIMIT),
    )(*operands)


def pair_up(i, n):
    return i ^ 1


def pair_down(i, n):
    return (((i + 1) % n) ^ 1) - 1 if ((i + 1) % n) ^ 1 else n - 1


def per_device(
    given_load, displacement, mass_coef, stiffness, bearing_node, stick_state, slip_prev, bearing_old, bearing_weight
):
    comps, rows, layers, radial = displacement.shape
    bearings = bearing_node.shape[0]
    sectors, bands = lax.axis_size("sector"), lax.axis_size("band")
    d = DEPTH
    slab, wedge = SectorSlab(comps, layers), Wedge(comps)

    def exchange(x, sector_partner=None, band_partner=None):
        pairs = []
        for s in range(sectors):
            for b in range(bands):
                t = s if sector_partner is None else sector_partner(s, sectors)
                q = b if band_partner is None else band_partner(b)
                if 0 <= q < bands:
                    pairs.append((s * bands + b, t * bands + q))
        return lax.ppermute(x, AXES, pairs)

    inner = lambda b: -1 if b in (0, bands - 1) else ((b + 1) ^ 1) - 1

    field, block = displacement.shape, mass_coef.shape
    slab_shape, band_shape = (slab.rows, radial), ((2 * comps + 2) * (rows // 2), 2 * d, radial)
    small = [
        pltpu.SMEM((bearings,), jnp.int32),
        pltpu.SMEM((bearings,), jnp.int32),
        pltpu.SMEM((2, bearings), F32),
        pltpu.SMEM((2, bearings), F32),
        pltpu.SMEM((bearings,), F32),
    ]
    work, slab_a, slab_b, band_b = kernel_call(
        functools.partial(local_kernel, radial=radial),
        [(2 * comps + 5, *block), slab_shape, slab_shape, band_shape],
        (displacement, given_load, mass_coef, stiffness, bearing_node, stick_state, slip_prev, bearing_old, bearing_weight),
        far=range(9),
        scratch=[field, *small, pltpu.SemaphoreType.DMA((12,))],
    )
    outer = lambda b: b ^ 1
    slab_b = exchange(slab_b, pair_down)
    slab_a = exchange(slab_a, pair_up)
    band_b = exchange(band_b, None, inner)
    (survey,) = kernel_call(survey_kernel, [(sectors * bands, 128)], (work,), scratch=[field] * 3)
    survey = lax.all_to_all(survey, AXES, 0, 0, tiled=True)
    corner_a, corner_b = kernel_call(
        functools.partial(corner_kernel, comps=comps, layers=layers),
        [(2 * wedge.blocks + band_shape[0], 2 * d, radial), (2 * wedge.blocks, 2 * d, radial)],
        (slab_a, slab_b, work, survey, band_b),
    )
    corner_b = exchange(corner_b, None, inner)
    corner_a = exchange(corner_a, None, outer)
    devices = sectors * bands
    extended = (rows + 2 * d, layers + 2 * d, radial)
    all_rows = extended[0]
    tile_field, tile_block = (comps, all_rows, TILE, radial), (all_rows, TILE, radial)
    *early, payload = kernel_call(
        functools.partial(early_kernel, bearings=bearings, sectors=sectors, bands=bands),
        [(comps, *extended)] * (ITERS + 1)
        + [extended] * 2
        + [tile_field, tile_field, tile_block, (comps + 2, all_rows, radial), (devices, 128)],
        (work, slab_a, slab_b, band_b, corner_a, survey),
        scratch=[(comps, *extended)] * 2 + [extended] * 5 + [(2, *extended)],
    )
    *basis, payload = kernel_call(
        late_kernel,
        [field] * (ITERS + 1) + [(devices, 128)],
        (*early, payload, corner_b, survey),
        scratch=[tile_field] * (ITERS + 3) + [tile_block] * 7 + [(2, *tile_block)],
    )
    received = lax.all_to_all(payload, AXES, 0, 0, tiled=True)
    increment, residual, force = kernel_call(
        functools.partial(combine_kernel, bearings=bearings, bands=bands),
        [field, field, (comps, bearings)],
        (received, survey, *basis),
    )
    return (increment, residual, force)


def solution(mesh):
    return jax.shard_map(
        per_device,
        mesh=mesh,
        in_specs=(
            P(None, "sector", "band", None),
            P(None, "sector", "band", None),
            P("sector", "band", None),
            P("sector", "band", None),
            P(("sector", "band")),
            P(("sector", "band")),
            P(None, ("sector", "band")),
            P(None, ("sector", "band")),
            P(("sector", "band")),
        ),
        out_specs=(
            P(None, "sector", "band", None),
            P(None, "sector", "band", None),
            P(None, ("sector", "band")),
        ),
        check_vma=False,
    )
```

```python
import functools

import jax
import jax.numpy as jnp
from jax import lax
from jax.experimental import pallas as pl
from jax.experimental.pallas import tpu as pltpu
from jax.sharding import PartitionSpec as P

ITERS = 4
DEPTH = ITERS

K_STICK = 4.0
K_VERT = 8.0
MU_FAST = 0.15
MU_SLOW = 0.04
RATE_GAIN = 2.0
RATE_DECAY = 2.0
V_FLOOR = 0.05
COMPONENT_SCALE = (1.0, 1.0, 2.0)

STATS = 1 + 2 * (ITERS - 1)
TINY = 1e-30
FLOOR = 0.25

AXES = ("sector", "band")
F32 = jnp.float32
PARAM_ROW, PARAM_LANE, PARAM_STICK, PARAM_SLIP, PARAM_OLD, PARAM_WEIGHT = (0, 1, 2, 3, 5, 7)
PARAMS = 8
PARAM_AT = 32
FORCE_AT = 64
VMEM_LIMIT = 24 * 1024 * 1024
TILE = 8


def conductance(left, right):
    return 2.0 * left * right / jnp.maximum(left + right, FLOOR)


def ahead(x, axis):
    return pltpu.roll(x, x.shape[axis] - 1, axis)


def behind(x, axis):
    return pltpu.roll(x, 1, axis)


def shifted(x, axis, by):
    size = 8 if axis == 0 else 128
    count = x.shape[axis] // size
    parts = [lax.slice_in_dim(x, i * size, (i + 1) * size, axis=axis) for i in range(count)]
    turned = [pltpu.roll(p, size - 1 if by == 1 else 1, axis) for p in parts]
    edge = lax.broadcasted_iota(jnp.int32, parts[0].shape, axis) == (size - 1 if by == 1 else 0)
    out = [jnp.where(edge, turned[i + by], turned[i]) if 0 <= i + by < count else turned[i] for i in range(count)]
    return out[0] if count == 1 else jnp.concatenate(out, axis=axis)


def round_up(n, multiple):
    return -(-n // multiple) * multiple


def put_band(out, at, r, u, stiff, mass, top):
    comps, rows, layers, _ = r.shape
    fields = [r.at[c] for c in range(comps)] + [u.at[c] for c in range(comps)] + [stiff, mass]
    for f, field in enumerate(fields):
        for pair in range(rows // 2):
            planes = [field[2 * pair + i] for i in range(2)]
            high = jnp.concatenate([x[layers - DEPTH :] for x in planes], axis=0)
            low = jnp.concatenate([x[:DEPTH] for x in planes], axis=0)
            out[at + f * (rows // 2) + pair] = jnp.where(top, high, low)


class SectorSlab:
    def __init__(self, comps, layers):
        d = DEPTH
        self.comps, self.layers = comps, layers
        self.stiff = comps * (d - 1) * layers
        self.mass = self.stiff + (d - 1) * layers
        self.disp = self.mass + (d - 2) * layers
        self.image = self.disp + comps * layers
        self.low = self.image + comps * layers
        self.rims = comps * (d - 1) + comps + 2
        self.high = self.low + self.rims
        self.rows = round_up(self.high + self.rims, 8)

    def residual_at(self, c, i):
        return (c * (DEPTH - 1) + i) * self.layers

    def rim_disp(self, c, n):
        return c * (DEPTH - 1) + n - 2

    def rim_residual(self, c):
        return self.comps * (DEPTH - 1) + c

    def rim_stiff(self):
        return self.rims - 2

    def rim_mass(self):
        return self.rims - 1


def parts_of(work):
    comps = (work.shape[0] - 5) // 2
    return work.at[0:comps], work.at[comps : 2 * comps], work.at[2 * comps : 2 * comps + 3], work.at[2 * comps + 3], work.at[2 * comps + 4]


def local_kernel(
    u_far, load_far, mass_far, stiff_far, node_far, stick_far, slip_far, old_far, weight_far,
    work, slab_a, slab_b, band_b,
    load, node, stick, slip, old, weight, arrived, *, radial,
):
    comps, rows, layers, width = load.shape
    d = DEPTH
    r, u, cond, mass, stiff = parts_of(work)
    half = rows // 2
    fields = [(stiff_far, stiff)]
    for part in (pl.ds(0, half), pl.ds(half, rows - half)):
        fields += [
            (u_far.at[:, part], u.at[:, part]),
            (mass_far.at[part], mass.at[part]),
            (load_far.at[:, part], load.at[:, part]),
        ]
    small = ((node_far, node), (stick_far, stick), (slip_far, slip), (old_far, old), (weight_far, weight))
    moves = [pltpu.make_async_copy(src, dst, arrived.at[n]) for n, (src, dst) in enumerate([*fields, *small])]
    for move in moves:
        move.start()
    lane = lax.broadcasted_iota(jnp.int32, (layers, width), 1)
    layer = lax.broadcasted_iota(jnp.int32, (layers, width), 0)
    moves[0].wait()
    for a in range(rows):
        k = stiff[a]
        cond[0, a] = jnp.where(lane < width - 1, conductance(k, ahead(k, 1)), 0.0)
        cond[1, a] = jnp.where(layer < layers - 1, conductance(k, ahead(k, 0)), 0.0)
        cond[2, a] = conductance(k, stiff[a + 1]) if a + 1 < rows else jnp.zeros((layers, width), F32)
    before = [None] * comps
    for a in range(rows):
        if a == 0:
            for move in moves[1:4]:
                move.wait()
        if a == half - 1:
            for move in moves[4:7]:
                move.wait()
        k_r, k_h, k_s = cond[0, a], cond[1, a], cond[2, a]
        m = mass[a]
        for c in range(comps):
            v = u[c, a]
            flux_r = k_r * (ahead(v, 1) - v)
            flux_h = k_h * (ahead(v, 0) - v)
            total = flux_r - behind(flux_r, 1) + flux_h - behind(flux_h, 0)
            if before[c] is not None:
                total = total - before[c]
            if a + 1 < rows:
                before[c] = k_s * (u[c, a + 1] - v)
                total = total + before[c]
            r[c, a] = load[c, a] - m * v + COMPONENT_SCALE[c] * total

    for move in moves[len(fields) :]:
        move.wait()
    col = lax.broadcasted_iota(jnp.int32, (8, 128), 1)
    tile = jnp.zeros((8, 128), F32)
    for j in range(node.shape[0]):
        at = node[j] // radial
        values = {
            PARAM_ROW: at.astype(F32),
            PARAM_LANE: (node[j] - at * radial).astype(F32),
            PARAM_STICK: stick[j].astype(F32),
            PARAM_SLIP: slip[0, j],
            PARAM_SLIP + 1: slip[1, j],
            PARAM_OLD: old[0, j],
            PARAM_OLD + 1: old[1, j],
            PARAM_WEIGHT: weight[j],
        }
        for p, value in values.items():
            tile = jnp.where(col == PARAM_AT + PARAMS * j + p, value, tile)
    cond[2, rows - 1, 0:8, 0:128] = tile

    slab = SectorSlab(comps, layers)
    even = lax.rem(lax.axis_index("sector"), 2) == 0
    for out, upper in ((slab_a, even), (slab_b, jnp.logical_not(even))):

        def row(n, upper=upper):
            return jnp.where(upper, rows - n, n - 1)

        for i in range(d - 1):
            first = jnp.where(upper, rows - (d - 1), 0)
            for c in range(comps):
                out[pl.ds(slab.residual_at(c, i), layers)] = r[c, first + i]
            out[pl.ds(slab.stiff + i * layers, layers)] = stiff[first + i]
        for i in range(d - 2):
            out[pl.ds(slab.mass + i * layers, layers)] = mass[jnp.where(upper, rows - (d - 2), 0) + i]
        at = row(d - 1)
        k_r, k_h, k_next, k_back = cond[0, at], cond[1, at], cond[2, at], cond[2, at - 1]
        for c in range(comps):
            out[pl.ds(slab.disp + c * layers, layers)] = u[c, row(1)]
            v = r[c, at]
            flux_r = k_r * (ahead(v, 1) - v)
            flux_h = k_h * (ahead(v, 0) - v)
            total = flux_r - behind(flux_r, 1) + flux_h - behind(flux_h, 0)
            total = total + k_next * (r[c, at + 1] - v) - k_back * (v - r[c, at - 1])
            out[pl.ds(slab.image + c * layers, layers)] = mass[at] * v - COMPONENT_SCALE[c] * total
        for group, layer_of in ((slab.low, slice(0, 1)), (slab.high, slice(layers - 1, layers))):
            for c in range(comps):
                for n in range(2, d + 1):
                    out[pl.ds(group + slab.rim_disp(c, n), 1)] = u[c, row(n), layer_of]
                out[pl.ds(group + slab.rim_residual(c), 1)] = r[c, row(d), layer_of]
            out[pl.ds(group + slab.rim_stiff(), 1)] = stiff[row(d), layer_of]
            out[pl.ds(group + slab.rim_mass(), 1)] = mass[row(d - 1), layer_of]
        end = slab.high + slab.rims
        if slab.rows > end:
            out[pl.ds(end, slab.rows - end)] = jnp.zeros((slab.rows - end, width), F32)

    even = lax.rem(lax.axis_index("band"), 2) == 0
    put_band(band_b, 0, r, u, stiff, mass, jnp.logical_not(even))


REACH = [DEPTH] + [max(DEPTH - n, 1) for n in range(2, DEPTH + 1)]


class Wedge:
    counts = REACH
    starts = [sum(REACH[:n]) for n in range(DEPTH)]
    height = round_up(sum(REACH), 8)

    def __init__(self, comps):
        self.stiff, self.mass, self.disp = comps, comps + 1, comps + 2
        self.blocks = 2 * comps + 2


def padded_block(parts):
    parts = list(parts)
    spare = Wedge.height - sum(p.shape[0] for p in parts)
    if spare:
        parts.append(jnp.zeros((spare, parts[0].shape[1]), F32))
    return jnp.concatenate(parts, axis=0)


def put_wedge(out, at, comps, layers, top, residual, stiff, mass, disp, edges):
    wedge, d = Wedge(comps), DEPTH
    sources = [functools.partial(residual, c) for c in range(comps)] + [stiff, mass]
    for f, source in enumerate(sources):
        planes = [source(n) for n in range(1, d + 1)]
        high = padded_block(p[layers - k :] for p, k in zip(planes, wedge.counts))
        low = padded_block(p[:k] for p, k in zip(planes, wedge.counts))
        out[at + f] = jnp.where(top, high, low)
    for c in range(comps):
        row, rims = disp(c), [edges(c, n) for n in range(1, d + 1)]
        high = padded_block([row[layers - d :]] + [rim[1] for rim in rims])
        low = padded_block([row[:d]] + [rim[0] for rim in rims])
        out[at + wedge.disp + c] = jnp.where(top, high, low)


def corner_kernel(slab_a, slab_b, work, survey, band_b, corner_a, corner_b, *, comps, layers):
    d = DEPTH
    slab, wedge = SectorSlab(comps, layers), Wedge(comps)
    band_even = lax.rem(lax.axis_index("band"), 2) == 0
    sector_even = lax.rem(lax.axis_index("sector"), 2) == 0
    for n, (side, above) in enumerate(((slab_a, sector_even), (slab_b, jnp.logical_not(sector_even)))):

        def plane(offset, side=side):
            return side[pl.ds(pl.multiple_of(offset, 8), layers)]

        def step(n, count, above=above):
            return jnp.where(above, n - 1, count - n)

        def rim(at, side=side):
            return [side[pl.ds(group + at, 1)] for group in (slab.low, slab.high)]

        def stiff_of(n):
            if n < d:
                return plane(slab.stiff + step(n, d - 1) * layers)
            return jnp.concatenate([jnp.broadcast_to(x, (layers // 2, x.shape[1])) for x in rim(slab.rim_stiff())], axis=0)

        def disp_rim(c, n):
            if n > 1:
                return rim(slab.rim_disp(c, n))
            row = plane(slab.disp + c * layers)
            return [row[0:1], row[layers - 1 :]]

        for out, top in ((corner_a, band_even), (corner_b, jnp.logical_not(band_even))):
            put_wedge(
                out,
                n * wedge.blocks,
                comps,
                layers,
                top,
                lambda c, n: plane(slab.residual_at(c, step(min(n, d - 1), d - 1))),
                stiff_of,
                lambda n: plane(slab.mass + step(min(n, d - 2), d - 2) * layers),
                lambda c: plane(slab.disp + c * layers),
                disp_rim,
            )
    r, u, _, mass, stiff = parts_of(work)
    put_band(corner_a, 2 * wedge.blocks, r, u, stiff, mass, band_even)


def dot(x, y):
    return jnp.sum((x * y).reshape(x.shape[0] // 8, 8, x.shape[1]), axis=0)


def total_of(x):
    return jnp.sum(jnp.sum(x, axis=0, keepdims=True), axis=1, keepdims=True)


def survey_kernel(work, row, image, basis_1, basis_2):
    r, _, cond, mass, _ = parts_of(work)
    comps, rows, layers, width = r.shape
    zero = jnp.zeros((8, width), F32)

    def apply(src):
        norm, product = zero, zero
        for a in range(rows):
            k_r, k_h, k_next = cond[0, a], cond[1, a], cond[2, a]
            for c in range(comps):
                v = src[c, a]
                flux_r = k_r * (ahead(v, 1) - v)
                flux_h = k_h * (ahead(v, 0) - v)
                total = flux_r - behind(flux_r, 1) + flux_h - behind(flux_h, 0)
                if a + 1 < rows:
                    total = total + k_next * (src[c, a + 1] - v)
                if a:
                    total = total - cond[2, a - 1] * (v - src[c, a - 1])
                out = mass[a] * v - COMPONENT_SCALE[c] * total
                image[c, a] = out
                norm, product = norm + dot(v, v), product + dot(v, out)
        return total_of(norm), total_of(product)

    level, back, weight_here, stats = r, None, None, []
    outs = (basis_1, basis_2)
    norm_back = None
    for step in range(ITERS - 1):
        norm, product = apply(level)
        if step:
            stats.append(norm / jnp.maximum(norm_back, TINY))
        else:
            weight_here = norm
        stats.append(product / jnp.maximum(norm, TINY))
        if step < ITERS - 2:
            a_k = jnp.broadcast_to(stats[-1], (layers, width))
            c_k = jnp.broadcast_to(stats[-2], (layers, width)) if step else None
            for a in range(rows):
                for c in range(comps):
                    x = image[c, a] - a_k * level[c, a]
                    outs[step][c, a] = x if back is None else x - c_k * back[c, a]
            back, level, norm_back = level, outs[step], norm
        else:
            a_k = jnp.broadcast_to(stats[-1], (layers, width))
            c_k = jnp.broadcast_to(stats[-2], (layers, width))
            last = zero
            for a in range(rows):
                for c in range(comps):
                    x = image[c, a] - a_k * level[c, a] - c_k * back[c, a]
                    last = last + dot(x, x)
            stats.append(total_of(last) / jnp.maximum(norm, TINY))
    col = lax.broadcasted_iota(jnp.int32, (8, 128), 1)
    tile = jnp.where(col == 0, weight_here, 0.0)
    for n, value in enumerate(stats):
        tile = jnp.where(col == 1 + n, weight_here * value, tile)
    tile = tile + cond[2, rows - 1, 0:8, 0:128]
    for n in range(row.shape[0] // 8):
        row[8 * n : 8 * n + 8] = tile


def coefficients(survey):
    total = jnp.sum(survey, axis=0, keepdims=True)
    col = lax.broadcasted_iota(jnp.int32, total.shape, 1)
    pick = lambda n: jnp.sum(jnp.where(col == n, total, 0.0), axis=1, keepdims=True)
    weight = jnp.maximum(pick(0), TINY)
    stats = [pick(n) / weight for n in range(1, STATS)]
    a, c = stats[0::2], stats[1::2]
    return a + [a[-1]], [None] + c


def bearing_law(moved, vertical, stick, slip, old, weight):
    trial = [K_STICK * (moved[i] - slip[i]) for i in range(2)]
    rate = [RATE_GAIN * (moved[i] - old[i]) for i in range(2)]
    slip_speed = jnp.sqrt(rate[0] * rate[0] + rate[1] * rate[1] + V_FLOOR * V_FLOOR)
    friction = MU_FAST - (MU_FAST - MU_SLOW) * jnp.exp(-RATE_DECAY * slip_speed)
    capacity = friction * weight
    magnitude = jnp.sqrt(trial[0] * trial[0] + trial[1] * trial[1])
    largest = jnp.maximum(magnitude, capacity)
    forces = [jnp.where(stick == 1.0, t, capacity * t / largest) for t in trial]
    return forces + [K_VERT * vertical]


def gram_pairs():
    return [(i, j) for i in range(ITERS) for j in range(i, ITERS + 1)]


def place_wedge(t, ux, kx, mx, block, at, wedge, comps, rows, above, near, upward):
    d = DEPTH
    for step in range(1, d + 1):
        row = jnp.where(above, d + rows - 1 + step, d - step)
        count, start = wedge.counts[step - 1], wedge.starts[step - 1]
        part = slice(start, start + count)
        where = slice(near, near + count) if upward else slice(near + 1 - count, near + 1)
        for c in range(comps):
            t[c, row, where] = block[at + c, part]
            ux[c, row, near : near + 1] = block[at + wedge.disp + c, d + step - 1 : d + step]
        kx[row, where] = block[at + wedge.stiff, part]
        mx[row, where] = block[at + wedge.mass, part]
    nearest = jnp.where(above, d + rows, d - 1)
    for c in range(comps):
        ux[c, nearest, slice(near, near + d) if upward else slice(near + 1 - d, near + 1)] = block[at + wedge.disp + c, 0:d]


def early_kernel(
    work, slab_a, slab_b, band_b, corner_a, survey,
    t0, t1, t2, t3, t4, kx, kh, late_t, late_u, late_m, late_image, raft, payload,
    raw, ux, mx, ks, kr, kh_back, kr_back, diag, image, turn,
    *, bearings, sectors, bands,
):
    r, u, _, mass, stiff = parts_of(work)
    comps, rows, layers, width = r.shape
    d = DEPTH
    slab, wedge = SectorSlab(comps, layers), Wedge(comps)
    sector, band = lax.axis_index("sector"), lax.axis_index("band")
    sector_even = lax.rem(sector, 2) == 0
    band_even = lax.rem(band, 2) == 0
    all_rows, all_layers = rows + 2 * d, layers + 2 * d
    own = pl.ds(d, layers)

    for a in range(rows):
        for c in range(comps):
            raw[c, d + a, own] = r[c, a]
            ux[c, d + a, own] = u[c, a]
        kx[d + a, own] = stiff[a]
        mx[d + a, own] = mass[a]
    sides = ((slab_a, sector_even), (slab_b, jnp.logical_not(sector_even)))
    empty = jnp.zeros((all_layers, width), F32)
    for side, above in sides:

        def row(n, above=above):
            return jnp.where(above, d + rows - 1 + n, d - n)

        for c in range(comps):
            raw[c, row(d)] = empty
        kx[row(d)], mx[row(d - 1)] = empty, empty
        for i in range(d - 1):
            first = jnp.where(above, d + rows, 1)
            for c in range(comps):
                raw[c, first + i, own] = side[pl.ds(slab.residual_at(c, i), layers)]
            kx[first + i, own] = side[pl.ds(slab.stiff + i * layers, layers)]
        for i in range(d - 2):
            mx[jnp.where(above, d + rows, 2) + i, own] = side[pl.ds(slab.mass + i * layers, layers)]
        for c in range(comps):
            ux[c, row(1), own] = side[pl.ds(slab.disp + c * layers, layers)]
            image[c, jnp.where(above, 1, 0), own] = side[pl.ds(slab.image + c * layers, layers)]
        for group, at in ((slab.low, slice(d, d + 1)), (slab.high, slice(d + layers - 1, d + layers))):
            rim = lambda place, group=group: side[pl.ds(group + place, 1)]
            for c in range(comps):
                for n in range(2, d + 1):
                    ux[c, row(n), at] = rim(slab.rim_disp(c, n))
                raw[c, row(d), at] = rim(slab.rim_residual(c))
            kx[row(d), at] = rim(slab.rim_stiff())
            mx[row(d - 1), at] = rim(slab.rim_mass())

    def place_bands(even):
        for side, first_block, upward in ((corner_a, 2 * wedge.blocks, even), (band_b, 0, not even)):
            where = pl.ds(d + layers if upward else 0, d)
            for a in range(rows):
                part = slice((a % 2) * d, (a % 2) * d + d)
                block = lambda f: side[first_block + f * (rows // 2) + a // 2, part]
                for c in range(comps):
                    raw[c, d + a, where] = block(c)
                    ux[c, d + a, where] = block(comps + c)
                kx[d + a, where] = block(2 * comps)
                mx[d + a, where] = block(2 * comps + 1)
        near = d + layers if even else d - 1
        for m, (_, above) in enumerate(sides):
            place_wedge(raw, ux, kx, mx, corner_a, m * wedge.blocks, wedge, comps, rows, above, near, even)
        late = pl.ds(0 if even else all_layers - TILE, TILE)
        for a in range(all_rows):
            for c in range(comps):
                late_t[c, a] = raw[c, a, late]
                late_u[c, a] = ux[c, a, late]
            late_m[a] = mx[a, late]
        for c in range(comps):
            for n in range(2):
                late_image[c, n] = image[c, n, late]

    @pl.when(band_even)
    def _():
        place_bands(True)

    @pl.when(jnp.logical_not(band_even))
    def _():
        place_bands(False)

    lane = lax.broadcasted_iota(jnp.int32, (all_layers, width), 1)
    layer = lax.broadcasted_iota(jnp.int32, (all_layers, width), 0)

    raft[...] = jnp.zeros_like(raft)
    payload[...] = jnp.zeros_like(payload)

    @pl.when(band == 0)
    def _():
        around = (sector, lax.rem(sector + 1, sectors), lax.rem(sector + sectors - 1, sectors))
        rows_of = jnp.concatenate([survey[pl.ds(x * bands, bands)] for x in around], axis=0)
        known = jnp.concatenate(
            [pltpu.roll(rows_of, 128 - PARAM_AT - PARAMS * j, 1) for j in range(bearings)], axis=0
        )
        each = len(around) * bands
        count = bearings * each
        within = lax.rem(lax.broadcasted_iota(jnp.int32, (count, 1), 0), each)
        shift = jnp.where(within < bands, d, jnp.where(within < 2 * bands, d + rows, d - rows))
        column = lambda p: known[:, p : p + 1]
        row_of = column(PARAM_ROW).astype(jnp.int32) + shift
        row_of = jnp.broadcast_to(row_of, (count, width))
        lane_of = jnp.broadcast_to(column(PARAM_LANE).astype(jnp.int32), (count, width))
        here = lane_of == lax.broadcasted_iota(jnp.int32, (count, width), 1)
        at_node = [jnp.zeros((count, width), F32) for _ in range(comps)]
        for a in range(all_rows):
            hit = row_of == a
            for c in range(comps):
                at_node[c] = jnp.where(hit, ux[c, a, d : d + 1], at_node[c])
        stick = jnp.broadcast_to(column(PARAM_STICK), (count, width))
        force = bearing_law(
            at_node[:2], at_node[2], stick,
            [column(PARAM_SLIP), column(PARAM_SLIP + 1)], [column(PARAM_OLD), column(PARAM_OLD + 1)], column(PARAM_WEIGHT),
        )
        force = [jnp.where(here, f, 0.0) for f in force]
        stiffness = [jnp.where(here & (stick == 1.0), K_STICK, 0.0), jnp.where(here, K_VERT, 0.0)]
        for a in range(all_rows):
            hit = row_of == a
            for q, value in enumerate(force + stiffness):
                raft[q, a : a + 1] = jnp.sum(jnp.where(hit, value, 0.0), axis=0, keepdims=True)
        place_of = lax.broadcasted_iota(jnp.int32, payload.shape, 0) - sector * bands
        col = lax.broadcasted_iota(jnp.int32, payload.shape, 1)
        reply = jnp.zeros(payload.shape, F32)
        for c in range(comps):
            total = jnp.sum(force[c], axis=1, keepdims=True)
            for q in range(bands):
                for j in range(bearings):
                    value = total[j * each + q : j * each + q + 1]
                    reply = jnp.where((place_of == q) & (col == FORCE_AT + c * bearings + j), value, reply)
        payload[...] = reply

    interface = (layer == d - 1) | (layer == d + layers - 1)

    given = {1: 0, all_rows - 2: 1}
    for a in range(all_rows):
        k = kx[a]
        k_h = conductance(k, ahead(k, 0))
        k_r = jnp.where(lane < width - 1, conductance(k, ahead(k, 1)), 0.0)
        kh[a], kh_back[a], kr[a], kr_back[a] = k_h, behind(k_h, 0), k_r, behind(k_r, 1)
        ks[a] = conductance(k, kx[min(a + 1, all_rows - 1)])
        for c in range(comps):
            v = ux[c, a]
            flux = jnp.where(interface, k_h * (ahead(v, 0) - v), 0.0)
            change = COMPONENT_SCALE[c] * (flux - behind(flux, 0))
            change = change - jnp.where(layer == d, raft[c, a : a + 1], 0.0)
            t0[c, a] = raw[c, a] + change
            if a in given:
                turn[c, given[a]] = change
    for a in (d - 1, d + rows - 1):
        for c in range(comps):
            flux = COMPONENT_SCALE[c] * (ks[a] * (ux[c, a + 1] - ux[c, a]))
            t0[c, a] = t0[c, a] + flux
            t0[c, a + 1] = t0[c, a + 1] - flux

    def diagonals(a, carry):
        around = kh[a] + kh_back[a] + kr[a] + kr_back[a] + ks[a] + ks[a - 1]
        diag[0, a] = mx[a] + COMPONENT_SCALE[0] * around + jnp.where(layer == d, raft[comps, pl.ds(a, 1)], 0.0)
        diag[1, a] = mx[a] + COMPONENT_SCALE[2] * around + jnp.where(layer == d, raft[comps + 1, pl.ds(a, 1)], 0.0)
        return carry

    lax.fori_loop(1, all_rows - 1, diagonals, 0, unroll=True)

    levels = (t0, t1, t2, t3, t4)
    shift_of, link_of = coefficients(survey[...])
    within = lax.broadcasted_iota(jnp.int32, (8, width), 0)
    for step in range(1, ITERS + 1):
        src, dst = levels[step - 1], levels[step]
        a_k = jnp.broadcast_to(shift_of[step - 1], (8, width))
        c_k = jnp.broadcast_to(link_of[step - 1], (8, width)) if step > 1 else None
        for a in range(step, all_rows - step):
            for start in range(0, all_layers, 8):
                part = slice(start, start + 8)
                k_h, k_low, k_r, k_left = kh[a, part], kh_back[a, part], kr[a, part], kr_back[a, part]
                k_next, k_back = ks[a, part], ks[a - 1, part]
                centres = [diag[n, a, part] - a_k for n in range(2)]
                for c in range(comps):
                    v = src[c, a, part]
                    upper, lower = ahead(v, 0), behind(v, 0)
                    if start + 8 < all_layers:
                        upper = jnp.where(within == 7, src[c, a, start + 8 : start + 9], upper)
                    if start:
                        lower = jnp.where(within == 0, src[c, a, start - 1 : start], lower)
                    around = k_next * src[c, a + 1, part] + k_back * src[c, a - 1, part]
                    around = around + (k_h * upper + k_low * lower)
                    around = around + (k_r * shifted(v, 1, 1) + k_left * shifted(v, 1, -1))
                    centre = centres[0 if c < 2 else 1] * v
                    if step > 1:
                        centre = centre - c_k * levels[step - 2][c, a, part]
                    dst[c, a, part] = centre - (around if COMPONENT_SCALE[c] == 1.0 else COMPONENT_SCALE[c] * around)
        if step == 1:
            a_wide = jnp.broadcast_to(shift_of[0], (all_layers, width))
            inside = (layer > d) & (layer < d + layers - 1)
            for a, n in given.items():
                for c in range(comps):
                    x = turn[c, n]
                    known = image[c, n] - COMPONENT_SCALE[c] * (kh[a] * ahead(x, 0) + kh_back[a] * behind(x, 0))
                    dst[c, a] = jnp.where(inside, known - a_wide * src[c, a], dst[c, a])


def late_kernel(
    t0, t1, t2, t3, t4, kx, kh, late_t, late_u, late_m, late_image, raft, payload_in, corner_b, survey,
    b0, b1, b2, b3, b4, payload,
    s0, s1, s2, s3, s4, raw, ux, k_tile, m_tile, ks, kh_tile, kh_back, kr, kr_back, diag, turn,
):
    comps, rows, layers, width = b0.shape
    d = DEPTH
    wedge = Wedge(comps)
    all_rows, all_layers = rows + 2 * d, layers + 2 * d
    sector_even = lax.rem(lax.axis_index("sector"), 2) == 0
    band_even = lax.rem(lax.axis_index("band"), 2) == 0
    lane = lax.broadcasted_iota(jnp.int32, (TILE, width), 1)
    layer = lax.broadcasted_iota(jnp.int32, (TILE, width), 0)
    shift_of, link_of = coefficients(survey[...])
    wide = lambda x: None if x is None else jnp.broadcast_to(x, (TILE, width))
    shift_of, link_of = [wide(x) for x in shift_of], [wide(x) for x in link_of]
    early, late = (t0, t1, t2, t3, t4), (s0, s1, s2, s3, s4)
    outs, pairs = (b0, b1, b2, b3, b4), gram_pairs()

    def run(even):
        off = 0 if even else all_layers - TILE

        def upper(x, whole, *at):
            x = ahead(x, 0)
            return jnp.where(layer == TILE - 1, whole[(*at, slice(TILE, TILE + 1))], x) if even else x

        def lower(x, whole, *at):
            x = behind(x, 0)
            return x if even else jnp.where(layer == 0, whole[(*at, slice(off - 1, off))], x)

        for a in range(all_rows):
            for c in range(comps):
                raw[c, a] = late_t[c, a]
                ux[c, a] = late_u[c, a]
            k_tile[a] = kx[a, off : off + TILE]
            m_tile[a] = late_m[a]
        near = d - 1 if even else d + layers - off
        for m, above in enumerate((sector_even, jnp.logical_not(sector_even))):
            place_wedge(raw, ux, k_tile, m_tile, corner_b, m * wedge.blocks, wedge, comps, rows, above, near, not even)

        given = {1: 0, all_rows - 2: 1}
        inside = (layer + off > d) & (layer + off < d + layers - 1)
        crossing = layer == (d - 1 if even else d + layers - 1 - off)
        on_raft = layer == d
        for a in range(all_rows):
            k = k_tile[a]
            k_h = conductance(k, upper(k, kx, a))
            kh_tile[a], kh_back[a] = k_h, lower(k_h, kh, a)
            k_r = jnp.where(lane < width - 1, conductance(k, ahead(k, 1)), 0.0)
            kr[a], kr_back[a] = k_r, behind(k_r, 1)
            if a + 1 < all_rows:
                ks[a] = conductance(k, k_tile[a + 1])
            for c in range(comps):
                v = ux[c, a]
                flux = jnp.where(crossing, k_h * (ahead(v, 0) - v), 0.0)
                change = COMPONENT_SCALE[c] * (flux - behind(flux, 0))
                if even:
                    change = change - jnp.where(on_raft, raft[c, a : a + 1], 0.0)
                s0[c, a] = raw[c, a] + change
                if a in given:
                    turn[c, given[a]] = change
        for a in (d - 1, d + rows - 1):
            for c in range(comps):
                flux = COMPONENT_SCALE[c] * (ks[a] * (ux[c, a + 1] - ux[c, a]))
                s0[c, a] = s0[c, a] + flux
                s0[c, a + 1] = s0[c, a + 1] - flux
        for a in range(1, all_rows - 1):
            around = kh_tile[a] + kh_back[a] + kr[a] + kr_back[a] + ks[a] + ks[a - 1]
            for n, scale in enumerate((COMPONENT_SCALE[0], COMPONENT_SCALE[2])):
                total = m_tile[a] + scale * around
                diag[n, a] = total + jnp.where(on_raft, raft[comps + n, a : a + 1], 0.0) if even else total
        for step in range(1, ITERS + 1):
            src, dst = late[step - 1], late[step]
            for a in range(step, all_rows - step):
                centres = [diag[n, a] - shift_of[step - 1] for n in range(2)]
                for c in range(comps):
                    v = src[c, a]
                    around = ks[a] * src[c, a + 1] + ks[a - 1] * src[c, a - 1]
                    around = around + (
                        kh_tile[a] * upper(v, early[step - 1], c, a) + kh_back[a] * lower(v, early[step - 1], c, a)
                    )
                    around = around + (kr[a] * shifted(v, 1, 1) + kr_back[a] * shifted(v, 1, -1))
                    centre = centres[0 if c < 2 else 1] * v
                    if step > 1:
                        centre = centre - link_of[step - 1] * late[step - 2][c, a]
                    out = centre - (around if COMPONENT_SCALE[c] == 1.0 else COMPONENT_SCALE[c] * around)
                    if step == 1 and a in given:
                        x = turn[c, given[a]]
                        known = late_image[c, given[a]] - COMPONENT_SCALE[c] * (
                            kh_tile[a] * ahead(x, 0) + kh_back[a] * behind(x, 0)
                        )
                        out = jnp.where(inside, known - shift_of[0] * v, out)
                    dst[c, a] = out

        sums = [jnp.zeros((8, width), F32) for _ in pairs]
        for a in range(rows):
            for c in range(comps):
                if even:
                    block = [jnp.concatenate([x[c, d + a, d:], t[c, d + a, TILE : d + layers]], axis=0) for t, x in zip(early, late)]
                else:
                    block = [jnp.concatenate([t[c, d + a, d:off], x[c, d + a, : d + layers - off]], axis=0) for t, x in zip(early, late)]
                for out, x in zip(outs, block):
                    out[c, a] = x
                sums = [s + dot(block[i], block[j]) for s, (i, j) in zip(sums, pairs)]
        col = lax.broadcasted_iota(jnp.int32, payload.shape, 1)
        reply = payload_in[...]
        for p, s in enumerate(sums):
            reply = jnp.where(col == p, total_of(s), reply)
        payload[...] = reply

    @pl.when(band_even)
    def _():
        run(True)

    @pl.when(jnp.logical_not(band_even))
    def _():
        run(False)


def combine_kernel(received, survey, b0, b1, b2, b3, b4, increment, residual, force, *, bearings, bands):
    comps, rows, layers, width = b0.shape
    sector = lax.axis_index("sector")
    total = jnp.sum(received[...], axis=0, keepdims=True)
    col = lax.broadcasted_iota(jnp.int32, total.shape, 1)
    table = {ij: jnp.sum(jnp.where(col == p, total, 0.0), axis=1, keepdims=True) for p, ij in enumerate(gram_pairs())}
    shift_of, link_of = coefficients(survey[...])
    g = lambda i, j: table[min(i, j), max(i, j)]
    zero, one = jnp.zeros_like(table[0, 0]), jnp.ones_like(table[0, 0])
    res = [one] + [zero] * ITERS
    direction, inc = list(res), [zero] * (ITERS + 1)
    norm = table[0, 0]
    for it in range(ITERS):
        image = [zero] * (ITERS + 1)
        for i in range(it + 1):
            image[i] = image[i] + shift_of[i] * direction[i]
            image[i + 1] = image[i + 1] + direction[i]
            if i:
                image[i - 1] = image[i - 1] + link_of[i] * direction[i]
        product = sum(
            direction[i] * sum(image[j] * g(i, j) for j in range(it + 2)) for i in range(it + 1)
        )
        alpha = norm / product
        inc = [x + alpha * y for x, y in zip(inc, direction)]
        res = [x - alpha * y for x, y in zip(res, image)]
        if it + 1 < ITERS:
            norm_next = sum(res[i] * sum(res[j] * g(i, j) for j in range(it + 2)) for i in range(it + 2))
            ratio = norm_next / norm
            direction = [x + ratio * y for x, y in zip(res, direction)]
            norm = norm_next
    basis = (b0, b1, b2, b3, b4)
    inc = [jnp.broadcast_to(x, (layers, width)) for x in inc[:ITERS]]
    res = [jnp.broadcast_to(x, (layers, width)) for x in res]

    def combine(a, carry):
        for c in range(comps):
            x = [b[c, a] for b in basis]
            increment[c, a] = sum(y * z for y, z in zip(inc, x))
            residual[c, a] = sum(y * z for y, z in zip(res, x))
        return carry

    lax.fori_loop(0, rows, combine, 0)
    mine = received[pl.ds(sector * bands, 1)]
    for c in range(comps):
        force[c : c + 1] = mine[:, FORCE_AT + c * bearings : FORCE_AT + (c + 1) * bearings]


def kernel_call(body, outs, operands, far=(), scratch=()):
    vmem = pl.BlockSpec(memory_space=pltpu.VMEM)
    operands = [pltpu.with_memory_space_constraint(x, pltpu.HBM) if i in far else x for i, x in enumerate(operands)]
    return pl.pallas_call(
        body,
        out_shape=[jax.ShapeDtypeStruct(s, F32) for s in outs],
        in_specs=[pl.BlockSpec(memory_space=pltpu.HBM) if i in far else vmem for i in range(len(operands))],
        out_specs=[vmem] * len(outs),
        scratch_shapes=[pltpu.VMEM(s, F32) if isinstance(s, tuple) else s for s in scratch],
        compiler_params=pltpu.CompilerParams(vmem_limit_bytes=VMEM_LIMIT),
    )(*operands)


def pair_up(i, n):
    return i ^ 1


def pair_down(i, n):
    return (((i + 1) % n) ^ 1) - 1 if ((i + 1) % n) ^ 1 else n - 1


def per_device(
    given_load, displacement, mass_coef, stiffness, bearing_node, stick_state, slip_prev, bearing_old, bearing_weight
):
    comps, rows, layers, radial = displacement.shape
    bearings = bearing_node.shape[0]
    sectors, bands = lax.axis_size("sector"), lax.axis_size("band")
    d = DEPTH
    slab, wedge = SectorSlab(comps, layers), Wedge(comps)

    def exchange(x, sector_partner=None, band_partner=None):
        pairs = []
        for s in range(sectors):
            for b in range(bands):
                t = s if sector_partner is None else sector_partner(s, sectors)
                q = b if band_partner is None else band_partner(b)
                if 0 <= q < bands:
                    pairs.append((s * bands + b, t * bands + q))
        return lax.ppermute(x, AXES, pairs)

    inner = lambda b: -1 if b in (0, bands - 1) else ((b + 1) ^ 1) - 1

    field, block = displacement.shape, mass_coef.shape
    slab_shape, band_shape = (slab.rows, radial), ((2 * comps + 2) * (rows // 2), 2 * d, radial)
    small = [
        pltpu.SMEM((bearings,), jnp.int32),
        pltpu.SMEM((bearings,), jnp.int32),
        pltpu.SMEM((2, bearings), F32),
        pltpu.SMEM((2, bearings), F32),
        pltpu.SMEM((bearings,), F32),
    ]
    work, slab_a, slab_b, band_b = kernel_call(
        functools.partial(local_kernel, radial=radial),
        [(2 * comps + 5, *block), slab_shape, slab_shape, band_shape],
        (displacement, given_load, mass_coef, stiffness, bearing_node, stick_state, slip_prev, bearing_old, bearing_weight),
        far=range(9),
        scratch=[field, *small, pltpu.SemaphoreType.DMA((12,))],
    )
    outer = lambda b: b ^ 1
    slab_b = exchange(slab_b, pair_down)
    slab_a = exchange(slab_a, pair_up)
    band_b = exchange(band_b, None, inner)
    (survey,) = kernel_call(survey_kernel, [(sectors * bands, 128)], (work,), scratch=[field] * 3)
    survey = lax.all_to_all(survey, AXES, 0, 0, tiled=True)
    corner_a, corner_b = kernel_call(
        functools.partial(corner_kernel, comps=comps, layers=layers),
        [(2 * wedge.blocks + band_shape[0], 2 * d, radial), (2 * wedge.blocks, 2 * d, radial)],
        (slab_a, slab_b, work, survey, band_b),
    )
    corner_b = exchange(corner_b, None, inner)
    corner_a = exchange(corner_a, None, outer)
    devices = sectors * bands
    extended = (rows + 2 * d, layers + 2 * d, radial)
    all_rows = extended[0]
    tile_field, tile_block = (comps, all_rows, TILE, radial), (all_rows, TILE, radial)
    *early, payload = kernel_call(
        functools.partial(early_kernel, bearings=bearings, sectors=sectors, bands=bands),
        [(comps, *extended)] * (ITERS + 1)
        + [extended] * 2
        + [tile_field, tile_field, tile_block, (comps, 2, TILE, radial), (comps + 2, all_rows, radial), (devices, 128)],
        (work, slab_a, slab_b, band_b, corner_a, survey),
        scratch=[(comps, *extended)] * 2 + [extended] * 5 + [(2, *extended)] + [(comps, 2, *extended[1:])] * 2,
    )
    *basis, payload = kernel_call(
        late_kernel,
        [field] * (ITERS + 1) + [(devices, 128)],
        (*early, payload, corner_b, survey),
        scratch=[tile_field] * (ITERS + 3) + [tile_block] * 7 + [(2, *tile_block), (comps, 2, TILE, radial)],
    )
    received = lax.all_to_all(payload, AXES, 0, 0, tiled=True)
    increment, residual, force = kernel_call(
        functools.partial(combine_kernel, bearings=bearings, bands=bands),
        [field, field, (comps, bearings)],
        (received, survey, *basis),
    )
    return (increment, residual, force)


def solution(mesh):
    return jax.shard_map(
        per_device,
        mesh=mesh,
        in_specs=(
            P(None, "sector", "band", None),
            P(None, "sector", "band", None),
            P("sector", "band", None),
            P("sector", "band", None),
            P(("sector", "band")),
            P(("sector", "band")),
            P(None, ("sector", "band")),
            P(None, ("sector", "band")),
            P(("sector", "band")),
        ),
        out_specs=(
            P(None, "sector", "band", None),
            P(None, "sector", "band", None),
            P(None, ("sector", "band")),
        ),
        check_vma=False,
    )
```

```python
import functools

import jax
import jax.numpy as jnp
from jax import lax
from jax.experimental import pallas as pl
from jax.experimental.pallas import tpu as pltpu
from jax.sharding import PartitionSpec as P

ITERS = 4
DEPTH = ITERS

K_STICK = 4.0
K_VERT = 8.0
MU_FAST = 0.15
MU_SLOW = 0.04
RATE_GAIN = 2.0
RATE_DECAY = 2.0
V_FLOOR = 0.05
COMPONENT_SCALE = (1.0, 1.0, 2.0)

STATS = 1 + 2 * (ITERS - 1)
TINY = 1e-30
FLOOR = 0.25

AXES = ("sector", "band")
F32 = jnp.float32
PARAM_ROW, PARAM_LANE, PARAM_STICK, PARAM_SLIP, PARAM_OLD, PARAM_WEIGHT = (0, 1, 2, 3, 5, 7)
PARAMS = 8
PARAM_AT = 32
FORCE_AT = 64
VMEM_LIMIT = 24 * 1024 * 1024
TILE = 8


def conductance(left, right):
    return 2.0 * left * right / jnp.maximum(left + right, FLOOR)


def ahead(x, axis):
    return pltpu.roll(x, x.shape[axis] - 1, axis)


def behind(x, axis):
    return pltpu.roll(x, 1, axis)


def shifted(x, axis, by):
    size = 8 if axis == 0 else 128
    count = x.shape[axis] // size
    parts = [lax.slice_in_dim(x, i * size, (i + 1) * size, axis=axis) for i in range(count)]
    turned = [pltpu.roll(p, size - 1 if by == 1 else 1, axis) for p in parts]
    edge = lax.broadcasted_iota(jnp.int32, parts[0].shape, axis) == (size - 1 if by == 1 else 0)
    out = [jnp.where(edge, turned[i + by], turned[i]) if 0 <= i + by < count else turned[i] for i in range(count)]
    return out[0] if count == 1 else jnp.concatenate(out, axis=axis)


def round_up(n, multiple):
    return -(-n // multiple) * multiple


def put_band(out, at, r, u, stiff, mass, top):
    comps, rows, layers, _ = r.shape
    fields = [r.at[c] for c in range(comps)] + [u.at[c] for c in range(comps)] + [stiff, mass]
    for f, field in enumerate(fields):
        for pair in range(rows // 2):
            planes = [field[2 * pair + i] for i in range(2)]
            high = jnp.concatenate([x[layers - DEPTH :] for x in planes], axis=0)
            low = jnp.concatenate([x[:DEPTH] for x in planes], axis=0)
            out[at + f * (rows // 2) + pair] = jnp.where(top, high, low)


class SectorSlab:
    def __init__(self, comps, layers):
        d = DEPTH
        self.comps, self.layers = comps, layers
        self.stiff = comps * (d - 1) * layers
        self.mass = self.stiff + (d - 1) * layers
        self.disp = self.mass + (d - 2) * layers
        self.image = self.disp + comps * layers
        self.low = self.image + comps * layers
        self.rims = comps * (d - 1) + comps + 2
        self.high = self.low + self.rims
        self.rows = round_up(self.high + self.rims, 8)

    def residual_at(self, c, i):
        return (c * (DEPTH - 1) + i) * self.layers

    def rim_disp(self, c, n):
        return c * (DEPTH - 1) + n - 2

    def rim_residual(self, c):
        return self.comps * (DEPTH - 1) + c

    def rim_stiff(self):
        return self.rims - 2

    def rim_mass(self):
        return self.rims - 1


def parts_of(work):
    comps = (work.shape[0] - 5) // 2
    return work.at[0:comps], work.at[comps : 2 * comps], work.at[2 * comps : 2 * comps + 3], work.at[2 * comps + 3], work.at[2 * comps + 4]


def local_kernel(
    u_far, load_far, mass_far, stiff_far, node_far, stick_far, slip_far, old_far, weight_far,
    work, slab_a, slab_b, band_b,
    load, node, stick, slip, old, weight, arrived, *, radial,
):
    comps, rows, layers, width = load.shape
    d = DEPTH
    r, u, cond, mass, stiff = parts_of(work)
    half = rows // 2
    fields = [(stiff_far, stiff)]
    for part in (pl.ds(0, half), pl.ds(half, rows - half)):
        fields += [
            (u_far.at[:, part], u.at[:, part]),
            (mass_far.at[part], mass.at[part]),
            (load_far.at[:, part], load.at[:, part]),
        ]
    small = ((node_far, node), (stick_far, stick), (slip_far, slip), (old_far, old), (weight_far, weight))
    moves = [pltpu.make_async_copy(src, dst, arrived.at[n]) for n, (src, dst) in enumerate([*fields, *small])]
    for move in moves:
        move.start()
    lane = lax.broadcasted_iota(jnp.int32, (layers, width), 1)
    layer = lax.broadcasted_iota(jnp.int32, (layers, width), 0)
    moves[0].wait()
    for a in range(rows):
        k = stiff[a]
        cond[0, a] = jnp.where(lane < width - 1, conductance(k, ahead(k, 1)), 0.0)
        cond[1, a] = jnp.where(layer < layers - 1, conductance(k, ahead(k, 0)), 0.0)
        cond[2, a] = conductance(k, stiff[a + 1]) if a + 1 < rows else jnp.zeros((layers, width), F32)
    before = [None] * comps
    for a in range(rows):
        if a == 0:
            for move in moves[1:4]:
                move.wait()
        if a == half - 1:
            for move in moves[4:7]:
                move.wait()
        k_r, k_h, k_s = cond[0, a], cond[1, a], cond[2, a]
        m = mass[a]
        for c in range(comps):
            v = u[c, a]
            flux_r = k_r * (ahead(v, 1) - v)
            flux_h = k_h * (ahead(v, 0) - v)
            total = flux_r - behind(flux_r, 1) + flux_h - behind(flux_h, 0)
            if before[c] is not None:
                total = total - before[c]
            if a + 1 < rows:
                before[c] = k_s * (u[c, a + 1] - v)
                total = total + before[c]
            r[c, a] = load[c, a] - m * v + COMPONENT_SCALE[c] * total

    for move in moves[len(fields) :]:
        move.wait()
    col = lax.broadcasted_iota(jnp.int32, (8, 128), 1)
    tile = jnp.zeros((8, 128), F32)
    for j in range(node.shape[0]):
        at = node[j] // radial
        values = {
            PARAM_ROW: at.astype(F32),
            PARAM_LANE: (node[j] - at * radial).astype(F32),
            PARAM_STICK: stick[j].astype(F32),
            PARAM_SLIP: slip[0, j],
            PARAM_SLIP + 1: slip[1, j],
            PARAM_OLD: old[0, j],
            PARAM_OLD + 1: old[1, j],
            PARAM_WEIGHT: weight[j],
        }
        for p, value in values.items():
            tile = jnp.where(col == PARAM_AT + PARAMS * j + p, value, tile)
    cond[2, rows - 1, 0:8, 0:128] = tile

    slab = SectorSlab(comps, layers)
    even = lax.rem(lax.axis_index("sector"), 2) == 0
    for out, upper in ((slab_a, even), (slab_b, jnp.logical_not(even))):

        def row(n, upper=upper):
            return jnp.where(upper, rows - n, n - 1)

        for i in range(d - 1):
            first = jnp.where(upper, rows - (d - 1), 0)
            for c in range(comps):
                out[pl.ds(slab.residual_at(c, i), layers)] = r[c, first + i]
            out[pl.ds(slab.stiff + i * layers, layers)] = stiff[first + i]
        for i in range(d - 2):
            out[pl.ds(slab.mass + i * layers, layers)] = mass[jnp.where(upper, rows - (d - 2), 0) + i]
        at = row(d - 1)
        k_r, k_h, k_next, k_back = cond[0, at], cond[1, at], cond[2, at], cond[2, at - 1]
        for c in range(comps):
            out[pl.ds(slab.disp + c * layers, layers)] = u[c, row(1)]
            v = r[c, at]
            flux_r = k_r * (ahead(v, 1) - v)
            flux_h = k_h * (ahead(v, 0) - v)
            total = flux_r - behind(flux_r, 1) + flux_h - behind(flux_h, 0)
            total = total + k_next * (r[c, at + 1] - v) - k_back * (v - r[c, at - 1])
            out[pl.ds(slab.image + c * layers, layers)] = mass[at] * v - COMPONENT_SCALE[c] * total
        for group, layer_of in ((slab.low, slice(0, 1)), (slab.high, slice(layers - 1, layers))):
            for c in range(comps):
                for n in range(2, d + 1):
                    out[pl.ds(group + slab.rim_disp(c, n), 1)] = u[c, row(n), layer_of]
                out[pl.ds(group + slab.rim_residual(c), 1)] = r[c, row(d), layer_of]
            out[pl.ds(group + slab.rim_stiff(), 1)] = stiff[row(d), layer_of]
            out[pl.ds(group + slab.rim_mass(), 1)] = mass[row(d - 1), layer_of]
        end = slab.high + slab.rims
        if slab.rows > end:
            out[pl.ds(end, slab.rows - end)] = jnp.zeros((slab.rows - end, width), F32)

    even = lax.rem(lax.axis_index("band"), 2) == 0
    put_band(band_b, 0, r, u, stiff, mass, jnp.logical_not(even))


REACH = [DEPTH] + [max(DEPTH - n, 1) for n in range(2, DEPTH + 1)]


class Wedge:
    counts = REACH
    starts = [sum(REACH[:n]) for n in range(DEPTH)]
    height = round_up(sum(REACH), 8)

    def __init__(self, comps):
        self.stiff, self.mass, self.disp = comps, comps + 1, comps + 2
        self.blocks = 2 * comps + 2


def padded_block(parts):
    parts = list(parts)
    spare = Wedge.height - sum(p.shape[0] for p in parts)
    if spare:
        parts.append(jnp.zeros((spare, parts[0].shape[1]), F32))
    return jnp.concatenate(parts, axis=0)


def put_wedge(out, at, comps, layers, top, residual, stiff, mass, disp, edges):
    wedge, d = Wedge(comps), DEPTH
    sources = [functools.partial(residual, c) for c in range(comps)] + [stiff, mass]
    for f, source in enumerate(sources):
        planes = [source(n) for n in range(1, d + 1)]
        high = padded_block(p[layers - k :] for p, k in zip(planes, wedge.counts))
        low = padded_block(p[:k] for p, k in zip(planes, wedge.counts))
        out[at + f] = jnp.where(top, high, low)
    for c in range(comps):
        row, rims = disp(c), [edges(c, n) for n in range(1, d + 1)]
        high = padded_block([row[layers - d :]] + [rim[1] for rim in rims])
        low = padded_block([row[:d]] + [rim[0] for rim in rims])
        out[at + wedge.disp + c] = jnp.where(top, high, low)


def corner_kernel(slab_a, slab_b, work, survey, band_b, corner_a, corner_b, *, comps, layers):
    d = DEPTH
    slab, wedge = SectorSlab(comps, layers), Wedge(comps)
    band_even = lax.rem(lax.axis_index("band"), 2) == 0
    sector_even = lax.rem(lax.axis_index("sector"), 2) == 0
    for n, (side, above) in enumerate(((slab_a, sector_even), (slab_b, jnp.logical_not(sector_even)))):

        def plane(offset, side=side):
            return side[pl.ds(pl.multiple_of(offset, 8), layers)]

        def step(n, count, above=above):
            return jnp.where(above, n - 1, count - n)

        def rim(at, side=side):
            return [side[pl.ds(group + at, 1)] for group in (slab.low, slab.high)]

        def stiff_of(n):
            if n < d:
                return plane(slab.stiff + step(n, d - 1) * layers)
            return jnp.concatenate([jnp.broadcast_to(x, (layers // 2, x.shape[1])) for x in rim(slab.rim_stiff())], axis=0)

        def disp_rim(c, n):
            if n > 1:
                return rim(slab.rim_disp(c, n))
            row = plane(slab.disp + c * layers)
            return [row[0:1], row[layers - 1 :]]

        for out, top in ((corner_a, band_even), (corner_b, jnp.logical_not(band_even))):
            put_wedge(
                out,
                n * wedge.blocks,
                comps,
                layers,
                top,
                lambda c, n: plane(slab.residual_at(c, step(min(n, d - 1), d - 1))),
                stiff_of,
                lambda n: plane(slab.mass + step(min(n, d - 2), d - 2) * layers),
                lambda c: plane(slab.disp + c * layers),
                disp_rim,
            )
    r, u, _, mass, stiff = parts_of(work)
    put_band(corner_a, 2 * wedge.blocks, r, u, stiff, mass, band_even)


def dot(x, y):
    return jnp.sum((x * y).reshape(x.shape[0] // 8, 8, x.shape[1]), axis=0)


def total_of(x):
    return jnp.sum(jnp.sum(x, axis=0, keepdims=True), axis=1, keepdims=True)


def survey_kernel(work, row, image, basis_1, basis_2):
    r, _, cond, mass, _ = parts_of(work)
    comps, rows, layers, width = r.shape
    zero = jnp.zeros((8, width), F32)

    def apply(src):
        norm, product = zero, zero
        for a in range(rows):
            k_r, k_h, k_next = cond[0, a], cond[1, a], cond[2, a]
            for c in range(comps):
                v = src[c, a]
                flux_r = k_r * (ahead(v, 1) - v)
                flux_h = k_h * (ahead(v, 0) - v)
                total = flux_r - behind(flux_r, 1) + flux_h - behind(flux_h, 0)
                if a + 1 < rows:
                    total = total + k_next * (src[c, a + 1] - v)
                if a:
                    total = total - cond[2, a - 1] * (v - src[c, a - 1])
                out = mass[a] * v - COMPONENT_SCALE[c] * total
                image[c, a] = out
                norm, product = norm + dot(v, v), product + dot(v, out)
        return total_of(norm), total_of(product)

    level, back, weight_here, stats = r, None, None, []
    outs = (basis_1, basis_2)
    norm_back = None
    for step in range(ITERS - 1):
        norm, product = apply(level)
        if step:
            stats.append(norm / jnp.maximum(norm_back, TINY))
        else:
            weight_here = norm
        stats.append(product / jnp.maximum(norm, TINY))
        if step < ITERS - 2:
            a_k = jnp.broadcast_to(stats[-1], (layers, width))
            c_k = jnp.broadcast_to(stats[-2], (layers, width)) if step else None
            for a in range(rows):
                for c in range(comps):
                    x = image[c, a] - a_k * level[c, a]
                    outs[step][c, a] = x if back is None else x - c_k * back[c, a]
            back, level, norm_back = level, outs[step], norm
        else:
            a_k = jnp.broadcast_to(stats[-1], (layers, width))
            c_k = jnp.broadcast_to(stats[-2], (layers, width))
            last = zero
            for a in range(rows):
                for c in range(comps):
                    x = image[c, a] - a_k * level[c, a] - c_k * back[c, a]
                    last = last + dot(x, x)
            stats.append(total_of(last) / jnp.maximum(norm, TINY))
    col = lax.broadcasted_iota(jnp.int32, (8, 128), 1)
    tile = jnp.where(col == 0, weight_here, 0.0)
    for n, value in enumerate(stats):
        tile = jnp.where(col == 1 + n, weight_here * value, tile)
    tile = tile + cond[2, rows - 1, 0:8, 0:128]
    for n in range(row.shape[0] // 8):
        row[8 * n : 8 * n + 8] = tile


def coefficients(survey):
    total = jnp.sum(survey, axis=0, keepdims=True)
    col = lax.broadcasted_iota(jnp.int32, total.shape, 1)
    pick = lambda n: jnp.sum(jnp.where(col == n, total, 0.0), axis=1, keepdims=True)
    weight = jnp.maximum(pick(0), TINY)
    stats = [pick(n) / weight for n in range(1, STATS)]
    a, c = stats[0::2], stats[1::2]
    return a + [a[-1]], [None] + c


def bearing_law(moved, vertical, stick, slip, old, weight):
    trial = [K_STICK * (moved[i] - slip[i]) for i in range(2)]
    rate = [RATE_GAIN * (moved[i] - old[i]) for i in range(2)]
    slip_speed = jnp.sqrt(rate[0] * rate[0] + rate[1] * rate[1] + V_FLOOR * V_FLOOR)
    friction = MU_FAST - (MU_FAST - MU_SLOW) * jnp.exp(-RATE_DECAY * slip_speed)
    capacity = friction * weight
    magnitude = jnp.sqrt(trial[0] * trial[0] + trial[1] * trial[1])
    largest = jnp.maximum(magnitude, capacity)
    forces = [jnp.where(stick == 1.0, t, capacity * t / largest) for t in trial]
    return forces + [K_VERT * vertical]


def gram_pairs():
    return [(0, j) for j in range(ITERS + 1)] + [(i, ITERS) for i in range(1, ITERS)]


def place_wedge(t, ux, kx, mx, block, at, wedge, comps, rows, above, near, upward):
    d = DEPTH
    for step in range(1, d + 1):
        row = jnp.where(above, d + rows - 1 + step, d - step)
        count, start = wedge.counts[step - 1], wedge.starts[step - 1]
        part = slice(start, start + count)
        where = slice(near, near + count) if upward else slice(near + 1 - count, near + 1)
        for c in range(comps):
            t[c, row, where] = block[at + c, part]
            ux[c, row, near : near + 1] = block[at + wedge.disp + c, d + step - 1 : d + step]
        kx[row, where] = block[at + wedge.stiff, part]
        mx[row, where] = block[at + wedge.mass, part]
    nearest = jnp.where(above, d + rows, d - 1)
    for c in range(comps):
        ux[c, nearest, slice(near, near + d) if upward else slice(near + 1 - d, near + 1)] = block[at + wedge.disp + c, 0:d]


def early_kernel(
    work, slab_a, slab_b, band_b, corner_a, survey,
    t0, t1, t2, t3, t4, kx, kh, late_t, late_u, late_m, late_image, raft, payload,
    raw, ux, mx, ks, kr, kh_back, kr_back, diag, image, turn,
    *, bearings, sectors, bands,
):
    r, u, _, mass, stiff = parts_of(work)
    comps, rows, layers, width = r.shape
    d = DEPTH
    slab, wedge = SectorSlab(comps, layers), Wedge(comps)
    sector, band = lax.axis_index("sector"), lax.axis_index("band")
    sector_even = lax.rem(sector, 2) == 0
    band_even = lax.rem(band, 2) == 0
    all_rows, all_layers = rows + 2 * d, layers + 2 * d
    own = pl.ds(d, layers)

    for a in range(rows):
        for c in range(comps):
            raw[c, d + a, own] = r[c, a]
            ux[c, d + a, own] = u[c, a]
        kx[d + a, own] = stiff[a]
        mx[d + a, own] = mass[a]
    sides = ((slab_a, sector_even), (slab_b, jnp.logical_not(sector_even)))
    empty = jnp.zeros((all_layers, width), F32)
    for side, above in sides:

        def row(n, above=above):
            return jnp.where(above, d + rows - 1 + n, d - n)

        for c in range(comps):
            raw[c, row(d)] = empty
        kx[row(d)], mx[row(d - 1)] = empty, empty
        for i in range(d - 1):
            first = jnp.where(above, d + rows, 1)
            for c in range(comps):
                raw[c, first + i, own] = side[pl.ds(slab.residual_at(c, i), layers)]
            kx[first + i, own] = side[pl.ds(slab.stiff + i * layers, layers)]
        for i in range(d - 2):
            mx[jnp.where(above, d + rows, 2) + i, own] = side[pl.ds(slab.mass + i * layers, layers)]
        for c in range(comps):
            ux[c, row(1), own] = side[pl.ds(slab.disp + c * layers, layers)]
            image[c, jnp.where(above, 1, 0), own] = side[pl.ds(slab.image + c * layers, layers)]
        for group, at in ((slab.low, slice(d, d + 1)), (slab.high, slice(d + layers - 1, d + layers))):
            rim = lambda place, group=group: side[pl.ds(group + place, 1)]
            for c in range(comps):
                for n in range(2, d + 1):
                    ux[c, row(n), at] = rim(slab.rim_disp(c, n))
                raw[c, row(d), at] = rim(slab.rim_residual(c))
            kx[row(d), at] = rim(slab.rim_stiff())
            mx[row(d - 1), at] = rim(slab.rim_mass())

    def place_bands(even):
        for side, first_block, upward in ((corner_a, 2 * wedge.blocks, even), (band_b, 0, not even)):
            where = pl.ds(d + layers if upward else 0, d)
            for a in range(rows):
                part = slice((a % 2) * d, (a % 2) * d + d)
                block = lambda f: side[first_block + f * (rows // 2) + a // 2, part]
                for c in range(comps):
                    raw[c, d + a, where] = block(c)
                    ux[c, d + a, where] = block(comps + c)
                kx[d + a, where] = block(2 * comps)
                mx[d + a, where] = block(2 * comps + 1)
        near = d + layers if even else d - 1
        for m, (_, above) in enumerate(sides):
            place_wedge(raw, ux, kx, mx, corner_a, m * wedge.blocks, wedge, comps, rows, above, near, even)
        late = pl.ds(0 if even else all_layers - TILE, TILE)
        for a in range(all_rows):
            for c in range(comps):
                late_t[c, a] = raw[c, a, late]
                late_u[c, a] = ux[c, a, late]
            late_m[a] = mx[a, late]
        for c in range(comps):
            for n in range(2):
                late_image[c, n] = image[c, n, late]

    @pl.when(band_even)
    def _():
        place_bands(True)

    @pl.when(jnp.logical_not(band_even))
    def _():
        place_bands(False)

    lane = lax.broadcasted_iota(jnp.int32, (all_layers, width), 1)
    layer = lax.broadcasted_iota(jnp.int32, (all_layers, width), 0)

    raft[...] = jnp.zeros_like(raft)
    payload[...] = jnp.zeros_like(payload)

    @pl.when(band == 0)
    def _():
        around = (sector, lax.rem(sector + 1, sectors), lax.rem(sector + sectors - 1, sectors))
        rows_of = jnp.concatenate([survey[pl.ds(x * bands, bands)] for x in around], axis=0)
        known = jnp.concatenate(
            [pltpu.roll(rows_of, 128 - PARAM_AT - PARAMS * j, 1) for j in range(bearings)], axis=0
        )
        each = len(around) * bands
        count = bearings * each
        within = lax.rem(lax.broadcasted_iota(jnp.int32, (count, 1), 0), each)
        shift = jnp.where(within < bands, d, jnp.where(within < 2 * bands, d + rows, d - rows))
        column = lambda p: known[:, p : p + 1]
        row_of = column(PARAM_ROW).astype(jnp.int32) + shift
        row_of = jnp.broadcast_to(row_of, (count, width))
        lane_of = jnp.broadcast_to(column(PARAM_LANE).astype(jnp.int32), (count, width))
        here = lane_of == lax.broadcasted_iota(jnp.int32, (count, width), 1)
        at_node = [jnp.zeros((count, width), F32) for _ in range(comps)]
        for a in range(all_rows):
            hit = row_of == a
            for c in range(comps):
                at_node[c] = jnp.where(hit, ux[c, a, d : d + 1], at_node[c])
        stick = jnp.broadcast_to(column(PARAM_STICK), (count, width))
        force = bearing_law(
            at_node[:2], at_node[2], stick,
            [column(PARAM_SLIP), column(PARAM_SLIP + 1)], [column(PARAM_OLD), column(PARAM_OLD + 1)], column(PARAM_WEIGHT),
        )
        force = [jnp.where(here, f, 0.0) for f in force]
        stiffness = [jnp.where(here & (stick == 1.0), K_STICK, 0.0), jnp.where(here, K_VERT, 0.0)]
        for a in range(all_rows):
            hit = row_of == a
            for q, value in enumerate(force + stiffness):
                raft[q, a : a + 1] = jnp.sum(jnp.where(hit, value, 0.0), axis=0, keepdims=True)
        place_of = lax.broadcasted_iota(jnp.int32, payload.shape, 0) - sector * bands
        col = lax.broadcasted_iota(jnp.int32, payload.shape, 1)
        reply = jnp.zeros(payload.shape, F32)
        for c in range(comps):
            total = jnp.sum(force[c], axis=1, keepdims=True)
            for q in range(bands):
                for j in range(bearings):
                    value = total[j * each + q : j * each + q + 1]
                    reply = jnp.where((place_of == q) & (col == FORCE_AT + c * bearings + j), value, reply)
        payload[...] = reply

    interface = (layer == d - 1) | (layer == d + layers - 1)

    given = {1: 0, all_rows - 2: 1}
    for a in range(all_rows):
        k = kx[a]
        k_h = conductance(k, ahead(k, 0))
        k_r = jnp.where(lane < width - 1, conductance(k, ahead(k, 1)), 0.0)
        kh[a], kh_back[a], kr[a], kr_back[a] = k_h, behind(k_h, 0), k_r, behind(k_r, 1)
        ks[a] = conductance(k, kx[min(a + 1, all_rows - 1)])
        for c in range(comps):
            v = ux[c, a]
            flux = jnp.where(interface, k_h * (ahead(v, 0) - v), 0.0)
            change = COMPONENT_SCALE[c] * (flux - behind(flux, 0))
            change = change - jnp.where(layer == d, raft[c, a : a + 1], 0.0)
            t0[c, a] = raw[c, a] + change
            if a in given:
                turn[c, given[a]] = change
    for a in (d - 1, d + rows - 1):
        for c in range(comps):
            flux = COMPONENT_SCALE[c] * (ks[a] * (ux[c, a + 1] - ux[c, a]))
            t0[c, a] = t0[c, a] + flux
            t0[c, a + 1] = t0[c, a + 1] - flux

    def diagonals(a, carry):
        around = kh[a] + kh_back[a] + kr[a] + kr_back[a] + ks[a] + ks[a - 1]
        diag[0, a] = mx[a] + COMPONENT_SCALE[0] * around + jnp.where(layer == d, raft[comps, pl.ds(a, 1)], 0.0)
        diag[1, a] = mx[a] + COMPONENT_SCALE[2] * around + jnp.where(layer == d, raft[comps + 1, pl.ds(a, 1)], 0.0)
        return carry

    lax.fori_loop(1, all_rows - 1, diagonals, 0, unroll=True)

    levels = (t0, t1, t2, t3, t4)
    shift_of, link_of = coefficients(survey[...])
    within = lax.broadcasted_iota(jnp.int32, (8, width), 0)
    for step in range(1, ITERS + 1):
        src, dst = levels[step - 1], levels[step]
        a_k = jnp.broadcast_to(shift_of[step - 1], (8, width))
        c_k = jnp.broadcast_to(link_of[step - 1], (8, width)) if step > 1 else None
        def level_rows(starts, step=step, src=src, dst=dst, a_k=a_k, c_k=c_k):
            for a in range(step, all_rows - step):
                for start in starts:
                    part = slice(start, start + 8)
                    k_h, k_low, k_r, k_left = kh[a, part], kh_back[a, part], kr[a, part], kr_back[a, part]
                    k_next, k_back = ks[a, part], ks[a - 1, part]
                    centres = [diag[n, a, part] - a_k for n in range(2)]
                    for c in range(comps):
                        v = src[c, a, part]
                        upper, lower = ahead(v, 0), behind(v, 0)
                        if start + 8 < all_layers:
                            upper = jnp.where(within == 7, src[c, a, start + 8 : start + 9], upper)
                        if start:
                            lower = jnp.where(within == 0, src[c, a, start - 1 : start], lower)
                        around = k_next * src[c, a + 1, part] + k_back * src[c, a - 1, part]
                        around = around + (k_h * upper + k_low * lower)
                        around = around + (k_r * shifted(v, 1, 1) + k_left * shifted(v, 1, -1))
                        centre = centres[0 if c < 2 else 1] * v
                        if step > 1:
                            centre = centre - c_k * levels[step - 2][c, a, part]
                        dst[c, a, part] = centre - (around if COMPONENT_SCALE[c] == 1.0 else COMPONENT_SCALE[c] * around)

        starts = range(0, all_layers, 8)
        if step < ITERS:
            level_rows(starts)
        else:
            pl.when(band_even)(functools.partial(level_rows, [x for x in starts if x >= TILE]))
            pl.when(jnp.logical_not(band_even))(functools.partial(level_rows, [x for x in starts if x < all_layers - TILE]))
        if step == 1:
            a_wide = jnp.broadcast_to(shift_of[0], (all_layers, width))
            inside = (layer > d) & (layer < d + layers - 1)
            for a, n in given.items():
                for c in range(comps):
                    x = turn[c, n]
                    known = image[c, n] - COMPONENT_SCALE[c] * (kh[a] * ahead(x, 0) + kh_back[a] * behind(x, 0))
                    dst[c, a] = jnp.where(inside, known - a_wide * src[c, a], dst[c, a])


def late_kernel(
    t0, t1, t2, t3, t4, kx, kh, late_t, late_u, late_m, late_image, raft, payload_in, corner_b, survey,
    b0, b1, b2, b3, b4, payload,
    s0, s1, s2, s3, s4, raw, ux, k_tile, m_tile, ks, kh_tile, kh_back, kr, kr_back, diag, turn,
):
    comps, rows, layers, width = b0.shape
    d = DEPTH
    wedge = Wedge(comps)
    all_rows, all_layers = rows + 2 * d, layers + 2 * d
    sector_even = lax.rem(lax.axis_index("sector"), 2) == 0
    band_even = lax.rem(lax.axis_index("band"), 2) == 0
    lane = lax.broadcasted_iota(jnp.int32, (TILE, width), 1)
    layer = lax.broadcasted_iota(jnp.int32, (TILE, width), 0)
    shift_of, link_of = coefficients(survey[...])
    wide = lambda x: None if x is None else jnp.broadcast_to(x, (TILE, width))
    shift_of, link_of = [wide(x) for x in shift_of], [wide(x) for x in link_of]
    early, late = (t0, t1, t2, t3, t4), (s0, s1, s2, s3, s4)
    outs, pairs = (b0, b1, b2, b3, b4), gram_pairs()

    def run(even):
        off = 0 if even else all_layers - TILE

        def upper(x, whole, *at):
            x = ahead(x, 0)
            return jnp.where(layer == TILE - 1, whole[(*at, slice(TILE, TILE + 1))], x) if even else x

        def lower(x, whole, *at):
            x = behind(x, 0)
            return x if even else jnp.where(layer == 0, whole[(*at, slice(off - 1, off))], x)

        for a in range(all_rows):
            for c in range(comps):
                raw[c, a] = late_t[c, a]
                ux[c, a] = late_u[c, a]
            k_tile[a] = kx[a, off : off + TILE]
            m_tile[a] = late_m[a]
        near = d - 1 if even else d + layers - off
        for m, above in enumerate((sector_even, jnp.logical_not(sector_even))):
            place_wedge(raw, ux, k_tile, m_tile, corner_b, m * wedge.blocks, wedge, comps, rows, above, near, not even)

        given = {1: 0, all_rows - 2: 1}
        inside = (layer + off > d) & (layer + off < d + layers - 1)
        crossing = layer == (d - 1 if even else d + layers - 1 - off)
        on_raft = layer == d
        for a in range(all_rows):
            k = k_tile[a]
            k_h = conductance(k, upper(k, kx, a))
            kh_tile[a], kh_back[a] = k_h, lower(k_h, kh, a)
            k_r = jnp.where(lane < width - 1, conductance(k, ahead(k, 1)), 0.0)
            kr[a], kr_back[a] = k_r, behind(k_r, 1)
            if a + 1 < all_rows:
                ks[a] = conductance(k, k_tile[a + 1])
            for c in range(comps):
                v = ux[c, a]
                flux = jnp.where(crossing, k_h * (ahead(v, 0) - v), 0.0)
                change = COMPONENT_SCALE[c] * (flux - behind(flux, 0))
                if even:
                    change = change - jnp.where(on_raft, raft[c, a : a + 1], 0.0)
                s0[c, a] = raw[c, a] + change
                if a in given:
                    turn[c, given[a]] = change
        for a in (d - 1, d + rows - 1):
            for c in range(comps):
                flux = COMPONENT_SCALE[c] * (ks[a] * (ux[c, a + 1] - ux[c, a]))
                s0[c, a] = s0[c, a] + flux
                s0[c, a + 1] = s0[c, a + 1] - flux
        for a in range(1, all_rows - 1):
            around = kh_tile[a] + kh_back[a] + kr[a] + kr_back[a] + ks[a] + ks[a - 1]
            for n, scale in enumerate((COMPONENT_SCALE[0], COMPONENT_SCALE[2])):
                total = m_tile[a] + scale * around
                diag[n, a] = total + jnp.where(on_raft, raft[comps + n, a : a + 1], 0.0) if even else total
        for step in range(1, ITERS + 1):
            src, dst = late[step - 1], late[step]
            for a in range(step, all_rows - step):
                centres = [diag[n, a] - shift_of[step - 1] for n in range(2)]
                for c in range(comps):
                    v = src[c, a]
                    around = ks[a] * src[c, a + 1] + ks[a - 1] * src[c, a - 1]
                    around = around + (
                        kh_tile[a] * upper(v, early[step - 1], c, a) + kh_back[a] * lower(v, early[step - 1], c, a)
                    )
                    around = around + (kr[a] * shifted(v, 1, 1) + kr_back[a] * shifted(v, 1, -1))
                    centre = centres[0 if c < 2 else 1] * v
                    if step > 1:
                        centre = centre - link_of[step - 1] * late[step - 2][c, a]
                    out = centre - (around if COMPONENT_SCALE[c] == 1.0 else COMPONENT_SCALE[c] * around)
                    if step == 1 and a in given:
                        x = turn[c, given[a]]
                        known = late_image[c, given[a]] - COMPONENT_SCALE[c] * (
                            kh_tile[a] * ahead(x, 0) + kh_back[a] * behind(x, 0)
                        )
                        out = jnp.where(inside, known - shift_of[0] * v, out)
                    dst[c, a] = out

        sums = [jnp.zeros((8, width), F32) for _ in pairs]
        for a in range(rows):
            for c in range(comps):
                if even:
                    block = [jnp.concatenate([x[c, d + a, d:], t[c, d + a, TILE : d + layers]], axis=0) for t, x in zip(early, late)]
                else:
                    block = [jnp.concatenate([t[c, d + a, d:off], x[c, d + a, : d + layers - off]], axis=0) for t, x in zip(early, late)]
                for out, x in zip(outs, block):
                    out[c, a] = x
                sums = [s + dot(block[i], block[j]) for s, (i, j) in zip(sums, pairs)]
        col = lax.broadcasted_iota(jnp.int32, payload.shape, 1)
        reply = payload_in[...]
        for p, s in enumerate(sums):
            reply = jnp.where(col == p, total_of(s), reply)
        payload[...] = reply

    @pl.when(band_even)
    def _():
        run(True)

    @pl.when(jnp.logical_not(band_even))
    def _():
        run(False)


def combine_kernel(received, survey, b0, b1, b2, b3, b4, increment, residual, force, *, bearings, bands):
    comps, rows, layers, width = b0.shape
    sector = lax.axis_index("sector")
    total = jnp.sum(received[...], axis=0, keepdims=True)
    col = lax.broadcasted_iota(jnp.int32, total.shape, 1)
    table = {ij: jnp.sum(jnp.where(col == p, total, 0.0), axis=1, keepdims=True) for p, ij in enumerate(gram_pairs())}
    shift_of, link_of = coefficients(survey[...])
    for i in range(ITERS - 1):
        for j in range(i + 1, ITERS):
            value = table[i, j + 1] + (shift_of[j] - shift_of[i]) * table[i, j] + link_of[j] * table[min(i, j - 1), max(i, j - 1)]
            table[i + 1, j] = value - link_of[i] * table[i - 1, j] if i else value
    g = lambda i, j: table[min(i, j), max(i, j)]
    zero, one = jnp.zeros_like(table[0, 0]), jnp.ones_like(table[0, 0])
    res = [one] + [zero] * ITERS
    direction, inc = list(res), [zero] * (ITERS + 1)
    norm = table[0, 0]
    for it in range(ITERS):
        image = [zero] * (ITERS + 1)
        for i in range(it + 1):
            image[i] = image[i] + shift_of[i] * direction[i]
            image[i + 1] = image[i + 1] + direction[i]
            if i:
                image[i - 1] = image[i - 1] + link_of[i] * direction[i]
        product = sum(
            direction[i] * sum(image[j] * g(i, j) for j in range(it + 2)) for i in range(it + 1)
        )
        alpha = norm / product
        inc = [x + alpha * y for x, y in zip(inc, direction)]
        res = [x - alpha * y for x, y in zip(res, image)]
        if it + 1 < ITERS:
            norm_next = sum(res[i] * sum(res[j] * g(i, j) for j in range(it + 2)) for i in range(it + 2))
            ratio = norm_next / norm
            direction = [x + ratio * y for x, y in zip(res, direction)]
            norm = norm_next
    basis = (b0, b1, b2, b3, b4)
    inc = [jnp.broadcast_to(x, (layers, width)) for x in inc[:ITERS]]
    res = [jnp.broadcast_to(x, (layers, width)) for x in res]

    def combine(a, carry):
        for c in range(comps):
            x = [b[c, a] for b in basis]
            increment[c, a] = sum(y * z for y, z in zip(inc, x))
            residual[c, a] = sum(y * z for y, z in zip(res, x))
        return carry

    lax.fori_loop(0, rows, combine, 0)
    mine = received[pl.ds(sector * bands, 1)]
    for c in range(comps):
        force[c : c + 1] = mine[:, FORCE_AT + c * bearings : FORCE_AT + (c + 1) * bearings]


def kernel_call(body, outs, operands, far=(), scratch=()):
    vmem = pl.BlockSpec(memory_space=pltpu.VMEM)
    operands = [pltpu.with_memory_space_constraint(x, pltpu.HBM) if i in far else x for i, x in enumerate(operands)]
    return pl.pallas_call(
        body,
        out_shape=[jax.ShapeDtypeStruct(s, F32) for s in outs],
        in_specs=[pl.BlockSpec(memory_space=pltpu.HBM) if i in far else vmem for i in range(len(operands))],
        out_specs=[vmem] * len(outs),
        scratch_shapes=[pltpu.VMEM(s, F32) if isinstance(s, tuple) else s for s in scratch],
        compiler_params=pltpu.CompilerParams(vmem_limit_bytes=VMEM_LIMIT),
    )(*operands)


def pair_up(i, n):
    return i ^ 1


def pair_down(i, n):
    return (((i + 1) % n) ^ 1) - 1 if ((i + 1) % n) ^ 1 else n - 1


def per_device(
    given_load, displacement, mass_coef, stiffness, bearing_node, stick_state, slip_prev, bearing_old, bearing_weight
):
    comps, rows, layers, radial = displacement.shape
    bearings = bearing_node.shape[0]
    sectors, bands = lax.axis_size("sector"), lax.axis_size("band")
    d = DEPTH
    slab, wedge = SectorSlab(comps, layers), Wedge(comps)

    def exchange(x, sector_partner=None, band_partner=None):
        pairs = []
        for s in range(sectors):
            for b in range(bands):
                t = s if sector_partner is None else sector_partner(s, sectors)
                q = b if band_partner is None else band_partner(b)
                if 0 <= q < bands:
                    pairs.append((s * bands + b, t * bands + q))
        return lax.ppermute(x, AXES, pairs)

    inner = lambda b: -1 if b in (0, bands - 1) else ((b + 1) ^ 1) - 1

    field, block = displacement.shape, mass_coef.shape
    slab_shape, band_shape = (slab.rows, radial), ((2 * comps + 2) * (rows // 2), 2 * d, radial)
    small = [
        pltpu.SMEM((bearings,), jnp.int32),
        pltpu.SMEM((bearings,), jnp.int32),
        pltpu.SMEM((2, bearings), F32),
        pltpu.SMEM((2, bearings), F32),
        pltpu.SMEM((bearings,), F32),
    ]
    work, slab_a, slab_b, band_b = kernel_call(
        functools.partial(local_kernel, radial=radial),
        [(2 * comps + 5, *block), slab_shape, slab_shape, band_shape],
        (displacement, given_load, mass_coef, stiffness, bearing_node, stick_state, slip_prev, bearing_old, bearing_weight),
        far=range(9),
        scratch=[field, *small, pltpu.SemaphoreType.DMA((12,))],
    )
    outer = lambda b: b ^ 1
    slab_b = exchange(slab_b, pair_down)
    slab_a = exchange(slab_a, pair_up)
    band_b = exchange(band_b, None, inner)
    (survey,) = kernel_call(survey_kernel, [(sectors * bands, 128)], (work,), scratch=[field] * 3)
    survey = lax.all_to_all(survey, AXES, 0, 0, tiled=True)
    corner_a, corner_b = kernel_call(
        functools.partial(corner_kernel, comps=comps, layers=layers),
        [(2 * wedge.blocks + band_shape[0], 2 * d, radial), (2 * wedge.blocks, 2 * d, radial)],
        (slab_a, slab_b, work, survey, band_b),
    )
    corner_b = exchange(corner_b, None, inner)
    corner_a = exchange(corner_a, None, outer)
    devices = sectors * bands
    extended = (rows + 2 * d, layers + 2 * d, radial)
    all_rows = extended[0]
    tile_field, tile_block = (comps, all_rows, TILE, radial), (all_rows, TILE, radial)
    *early, payload = kernel_call(
        functools.partial(early_kernel, bearings=bearings, sectors=sectors, bands=bands),
        [(comps, *extended)] * (ITERS + 1)
        + [extended] * 2
        + [tile_field, tile_field, tile_block, (comps, 2, TILE, radial), (comps + 2, all_rows, radial), (devices, 128)],
        (work, slab_a, slab_b, band_b, corner_a, survey),
        scratch=[(comps, *extended)] * 2 + [extended] * 5 + [(2, *extended)] + [(comps, 2, *extended[1:])] * 2,
    )
    *basis, payload = kernel_call(
        late_kernel,
        [field] * (ITERS + 1) + [(devices, 128)],
        (*early, payload, corner_b, survey),
        scratch=[tile_field] * (ITERS + 3) + [tile_block] * 7 + [(2, *tile_block), (comps, 2, TILE, radial)],
    )
    received = lax.all_to_all(payload, AXES, 0, 0, tiled=True)
    increment, residual, force = kernel_call(
        functools.partial(combine_kernel, bearings=bearings, bands=bands),
        [field, field, (comps, bearings)],
        (received, survey, *basis),
    )
    return (increment, residual, force)


def solution(mesh):
    return jax.shard_map(
        per_device,
        mesh=mesh,
        in_specs=(
            P(None, "sector", "band", None),
            P(None, "sector", "band", None),
            P("sector", "band", None),
            P("sector", "band", None),
            P(("sector", "band")),
            P(("sector", "band")),
            P(None, ("sector", "band")),
            P(None, ("sector", "band")),
            P(("sector", "band")),
        ),
        out_specs=(
            P(None, "sector", "band", None),
            P(None, "sector", "band", None),
            P(None, ("sector", "band")),
        ),
        check_vma=False,
    )
```
